32 devices in a mesh: img: 2 (over y), row: 4 (over x, core), col: 4 (over z).
Axes of the slice: x: 2, y: 2, z: 4, core: 2. Of those that a mesh axis runs over, the one named last changes fastest.
Arguments:
- tokens: bfloat16 [24, 32, 32, 1152], P('img', 'row', 'col'), may hold values from -6 to 6
- conditioning: bfloat16 [24, 4, 1152], P('img'), may hold values from -6 to 6
- images_in_slot: int32 [24], P('img'), may hold values from 1 to 4, as said below
- w_qkv: bfloat16 [1152, 3456], replicated, may hold values from -0.1875 to 0.1875
- b_qv: bfloat16 [2304], replicated, may hold values from -3 to 3
- w_proj: bfloat16 [1152, 1152], replicated, may hold values from -0.375 to 0.375
- b_proj: bfloat16 [1152], replicated, may hold values from -3 to 3
- w_up: bfloat16 [1152, 4608], replicated, may hold values from -0.1875 to 0.1875
- b_up: bfloat16 [4608], replicated, may hold values from -3 to 3
- w_down: bfloat16 [4608, 1152], replicated, may hold values from -0.09375 to 0.09375
- b_down: bfloat16 [1152], replicated, may hold values from -3 to 3
- w_ada: bfloat16 [1152, 6912], replicated, may hold values from -0.1875 to 0.1875
- b_ada: bfloat16 [6912], replicated, may hold values from -2 to 2
- cotangent: bfloat16 [24, 32, 32, 1152], P('img', 'row', 'col'), may hold values from -6 to 6
Outputs:
- output: bfloat16 [24, 32, 32, 1152], P('img', 'row', 'col')
- grad_tokens: float32 [24, 32, 32, 1152], P('img', 'row', 'col')
- grad_conditioning: float32 [24, 4, 1152], P('img')
- grad_w_qkv: float32 [1152, 3456], P(('row', 'col'))
- grad_b_qv: float32 [2304], P(('row', 'col'))
- grad_w_proj: float32 [1152, 1152], P(('row', 'col'))
- grad_b_proj: float32 [1152], P(('row', 'col'))
- grad_w_up: float32 [1152, 4608], P(('row', 'col'))
- grad_b_up: float32 [4608], P(('row', 'col'))
- grad_w_down: float32 [4608, 1152], P(('row', 'col'))
- grad_b_down: float32 [1152], P(('row', 'col'))
- grad_w_ada: float32 [1152, 6912], P(('row', 'col'))
- grad_b_ada: float32 [6912], P(('row', 'col'))
The draws below stay inside these ranges and needn't reach their ends.
Inputs may be any that keep to these rules, and one draw needn't show every extreme that they name: `images_in_slot`: each value is 1 (one image fills the slot's 32 x 32 grid) or 4 (four images, one in each quadrant of 16 x 16 tokens); among the 12 slots of each index of img at least one holds 1 image.
All inputs are finite; a program needn't handle non-finite values.
Results may differ from the reference program's by a relative error of at most 0.04.
Values may be sent and summed in bfloat16 or wider, within the bound.
A program may use at most 576 MiB of HBM per device.

```python
import math
import jax
import jax.numpy as jnp
from jax import lax

D = 1152
HEADS = 16
FF = 4608
GRID = 32
SLOT_DEV = 12
SLOTS = 24


def draw_images_in_slot(key, part):
    key = jax.random.fold_in(key, 7)
    flip_key, order_key = jax.random.split(key)
    groups = SLOTS // SLOT_DEV
    coin_flips = jax.random.randint(flip_key, (groups, SLOT_DEV), 0, 2)
    scores = jax.random.randint(order_key, (groups, SLOT_DEV), 0, 1 << 20) * SLOT_DEV + jnp.arange(SLOT_DEV, dtype=jnp.int32)[None, :]
    ordering = jnp.argsort(scores, axis=1)
    ranking = jnp.argsort(ordering, axis=1)
    slot_kinds = jnp.where(ranking == 0, 1, jnp.where(ranking == 1, 4, 1 + 3 * coin_flips))
    return slot_kinds.reshape(SLOTS).astype(jnp.int32)


def steps_of(key, dims, shards, smallest, top_value):
    gain, own = 1.0, jax.random.fold_in(key, 6)
    for position, blocks in shards:
        steps = jnp.exp(jax.random.uniform(jax.random.fold_in(own, position), (blocks,), jnp.float32, smallest / len(shards), top_value / len(shards)))
        gain = gain * jnp.repeat(steps, dims[position] // blocks).reshape([-1 if axis == position else 1 for axis in range(len(dims))])
    return gain


def normal_values(rng, dims, width, reach, pieces=(), kind=jnp.bfloat16):
    factor_of = steps_of(rng, dims, pieces, -0.22, 0.18) if pieces else 1.0
    values = jax.random.normal(rng, dims, jnp.float32) * width * factor_of
    return jnp.minimum(jnp.maximum(values, -reach), reach).astype(kind)


def setup_inputs(seed: int = 0) -> dict:
    splits = jax.random.split(jax.random.key(seed), 15)
    tokens = normal_values(splits[0], (SLOTS, GRID, GRID, D), 1.0, 6.0, ((0, 2), (1, 4), (2, 4)))
    conditioning = normal_values(splits[1], (SLOTS, 4, D), 1.0, 6.0, ((0, 2),))
    images_in_slot = draw_images_in_slot(jax.random.fold_in(splits[14], 71), 0)
    w_qkv = normal_values(splits[3], (D, 3 * D), D ** -0.5, 0.1875)
    b_qv = normal_values(splits[4], (2 * D,), 0.5, 3.0)
    w_proj = normal_values(splits[5], (D, D), (D // 4) ** -0.5, 0.375)
    b_proj = normal_values(splits[6], (D,), 0.5, 3.0)
    w_up = normal_values(splits[7], (D, FF), D ** -0.5, 0.1875)
    b_up = normal_values(splits[8], (FF,), 0.5, 3.0)
    w_down = normal_values(splits[9], (FF, D), FF ** -0.5, 0.09375)
    b_down = normal_values(splits[10], (D,), 0.5, 3.0)
    w_ada = normal_values(splits[11], (D, 6 * D), D ** -0.5, 0.1875)
    b_ada = normal_values(splits[12], (6 * D,), 0.3, 2.0)
    cotangent = normal_values(splits[13], (SLOTS, GRID, GRID, D), 1.0, 6.0, ((0, 2), (1, 4), (2, 4)))
    return dict(tokens=tokens, conditioning=conditioning, images_in_slot=images_in_slot, w_qkv=w_qkv, b_qv=b_qv, w_proj=w_proj, b_proj=b_proj, w_up=w_up, b_up=b_up, w_down=w_down, b_down=b_down, w_ada=w_ada, b_ada=b_ada, cotangent=cotangent)


norm_eps = 1e-06
masked_score = -1e+30
highest = lax.Precision.HIGHEST

@jax.custom_vjp
def low(v):
    return lax.optimization_barrier(v.astype(jnp.bfloat16)).astype(jnp.float32)

@jax.custom_vjp
def low_back(v):
    return v

def low_keep(v):
    return (low(v), None)

def low_pass(kept, grad):
    return (grad,)

def back_keep(v):
    return (v, None)

def back_low(kept, grad):
    return (low(grad),)
low.defvjp(low_keep, low_pass)
low_back.defvjp(back_keep, back_low)

def layer_norm(values):
    center = values - lax.optimization_barrier(jnp.mean(values, axis=-1, keepdims=True))
    spread = lax.optimization_barrier(jnp.mean(center * center, axis=-1, keepdims=True))
    return center * lax.rsqrt(spread + norm_eps)

def modulate(values, shift_term, scale_term):
    return layer_norm(values) * (1.0 + scale_term) + shift_term

def project(values, weight):
    return jnp.einsum('...d,de->...e', values, weight, precision=highest)

def attend_group(queries, key_block, value_block, segment):
    head_size = queries.shape[-1]
    scores = jnp.einsum('gqhe,gkhe->ghqk', queries, key_block, precision=highest) * (1.0 / math.sqrt(head_size))
    scores = low_back(scores)
    same_image = segment[:, None, :, None] == segment[:, None, None, :]
    scores = jnp.where(same_image, scores, masked_score)
    row_max = lax.optimization_barrier(jnp.max(scores, axis=-1, keepdims=True))
    exponent = jnp.exp(scores - row_max)
    row_total = lax.optimization_barrier(jnp.sum(exponent, axis=-1, keepdims=True))
    summed = low_back(jnp.einsum('ghqk,gkhe->gqhe', low(exponent), value_block, precision=highest))
    return summed / jnp.transpose(row_total, (0, 2, 1, 3))

def attend_all(queries, key_block, value_block, segment):
    slot_count = queries.shape[0]
    grouped = math.gcd(slot_count, 2)
    shaped = tuple((member.reshape((slot_count // grouped, grouped) + member.shape[1:]) for member in (queries, key_block, value_block, segment)))

    def scan_step(carried, sliced):
        return (carried, jax.checkpoint(attend_group)(*sliced))
    _, outputs = lax.scan(scan_step, jnp.zeros((), jnp.float32), shaped)
    return outputs.reshape(queries.shape)

def forward(tokens, conditioning, w_qkv, b_qv, w_proj, b_proj, w_up, b_up, w_down, b_down, w_ada, b_ada, images_in_slot):
    slot_count, grid_side, _, model_width = tokens.shape
    half_grid = grid_side // 2
    head_count = HEADS
    head_size = model_width // head_count
    silu_cond = low(jax.nn.silu(conditioning))
    modulation = project(silu_cond, w_ada) + b_ada
    four_way = images_in_slot == 4
    quarter_ids = jnp.arange(4, dtype=jnp.int32)
    picked = jnp.where(four_way[:, None], quarter_ids[None, :], 0)
    one_hot = (picked[:, :, None] == quarter_ids[None, None, :]).astype(jnp.float32)
    chosen = jnp.einsum('sqr,sre->sqe', one_hot, modulation, precision=highest)
    chosen = chosen.reshape(slot_count, 2, 2, 6, model_width)[:, :, None, :, None]
    shift_one = chosen[..., 0, :]
    scale_one = chosen[..., 1, :]
    gate_one = chosen[..., 2, :]
    shift_two = chosen[..., 3, :]
    scale_two = chosen[..., 4, :]
    gate_two = chosen[..., 5, :]
    inputs = tokens.reshape(slot_count, 2, half_grid, 2, half_grid, model_width)
    normed_one = low(modulate(inputs, shift_one, scale_one))
    projected = project(normed_one, w_qkv)
    queries = low(low_back(projected[..., :model_width] + b_qv[:model_width]))
    key_block = low(low_back(projected[..., model_width:2 * model_width]))
    value_block = low(low_back(projected[..., 2 * model_width:] + b_qv[model_width:]))
    positions = jnp.arange(grid_side * grid_side, dtype=jnp.int32)
    quarter = (positions // grid_side >= half_grid).astype(jnp.int32) * 2 + (positions % grid_side >= half_grid).astype(jnp.int32)
    segment = jnp.where(four_way[:, None], quarter[None, :], 0)

    def to_heads(member):
        return member.reshape(slot_count, grid_side * grid_side, head_count, head_size)
    attended = attend_all(to_heads(queries), to_heads(key_block), to_heads(value_block), segment)
    attended = low(attended.reshape(inputs.shape))
    branch_one = low_back(project(attended, w_proj) + b_proj)
    middle = inputs + gate_one * branch_one
    normed_two = low(modulate(middle, shift_two, scale_two))
    hidden_pre = low_back(project(normed_two, w_up) + b_up)
    hidden = low(jax.nn.gelu(hidden_pre, approximate=True))
    branch_two = low_back(project(hidden, w_down) + b_down)
    result = middle + gate_two * branch_two
    return result.reshape(slot_count, grid_side, grid_side, model_width)

def reference(tokens, conditioning, images_in_slot, w_qkv, b_qv, w_proj, b_proj, w_up, b_up, w_down, b_down, w_ada, b_ada, cotangent):
    floats = tuple((member.astype(jnp.float32) for member in (tokens, conditioning, w_qkv, b_qv, w_proj, b_proj, w_up, b_up, w_down, b_down, w_ada, b_ada)))

    def wrapped(*members):
        return forward(*members, images_in_slot)
    result, backward = jax.vjp(wrapped, *floats)
    grads = backward(cotangent.astype(jnp.float32))
    return (result.astype(jnp.bfloat16), grads[0], grads[1], grads[2], grads[3], grads[4], grads[5], grads[6], grads[7], grads[8], grads[9], grads[10], grads[11])
```

```python
import functools
import math

import jax
import jax.numpy as jnp
from jax import lax
from jax.experimental import pallas as pl
from jax.experimental.pallas import tpu as pltpu
from jax.sharding import PartitionSpec as P

HEADS = 16
EPS = 1e-06
LOG2E = math.log2(math.e)
GELU_A = math.sqrt(2.0 / math.pi)
GELU_B = 0.044715
VMEM_LIMIT = 60 * 2**20

f32 = jnp.float32
bf16 = jnp.bfloat16
NT = (((1,), (1,)), ((), ()))
NN = (((1,), (0,)), ((), ()))
TN = (((0,), (0,)), ((), ()))

VMEM = pl.BlockSpec(memory_space=pltpu.VMEM)
SMEM = pl.BlockSpec(memory_space=pltpu.SMEM)


def dot(left, right, dims):
    return lax.dot_general(left, right, dims, preferred_element_type=f32)


def shaped(shape, dtype=bf16):
    return jax.ShapeDtypeStruct(shape, dtype)


def norm(values):
    center = values - jnp.mean(values, axis=-1, keepdims=True)
    rstd = lax.rsqrt(jnp.mean(center * center, axis=-1, keepdims=True) + EPS)
    return center * rstd, rstd


def qkv_kernel(blk, core_ref, x_ref, mod_ref, w_ref, b_ref, other_ref, mine_ref, nt_ref, n_s):
    half, step = pl.program_id(0), pl.program_id(1)
    rows = x_ref.shape[0]

    @pl.when(half == 0)
    def _():
        parts = []
        for i in range(rows // blk):
            y, _ = norm(x_ref[i * blk : (i + 1) * blk].astype(f32))
            parts.append((y * (1.0 + mod_ref[i, 1:2]) + mod_ref[i, 0:1]).astype(bf16))
        normed = jnp.concatenate(parts, axis=0)
        n_s[step] = normed
        nt_ref[...] = normed.T

    result = (dot(n_s[step], w_ref[0], NN) + b_ref[0]).astype(bf16)

    @pl.when(half == 0)
    def _():
        other_ref[...] = result

    @pl.when(half == 1)
    def _():
        mine_ref[...] = result


def qkv(core, x, mod, w_half, b_half, blk):
    tokens, width = x.shape
    wide = w_half.shape[2]
    steps = 3
    rows = tokens // steps
    last = steps - 1
    return pl.pallas_call(
        functools.partial(qkv_kernel, blk),
        grid_spec=pltpu.PrefetchScalarGridSpec(
            num_scalar_prefetch=1,
            grid=(2, steps),
            in_specs=[
                pl.BlockSpec((rows, width), lambda h, s, c: (s, 0)),
                pl.BlockSpec((rows // blk, 6, width), lambda h, s, c: (s, 0, 0)),
                pl.BlockSpec((1, width, wide), lambda h, s, c: (1 - c[0] + h * (2 * c[0] - 1), 0, 0)),
                pl.BlockSpec((1, 1, wide), lambda h, s, c: (1 - c[0] + h * (2 * c[0] - 1), 0, 0)),
            ],
            out_specs=[
                pl.BlockSpec((rows, wide), lambda h, s, c: (jnp.where(h == 0, s, last), 0)),
                pl.BlockSpec((rows, wide), lambda h, s, c: (jnp.where(h == 0, 0, s), 0)),
                pl.BlockSpec((width, rows), lambda h, s, c: (0, jnp.where(h == 0, s, last))),
            ],
            scratch_shapes=[pltpu.VMEM((steps, rows, width), bf16)],
        ),
        out_shape=(shaped((tokens, wide)), shaped((tokens, wide)), shaped((width, tokens))),
        compiler_params=pltpu.CompilerParams(vmem_limit_bytes=VMEM_LIMIT),
        cost_estimate=pl.CostEstimate(
            flops=4 * tokens * width * wide, bytes_accessed=20 * 2**20, transcendentals=tokens
        ),
        name="qkv",
    )(core, x, mod, w_half, b_half)


def head_window(head, hd):
    first = head * hd
    start = pl.multiple_of((first // 128) * 128, 128)
    lane = lax.broadcasted_iota(jnp.int32, (1, 256), 1) + start
    inside = jnp.logical_and(lane >= first, lane < first + hd)
    return pl.ds(start, 256), inside


def gather_rows(dst, col, sources, base, count):
    pad = dst.shape[1]
    for i in range(count):
        for j, src in enumerate(sources):
            row = 256 * i + 128 * j
            dst[row : row + 128] = src[base + 128 * i : base + 128 * i + 128, col : col + pad]


def attend_kernel(heads, hd, count, shared, flag_ref, mine_ref, sib_ref, *rest):
    if shared:
        far_ref, *rest = rest
    o_mine, o_sib, stat, q_s, k_s, v_s, o_s = rest
    pad = q_s.shape[1]
    scale = LOG2E / math.sqrt(hd)
    base = mine_ref.shape[0] - 128 * count if shared else 0
    pair = (mine_ref, sib_ref)
    gather_rows(q_s, 0, pair, base, count)
    gather_rows(k_s, pad, pair, base, count)
    gather_rows(v_s, 2 * pad, pair, base, count)
    if shared:
        k_s[256 * count :] = far_ref[:, 0:pad]
        v_s[256 * count :] = far_ref[:, pad : 2 * pad]
    o_s[...] = jnp.zeros_like(o_s)
    stat[...] = jnp.zeros_like(stat)
    lane = lax.broadcasted_iota(jnp.int32, (1, 128), 1)

    def run(single):
        def body(head, carry):
            win, inside = head_window(head, hd)
            for i in range(count):
                rows = slice(256 * i, 256 * i + 256)
                keys = slice(None) if single else rows
                q = jnp.where(inside, q_s[rows, win], jnp.zeros((), bf16))
                s = dot(q, k_s[keys, win], NT)
                top = jnp.max(s, axis=1, keepdims=True)
                p = jnp.exp2((s - top) * scale)
                total = jnp.sum(p, axis=1, keepdims=True)
                o = dot(p.astype(bf16), v_s[keys, win], NN) / total
                o_s[rows, win] = jnp.where(inside, o.astype(bf16), o_s[rows, win])
                stat[rows] = jnp.where(lane == head, top * scale + jnp.log2(total), stat[rows])
            return carry

        lax.fori_loop(0, heads, body, 0)

    one = flag_ref[0] == 1
    pl.when(one)(lambda: run(True))
    pl.when(jnp.logical_not(one))(lambda: run(False))
    for i in range(count):
        o_mine[128 * i : 128 * i + 128] = o_s[256 * i : 256 * i + 128]
        o_sib[128 * i : 128 * i + 128] = o_s[256 * i + 128 : 256 * i + 256]


def attend(flag, mine, sib, far, heads, hd, count):
    pad = mine.shape[1] // 3
    keys = 256 * count + (0 if far is None else far.shape[0])
    tokens = 128 * count
    inputs = [flag, mine, sib] + ([] if far is None else [far])
    return pl.pallas_call(
        functools.partial(attend_kernel, heads, hd, count, far is not None),
        out_shape=(
            shaped((tokens, pad)),
            shaped((tokens, pad)),
            shaped((2 * tokens, 128), f32),
        ),
        in_specs=[SMEM] + [VMEM] * (len(inputs) - 1),
        out_specs=(VMEM,) * 3,
        scratch_shapes=[
            pltpu.VMEM((2 * tokens, pad), bf16),
            pltpu.VMEM((keys, pad), bf16),
            pltpu.VMEM((keys, pad), bf16),
            pltpu.VMEM((2 * tokens, pad), bf16),
        ],
        compiler_params=pltpu.CompilerParams(vmem_limit_bytes=VMEM_LIMIT),
        cost_estimate=pl.CostEstimate(
            flops=1024 * heads * tokens * keys,
            bytes_accessed=8 * 2**20,
            transcendentals=heads * 2 * tokens * keys,
        ),
        name="attend_far" if far is not None else "attend_near",
    )(*inputs)


def attend_back_kernel(heads, hd, count, shared, flag_ref, mine_ref, sib_ref, *rest):
    d_mine, d_sib, o_mine, o_sib, stat, *rest = rest
    if shared:
        far_ref, g_mine, g_sib, g_far, *rest = rest
    else:
        g_mine, g_sib, *rest = rest
    q_s, k_s, v_s, do_s, kt_s, dqt_s, dk_s, dv_s, p_s, ds_s, lse_s, dd_s = rest
    pad = q_s.shape[1]
    inv = 1.0 / math.sqrt(hd)
    scale = LOG2E * inv
    base = mine_ref.shape[0] - 128 * count if shared else 0
    pair = (mine_ref, sib_ref)
    gather_rows(q_s, 0, pair, base, count)
    gather_rows(k_s, pad, pair, base, count)
    gather_rows(v_s, 2 * pad, pair, base, count)
    gather_rows(do_s, 0, (d_mine, d_sib), 0, count)
    if shared:
        k_s[256 * count :] = far_ref[:, 0:pad]
        v_s[256 * count :] = far_ref[:, pad : 2 * pad]
    kt_s[...] = k_s[...].astype(f32).T
    dqt_s[...] = jnp.zeros_like(dqt_s)
    dk_s[...] = jnp.zeros_like(dk_s)
    dv_s[...] = jnp.zeros_like(dv_s)
    row = lax.broadcasted_iota(jnp.int32, (heads, pad), 0)
    col = lax.broadcasted_iota(jnp.int32, (heads, pad), 1)
    member = jnp.where(jnp.logical_and(col >= row * hd, col < row * hd + hd), 1.0, 0.0).astype(bf16)
    for i in range(count):
        rows = slice(256 * i, 256 * i + 256)
        lse_s[i] = stat[rows].T[0:heads]
        o = jnp.concatenate(
            [o_mine[128 * i : 128 * i + 128], o_sib[128 * i : 128 * i + 128]], axis=0
        )
        both = do_s[rows].astype(f32) * o.astype(f32)
        high = both.astype(bf16)
        low = (both - high.astype(f32)).astype(bf16)
        dd_s[i] = dot(member, high, NT) + dot(member, low, NT)

    def run(single):
        def body(head, carry):
            win, inside = head_window(head, hd)
            mine = pl.ds(pl.multiple_of(head * hd, 8), hd)
            zero = jnp.zeros((), bf16)
            for i in range(count):
                rows = slice(256 * i, 256 * i + 256)
                keys = slice(None) if single else rows
                q = jnp.where(inside, q_s[rows, win], zero)
                do = jnp.where(inside, do_s[rows, win], zero)
                lse = lse_s[i, pl.ds(head, 1)]
                dd = dd_s[i, pl.ds(head, 1)]
                s = dot(k_s[keys, win], q, NT)
                p = jnp.exp2(s * scale - lse)
                dp = dot(v_s[keys, win], do, NT)
                ds = (p * (dp - dd)).astype(bf16)
                p = p.astype(bf16)
                if single:
                    p_s[:, rows] = p
                    ds_s[:, rows] = ds
                else:
                    dv_s[rows, win] += dot(p, do, NN)
                    dk_s[rows, win] += dot(ds, q, NN)
                    dqt_s[mine, rows] = dot(kt_s[mine, rows].astype(bf16), ds, NN)
            if single:
                q = jnp.where(inside, q_s[:, win], zero)
                do = jnp.where(inside, do_s[:, win], zero)
                dv_s[:, win] += dot(p_s[...], do, NN)
                dk_s[:, win] += dot(ds_s[...], q, NN)
                dqt_s[mine, :] = dot(kt_s[mine, :].astype(bf16), ds_s[...], NN)
            return carry

        lax.fori_loop(0, heads, body, 0)

    one = flag_ref[0] == 1
    pl.when(one)(lambda: run(True))
    pl.when(jnp.logical_not(one))(lambda: run(False))
    for i in range(count):
        for j, dst in enumerate((g_mine, g_sib)):
            rows = slice(256 * i + 128 * j, 256 * i + 128 * j + 128)
            out = slice(128 * i, 128 * i + 128)
            dst[out, 0:pad] = (dqt_s[:, rows] * inv).T.astype(bf16)
            dst[out, pad : 2 * pad] = (dk_s[rows] * inv).astype(bf16)
            dst[out, 2 * pad : 3 * pad] = dv_s[rows].astype(bf16)
    if shared:
        g_far[:, 0:pad] = (dk_s[256 * count :] * inv).astype(bf16)
        g_far[:, pad : 2 * pad] = dv_s[256 * count :].astype(bf16)


def attend_back(flag, mine, sib, d_mine, d_sib, o_mine, o_sib, stat, far, heads, hd, count):
    pad = mine.shape[1] // 3
    tokens = 128 * count
    keys = 2 * tokens + (0 if far is None else far.shape[0])
    inputs = [flag, mine, sib, d_mine, d_sib, o_mine, o_sib, stat] + ([] if far is None else [far])
    outs = [shaped((tokens, 3 * pad)), shaped((tokens, 3 * pad))]
    if far is not None:
        outs.append(shaped((far.shape[0], 2 * pad)))
    return pl.pallas_call(
        functools.partial(attend_back_kernel, heads, hd, count, far is not None),
        out_shape=tuple(outs),
        in_specs=[SMEM] + [VMEM] * (len(inputs) - 1),
        out_specs=(VMEM,) * len(outs),
        scratch_shapes=[
            pltpu.VMEM((2 * tokens, pad), bf16),
            pltpu.VMEM((keys, pad), bf16),
            pltpu.VMEM((keys, pad), bf16),
            pltpu.VMEM((2 * tokens, pad), bf16),
            pltpu.VMEM((pad, keys), f32),
            pltpu.VMEM((pad, 2 * tokens), f32),
            pltpu.VMEM((keys, pad), f32),
            pltpu.VMEM((keys, pad), f32),
            pltpu.VMEM((keys, 2 * tokens), bf16),
            pltpu.VMEM((keys, 2 * tokens), bf16),
            pltpu.VMEM((count, heads, 256), f32),
            pltpu.VMEM((count, heads, 256), f32),
        ],
        compiler_params=pltpu.CompilerParams(vmem_limit_bytes=VMEM_LIMIT),
        cost_estimate=pl.CostEstimate(
            flops=2560 * heads * tokens * keys,
            bytes_accessed=12 * 2**20,
            transcendentals=heads * 2 * tokens * keys,
        ),
        name="attend_far_back" if far is not None else "attend_near_back",
    )(*inputs)


def middle_kernel(
    blk,
    core_ref,
    x_ref,
    cot_ref,
    am_ref,
    ao_ref,
    mod_ref,
    wpm_ref,
    wpo_ref,
    bp_ref,
    bd_ref,
    wu_ref,
    bu_ref,
    wd_ref,
    out_ref,
    gmid_ref,
    dom_ref,
    doo_ref,
    dwum_ref,
    dwuo_ref,
    dwd_ref,
    dbu_ref,
    dwpm_ref,
    dwpo_ref,
    dmod_ref,
    dbp_ref,
    dbd_ref,
    mid_s,
    br1_s,
    n_s,
    nt_s,
    db2_s,
    br2_s,
    gn_s,
    db1_s,
):
    step = pl.program_id(0)
    tokens, width = x_ref.shape
    blocks = tokens // blk
    part = width // 4

    @pl.when(step == 0)
    def _():
        br1_s[...] = (
            dot(am_ref[...], wpm_ref[...], NN) + dot(ao_ref[...], wpo_ref[...], NN) + bp_ref[...]
        )
        for i in range(blocks):
            rows = slice(i * blk, (i + 1) * blk)
            mid = x_ref[rows].astype(f32) + mod_ref[i, 2:3] * br1_s[rows]
            mid_s[rows] = mid
            y, _ = norm(mid)
            n = (y * (1.0 + mod_ref[i, 4:5]) + mod_ref[i, 3:4]).astype(bf16)
            n_s[rows] = n
            db2_s[rows] = (mod_ref[i, 5:6] * cot_ref[rows].astype(f32)).astype(bf16)
        for g in range(4):
            place = (g % 2 + core_ref[0] - 2 * (g % 2) * core_ref[0]) * (2 * part) + (g // 2) * part
            nt_s[pl.ds(pl.multiple_of(place, 16), part)] = (
                n_s[:, g * part : (g + 1) * part].astype(f32).T.astype(bf16)
            )
        br2_s[...] = jnp.zeros_like(br2_s)
        gn_s[...] = jnp.zeros_like(gn_s)

    pre = dot(n_s[...], wu_ref[...], NN) + bu_ref[...]
    square = pre * pre
    t = jnp.tanh(pre * (GELU_A + (GELU_A * GELU_B) * square))
    hidden = (0.5 * pre * (1.0 + t)).astype(bf16)
    slope = 0.5 * (1.0 + t) + 0.5 * pre * (1.0 - t * t) * (
        GELU_A + (3.0 * GELU_A * GELU_B) * square
    )
    br2_s[...] += dot(hidden, wd_ref[...], NN)
    gpre = dot(db2_s[...], wd_ref[...], NT) * slope
    gp = gpre.astype(bf16)
    gn_s[...] += dot(gp, wu_ref[...], NT)
    dwd_ref[...] = dot(hidden, db2_s[...], TN).astype(bf16)
    dwum_ref[...] = dot(nt_s[0 : 2 * part], gp, NN).astype(bf16)
    dwuo_ref[...] = dot(nt_s[2 * part : 4 * part], gp, NN).astype(bf16)
    dbu_ref[...] = jnp.sum(gpre, axis=0, keepdims=True)

    @pl.when(step == pl.num_programs(0) - 1)
    def _():
        dbp = jnp.zeros((1, width), f32)
        dbd = jnp.zeros((1, width), f32)
        for i in range(blocks):
            rows = slice(i * blk, (i + 1) * blk)
            cot = cot_ref[rows].astype(f32)
            br2 = br2_s[rows] + bd_ref[...]
            mid = mid_s[rows]
            out_ref[rows] = (mid + mod_ref[i, 5:6] * br2).astype(bf16)
            y, rstd = norm(mid)
            gn = gn_s[rows]
            u = gn * (1.0 + mod_ref[i, 4:5])
            gmid = cot + rstd * (
                u
                - jnp.mean(u, axis=-1, keepdims=True)
                - y * jnp.mean(u * y, axis=-1, keepdims=True)
            )
            gmid_ref[rows] = gmid.astype(bf16)
            db1 = mod_ref[i, 2:3] * gmid
            db1_s[rows] = db1.astype(bf16)
            dbp += jnp.sum(db1, axis=0, keepdims=True)
            dbd += jnp.sum(db2_s[rows].astype(f32), axis=0, keepdims=True)
            dmod_ref[i, 0:1] = jnp.sum(gmid * br1_s[rows], axis=0, keepdims=True)
            dmod_ref[i, 1:2] = jnp.sum(gn, axis=0, keepdims=True)
            dmod_ref[i, 2:3] = jnp.sum(gn * y, axis=0, keepdims=True)
            dmod_ref[i, 3:4] = jnp.sum(cot * br2, axis=0, keepdims=True)
        dbp_ref[...] = dbp
        dbd_ref[...] = dbd
        dom_ref[...] = dot(db1_s[...], wpm_ref[...], NT).astype(bf16)
        doo_ref[...] = dot(db1_s[...], wpo_ref[...], NT).astype(bf16)
        dwpm_ref[...] = dot(am_ref[...], db1_s[...], TN).astype(bf16)
        dwpo_ref[...] = dot(ao_ref[...], db1_s[...], TN).astype(bf16)


def middle(core, x, cot, att_m, att_o, mod, wp_m, wp_o, b_proj, b_down, w_up, b_up, w_down, blk):
    tokens, width = x.shape
    pad = att_m.shape[1]
    hidden = w_up.shape[1]
    chunk = 512
    steps = hidden // chunk
    half = width // 2

    def whole(shape):
        return pl.BlockSpec(shape, lambda j, c: (0,) * len(shape))

    return pl.pallas_call(
        functools.partial(middle_kernel, blk),
        grid_spec=pltpu.PrefetchScalarGridSpec(
            num_scalar_prefetch=1,
            grid=(steps,),
            in_specs=[VMEM] * 9
            + [
                pl.BlockSpec((width, chunk), lambda j, c: (0, j)),
                pl.BlockSpec((1, chunk), lambda j, c: (0, j)),
                pl.BlockSpec((chunk, width), lambda j, c: (j, 0)),
            ],
            out_specs=[VMEM] * 4
            + [
                pl.BlockSpec((half, chunk), lambda j, c: (0, j)),
                pl.BlockSpec((half, chunk), lambda j, c: (0, j)),
                pl.BlockSpec((chunk, width), lambda j, c: (j, 0)),
                pl.BlockSpec((1, chunk), lambda j, c: (0, j)),
            ]
            + [VMEM] * 5,
            scratch_shapes=[
                pltpu.VMEM((tokens, width), f32),
                pltpu.VMEM((tokens, width), f32),
                pltpu.VMEM((tokens, width), bf16),
                pltpu.VMEM((width, tokens), bf16),
                pltpu.VMEM((tokens, width), bf16),
                pltpu.VMEM((tokens, width), f32),
                pltpu.VMEM((tokens, width), f32),
                pltpu.VMEM((tokens, width), bf16),
            ],
        ),
        out_shape=(
            shaped((tokens, width)),
            shaped((tokens, width)),
            shaped((tokens, pad)),
            shaped((tokens, pad)),
            shaped((half, hidden)),
            shaped((half, hidden)),
            shaped((hidden, width)),
            shaped((1, hidden), f32),
            shaped((pad, width)),
            shaped((pad, width)),
            shaped((tokens // blk, 4, width), f32),
            shaped((1, width), f32),
            shaped((1, width), f32),
        ),
        compiler_params=pltpu.CompilerParams(vmem_limit_bytes=VMEM_LIMIT),
        cost_estimate=pl.CostEstimate(
            flops=2 * tokens * width * (6 * hidden + 6 * pad),
            bytes_accessed=60 * 2**20,
            transcendentals=tokens * hidden,
        ),
        name="middle",
    )(core, x, cot, att_m, att_o, mod, wp_m, wp_o, b_proj, b_down, w_up, b_up, w_down)


def first_back_kernel(blk, x_ref, ga_ref, gb_ref, gmid_ref, mod_ref, out_ref, dmod_ref):
    for i in range(x_ref.shape[0] // blk):
        rows = slice(i * blk, (i + 1) * blk)
        y, rstd = norm(x_ref[rows].astype(f32))
        gn = ga_ref[rows].astype(f32) + gb_ref[rows].astype(f32)
        u = gn * (1.0 + mod_ref[i, 1:2])
        back = rstd * (
            u - jnp.mean(u, axis=-1, keepdims=True) - y * jnp.mean(u * y, axis=-1, keepdims=True)
        )
        out_ref[rows] = (gmid_ref[rows].astype(f32) + back).astype(bf16)
        dmod_ref[i, 0:1] = jnp.sum(gn, axis=0, keepdims=True)
        dmod_ref[i, 1:2] = jnp.sum(gn * y, axis=0, keepdims=True)


def first_back(x, part_a, part_b, gmid, mod, blk):
    tokens, width = x.shape
    steps = 3
    rows = tokens // steps
    each = pl.BlockSpec((rows, width), lambda s: (s, 0))
    return pl.pallas_call(
        functools.partial(first_back_kernel, blk),
        grid=(steps,),
        in_specs=[each] * 4 + [pl.BlockSpec((rows // blk, 6, width), lambda s: (s, 0, 0))],
        out_specs=[each, pl.BlockSpec((rows // blk, 2, width), lambda s: (s, 0, 0))],
        out_shape=(shaped((tokens, width)), shaped((tokens // blk, 2, width), f32)),
        compiler_params=pltpu.CompilerParams(vmem_limit_bytes=VMEM_LIMIT),
        cost_estimate=pl.CostEstimate(
            flops=20 * tokens * width, bytes_accessed=10 * tokens * width, transcendentals=tokens
        ),
        name="first_back",
    )(x, part_a, part_b, gmid, mod)


def place_kernel(order_ref, in_ref, out_ref):
    out_ref[...] = in_ref[...].astype(out_ref.dtype)


def place(order, tiles, dtype):
    count = tiles.shape[0]
    block = (1,) + tiles.shape[1:]
    return pl.pallas_call(
        place_kernel,
        grid_spec=pltpu.PrefetchScalarGridSpec(
            num_scalar_prefetch=1,
            grid=(count,),
            in_specs=[pl.BlockSpec(block, lambda i, o: (o[i], 0, 0))],
            out_specs=pl.BlockSpec(block, lambda i, o: (i, 0, 0)),
        ),
        out_shape=shaped(tiles.shape, dtype),
        cost_estimate=pl.CostEstimate(
            flops=0, bytes_accessed=6 * math.prod(tiles.shape), transcendentals=0
        ),
        name="place",
    )(order, tiles)


def pick(values, index, axis=0):
    return lax.dynamic_index_in_dim(values, index, axis, keepdims=False)


def over_core(v):
    return lax.ppermute(v, "row", [(r, r ^ 1) for r in range(4)])


def over_x(v):
    return lax.ppermute(v, "row", [(r, r ^ 2) for r in range(4)])


def over_col(v, far):
    return lax.ppermute(v, "col", [(i, i ^ far) for i in range(4)])


def over_plane(v, dx, dz):
    swap = [(i, ((i // 4) ^ (2 * dx)) * 4 + ((i % 4) ^ dz)) for i in range(16)]
    return lax.ppermute(v, ("row", "col"), swap)


def over_img(v):
    if lax.axis_size("img") == 2:
        return v.astype(f32) + lax.ppermute(v, "img", [(0, 1), (1, 0)]).astype(f32)
    return lax.psum(v, "img").astype(f32)


def plus(a, b):
    return (a.astype(f32) + b.astype(f32)).astype(bf16)


def shards(
    tokens,
    conditioning,
    images_in_slot,
    w_qkv,
    b_qv,
    w_proj,
    b_proj,
    w_up,
    b_up,
    w_down,
    b_down,
    w_ada,
    b_ada,
    cotangent,
):
    slots, rows_tile, cols_tile, width = tokens.shape
    tile = rows_tile * cols_tile
    blk = 2 * tile
    count = slots * tile
    main = 8 * tile
    hd = width // HEADS
    heads = HEADS // 2
    half = width // 2
    pad = -(-half // 128) * 128
    hidden = w_up.shape[1]
    r, z = lax.axis_index("row"), lax.axis_index("col")
    x, core = r // 2, r % 2
    core_arr = core.reshape(1).astype(jnp.int32)
    assert lax.axis_size("row") == 4 and lax.axis_size("col") == 4 and slots == 12

    def spread(values):
        grouped = values.reshape(4, 3, tile, width)
        near, far, shared = [], [], []
        for dz in range(4):
            group = pick(grouped, z ^ dz)
            own = jnp.stack([pick(group, x), group[2]])
            other = pick(group, 1 - x)
            if dz:
                own = over_plane(own, 0, dz)
            near.append(own[0])
            shared.append(own[1])
            far.append(over_plane(other, 1, dz))
        return jnp.concatenate(near + far + shared, axis=0)

    def collect(values, dtype):
        tiles = values.reshape(12, tile, width)
        near, far, shared = [], [], []
        for dz in range(4):
            own = jnp.stack([tiles[dz], tiles[8 + dz]])
            if dz:
                own = over_plane(own, 0, dz)
            near.append(own[0])
            shared.append(own[1])
            far.append(over_plane(tiles[4 + dz], 1, dz))
        stacked = jnp.stack(near + far + shared)
        slot = jnp.arange(12, dtype=jnp.int32)
        kind = slot % 3
        dz = (slot // 3) ^ z
        order = jnp.where(kind == 2, 8 + dz, ((kind ^ x) & 1) * 4 + dz)
        return place(order, stacked, dtype).reshape(tokens.shape)

    inputs = spread(tokens)
    upstream = spread(cotangent)

    four_way = images_in_slot == 4
    kinds = pick(four_way.reshape(4, 3), z)
    main_four, shared_four = pick(kinds, x), kinds[2]
    quarter = jnp.stack([2 * (x ^ dx) + ((z // 2) ^ dz) for dx in range(2) for dz in range(2)])
    picks = jnp.concatenate(
        [jnp.where(main_four, quarter, 0), jnp.where(shared_four, quarter[:2], 0)]
    )
    places = jnp.concatenate([jnp.full((4,), x, jnp.int32), jnp.full((2,), 2, jnp.int32)]) * 4 + picks
    flag_main = jnp.where(main_four, 0, 1).reshape(1).astype(jnp.int32)
    flag_shared = jnp.where(shared_four, 0, 1).reshape(1).astype(jnp.int32)
    cond = conditioning.astype(f32)
    silu = jax.nn.silu(cond).astype(bf16)
    silu_groups = silu.reshape(4, 12, width)
    chosen = jnp.take(pick(silu_groups, z), places, axis=0)
    mod = (jnp.dot(chosen, w_ada, preferred_element_type=f32) + b_ada).reshape(6, 6, width)

    def widen(v, axis):
        return jnp.pad(v, [(0, pad - half) if a == axis else (0, 0) for a in range(v.ndim)])

    w_half = widen(w_qkv.reshape(width, 3, 2, half), 3).transpose(2, 0, 1, 3)
    w_half = w_half.reshape(2, width, 3 * pad)
    b_three = jnp.stack([b_qv[:width], jnp.zeros_like(b_qv[:width]), b_qv[width:]])
    b_half = widen(b_three.reshape(3, 2, half).astype(f32), 2).transpose(1, 0, 2)
    b_half = b_half.reshape(2, 1, 3 * pad)
    w_proj_half = widen(w_proj.reshape(2, half, width), 1)
    wp_mine, wp_other = pick(w_proj_half, core), pick(w_proj_half, 1 - core)

    qkv_other, qkv_mine, normed_t = qkv(core_arr, inputs, mod, w_half, b_half, blk)
    qkv_sib = over_core(qkv_other)
    normed_sib = over_core(normed_t)
    far_kv = over_x(jnp.concatenate([qkv_mine[main:, pad:], qkv_sib[main:, pad:]], axis=0))
    om_near, os_near, stat_near = attend(flag_main, qkv_mine, qkv_sib, None, heads, hd, 4)
    back_near = over_core(os_near)
    om_far, os_far, stat_far = attend(flag_shared, qkv_mine, qkv_sib, far_kv, heads, hd, 2)
    back_far = over_core(os_far)
    att_mine = jnp.concatenate([om_near, om_far], axis=0)
    att_other = jnp.concatenate([back_near, back_far], axis=0)

    (
        out,
        gmid,
        do_mine,
        do_other,
        dwu_mine,
        dwu_other,
        dwd,
        dbu,
        dwp_mine,
        dwp_other,
        dmod_mid,
        dbp,
        dbd,
    ) = middle(
        core_arr,
        inputs,
        upstream,
        att_mine,
        att_other,
        mod,
        wp_mine,
        wp_other,
        b_proj.astype(f32).reshape(1, width),
        b_down.astype(f32).reshape(1, width),
        w_up,
        b_up.astype(f32).reshape(1, hidden),
        w_down,
        blk,
    )
    output = collect(out, bf16)
    do_sib = over_core(do_other)

    def reduce_plane(mine):
        got = over_x(pick(mine, 1 - x))
        mine = plus(pick(mine, x), got)
        return reduce_col(mine)

    def reduce_col(mine):
        split = mine.reshape((2, 2) + mine.shape[1:])
        got = over_col(pick(split, 1 - z % 2, 1), 1)
        mine = plus(pick(split, z % 2, 1), got)
        got = over_col(pick(mine, 1 - z // 2), 2)
        mine = plus(pick(mine, z // 2), got)
        return over_img(mine)

    dwd_halves = dwd.reshape(2, 2, hidden // 4, width)
    dwd_sum = plus(pick(dwd_halves, core, 1), over_core(pick(dwd_halves, 1 - core, 1)))
    grad_w_down = reduce_plane(dwd_sum.reshape(2, 4, hidden // 16, width))
    dwu_sum = plus(dwu_mine, over_core(dwu_other))
    grad_w_up = reduce_plane(dwu_sum.reshape(2, 4, width // 16, hidden))
    dwp = jnp.stack([dwp_mine, dwp_other])
    dwp = jnp.stack([pick(dwp, core), pick(dwp, 1 - core)])[:, :half]
    dwp = dwp.reshape(2, 2, half // 2, width)
    dwp_sum = plus(pick(dwp, core, 1), over_core(pick(dwp, 1 - core, 1)))
    grad_w_proj = reduce_plane(dwp_sum.reshape(2, 4, width // 16, width))

    gm_far, gs_far, g_far = attend_back(
        flag_shared,
        qkv_mine,
        qkv_sib,
        do_mine[main:],
        do_sib[main:],
        om_far,
        os_far,
        stat_far,
        far_kv,
        heads,
        hd,
        2,
    )
    far_back = over_x(g_far)
    gm_near, gs_near = attend_back(
        flag_main, qkv_mine, qkv_sib, do_mine, do_sib, om_near, os_near, stat_near, None, heads, hd, 4
    )
    gm_far = jnp.concatenate([gm_far[:, :pad], plus(gm_far[:, pad:], far_back[: count - main])], 1)
    gs_far = jnp.concatenate([gs_far[:, :pad], plus(gs_far[:, pad:], far_back[count - main :])], 1)
    g_mine = jnp.concatenate([gm_near, gm_far], axis=0)
    g_sib = jnp.concatenate([gs_near, gs_far], axis=0)
    w_half_mine = pick(w_half, core)
    gn_other = over_core(dot(g_sib, w_half_mine, NT).astype(bf16))
    gn_mine = dot(g_mine, w_half_mine, NT).astype(bf16)
    dwq = (dot(normed_t, g_mine, NN) + dot(normed_sib, g_sib, NN)).astype(bf16)
    dwq = reduce_plane(
        dwq.reshape(2, 2, 4, width // 16, 3 * pad).transpose(0, 2, 1, 3, 4)
    )
    swap = over_core(pick(dwq, 1 - core).astype(bf16))
    parts = jnp.stack([pick(dwq, core), swap.astype(f32)])
    parts = jnp.stack([pick(parts, core), pick(parts, 1 - core)])
    parts = parts.reshape(2, width // 16, 3, pad)[..., :half]
    grad_w_qkv = parts.transpose(1, 2, 0, 3).reshape(width // 16, 3 * width)

    grad_x, dmod_first = first_back(inputs, gn_mine, gn_other, gmid, mod, blk)
    grad_tokens = collect(grad_x, f32)

    one_hot = (jnp.arange(12, dtype=jnp.int32)[:, None] == places[None, :]).astype(f32)
    silu_rel = jnp.concatenate([pick(silu_groups, z ^ dz) for dz in range(4)], axis=0)
    rank = r * 4 + z
    silu_rows = lax.dynamic_slice_in_dim(silu_rel, rank * (width // 16), width // 16, 1)

    def modulation_grads(dmod, columns):
        values = jnp.sum(one_hot[:, :, None] * dmod.reshape(1, 6, -1), axis=1).astype(bf16)
        values = plus(values, over_core(values))
        values = plus(values, over_x(values))
        every = jnp.concatenate(
            [values] + [over_col(values, dz) for dz in range(1, 4)], axis=0
        )
        d_w = over_img(dot(silu_rows, every, TN).astype(bf16))
        d_b = jnp.sum(every.astype(f32), axis=0)
        d_s = dot(every, w_ada[:, columns], NT)
        return d_w, d_b, d_s

    late = modulation_grads(dmod_first, slice(0, 2 * width))
    early = modulation_grads(dmod_mid, slice(2 * width, 6 * width))
    grad_w_ada = jnp.concatenate([late[0], early[0]], axis=1)
    d_s = (late[2] + early[2]).reshape(4, 12, width)
    d_s = jnp.stack([pick(d_s, z ^ g) for g in range(4)]).reshape(slots, 4, width)
    sig = jax.nn.sigmoid(cond)
    grad_conditioning = d_s * (sig * (1.0 + cond * (1.0 - sig)))

    db_three = jnp.sum(g_mine.astype(f32), axis=0) + jnp.sum(g_sib.astype(f32), axis=0)
    db_three = db_three.reshape(3, pad)[:, :half]
    db_three = jnp.where(
        (jnp.arange(2) == core)[None, :, None], db_three[:, None, :], 0.0
    ).reshape(3, width)
    small = jnp.concatenate([db_three[0], db_three[2], dbp[0], dbu[0], dbd[0]])
    small = lax.psum(small, ("row", "col", "img"))
    d_ada = jnp.concatenate([late[1], early[1]])
    d_ada = lax.dynamic_slice_in_dim(d_ada, rank * (6 * width // 16), 6 * width // 16, 0)
    grad_b_ada = over_img(d_ada)

    def own(start, size):
        return lax.dynamic_slice_in_dim(small, start + rank * (size // 16), size // 16, 0)

    return (
        output,
        grad_tokens,
        grad_conditioning,
        grad_w_qkv,
        own(0, 2 * width),
        grad_w_proj,
        own(2 * width, width),
        grad_w_up,
        own(3 * width, hidden),
        grad_w_down,
        own(3 * width + hidden, width),
        grad_w_ada,
        grad_b_ada,
    )


def solution(mesh):
    grid = P("img", "row", "col", None)
    plane = ("row", "col")
    return jax.shard_map(
        shards,
        mesh=mesh,
        in_specs=(grid, P("img", None, None), P("img")) + (P(),) * 10 + (grid,),
        out_specs=(grid, grid, P("img", None, None))
        + (P(plane, None), P(plane)) * 5,
        check_vma=False,
    )
```

```python
import functools
import math

import jax
import jax.numpy as jnp
from jax import lax
from jax.experimental import pallas as pl
from jax.experimental.pallas import tpu as pltpu
from jax.sharding import PartitionSpec as P

HEADS = 16
EPS = 1e-06
LOG2E = math.log2(math.e)
GELU_A = math.sqrt(2.0 / math.pi)
GELU_B = 0.044715
VMEM_LIMIT = 60 * 2**20

f32 = jnp.float32
bf16 = jnp.bfloat16
NT = (((1,), (1,)), ((), ()))
NN = (((1,), (0,)), ((), ()))
TN = (((0,), (0,)), ((), ()))

VMEM = pl.BlockSpec(memory_space=pltpu.VMEM)
SMEM = pl.BlockSpec(memory_space=pltpu.SMEM)


def dot(left, right, dims):
    return lax.dot_general(left, right, dims, preferred_element_type=f32)


def shaped(shape, dtype=bf16):
    return jax.ShapeDtypeStruct(shape, dtype)


def norm(values):
    center = values - jnp.mean(values, axis=-1, keepdims=True)
    rstd = lax.rsqrt(jnp.mean(center * center, axis=-1, keepdims=True) + EPS)
    return center * rstd, rstd


def plus(a, b):
    return (a.astype(f32) + b.astype(f32)).astype(bf16)


def qkv_kernel(blk, core_ref, x_ref, mod_ref, w_ref, b_ref, other_ref, mine_ref, nt_ref, n_s):
    half, step = pl.program_id(0), pl.program_id(1)
    rows = x_ref.shape[0]

    @pl.when(half == 0)
    def _():
        parts = []
        for i in range(rows // blk):
            y, _ = norm(x_ref[i * blk : (i + 1) * blk].astype(f32))
            parts.append((y * (1.0 + mod_ref[i, 1:2]) + mod_ref[i, 0:1]).astype(bf16))
        normed = jnp.concatenate(parts, axis=0)
        n_s[step] = normed
        nt_ref[...] = normed.T

    result = (dot(n_s[step], w_ref[0], NN) + b_ref[0]).astype(bf16)

    @pl.when(half == 0)
    def _():
        other_ref[...] = result

    @pl.when(half == 1)
    def _():
        mine_ref[...] = result


def qkv(core, x, mod, w_half, b_half, blk):
    tokens, width = x.shape
    wide = w_half.shape[2]
    steps = 3
    rows = tokens // steps
    last = steps - 1
    return pl.pallas_call(
        functools.partial(qkv_kernel, blk),
        grid_spec=pltpu.PrefetchScalarGridSpec(
            num_scalar_prefetch=1,
            grid=(2, steps),
            in_specs=[
                pl.BlockSpec((rows, width), lambda h, s, c: (s, 0)),
                pl.BlockSpec((rows // blk, 6, width), lambda h, s, c: (s, 0, 0)),
                pl.BlockSpec((1, width, wide), lambda h, s, c: (1 - c[0] + h * (2 * c[0] - 1), 0, 0)),
                pl.BlockSpec((1, 1, wide), lambda h, s, c: (1 - c[0] + h * (2 * c[0] - 1), 0, 0)),
            ],
            out_specs=[
                pl.BlockSpec((rows, wide), lambda h, s, c: (jnp.where(h == 0, s, last), 0)),
                pl.BlockSpec((rows, wide), lambda h, s, c: (jnp.where(h == 0, 0, s), 0)),
                pl.BlockSpec((width, rows), lambda h, s, c: (0, jnp.where(h == 0, s, last))),
            ],
            scratch_shapes=[pltpu.VMEM((steps, rows, width), bf16)],
        ),
        out_shape=(shaped((tokens, wide)), shaped((tokens, wide)), shaped((width, tokens))),
        compiler_params=pltpu.CompilerParams(vmem_limit_bytes=VMEM_LIMIT),
        cost_estimate=pl.CostEstimate(
            flops=4 * tokens * width * wide, bytes_accessed=20 * 2**20, transcendentals=tokens
        ),
        name="qkv",
    )(core, x, mod, w_half, b_half)


def head_window(head, hd):
    first = head * hd
    start = pl.multiple_of((first // 128) * 128, 128)
    lane = lax.broadcasted_iota(jnp.int32, (1, 256), 1) + start
    inside = jnp.logical_and(lane >= first, lane < first + hd)
    return pl.ds(start, 256), inside


def gather_rows(dst, col, sources, base, count):
    pad = dst.shape[1]
    for i in range(count):
        for j, src in enumerate(sources):
            row = 256 * i + 128 * j
            dst[row : row + 128] = src[base + 128 * i : base + 128 * i + 128, col : col + pad]


def attend_kernel(heads, hd, count, shared, flag_ref, mine_ref, sib_ref, *rest):
    if shared:
        far_ref, *rest = rest
    o_mine, o_sib, stat, q_s, k_s, v_s, o_s = rest
    pad = q_s.shape[1]
    scale = LOG2E / math.sqrt(hd)
    base = mine_ref.shape[0] - 128 * count if shared else 0
    pair = (mine_ref, sib_ref)
    gather_rows(q_s, 0, pair, base, count)
    gather_rows(k_s, pad, pair, base, count)
    gather_rows(v_s, 2 * pad, pair, base, count)
    if shared:
        k_s[256 * count :] = far_ref[:, 0:pad]
        v_s[256 * count :] = far_ref[:, pad : 2 * pad]
    o_s[...] = jnp.zeros_like(o_s)
    stat[...] = jnp.zeros_like(stat)
    lane = lax.broadcasted_iota(jnp.int32, (1, 128), 1)

    def run(single):
        def body(head, carry):
            win, inside = head_window(head, hd)
            for i in range(count):
                rows = slice(256 * i, 256 * i + 256)
                keys = slice(None) if single else rows
                q = jnp.where(inside, q_s[rows, win], jnp.zeros((), bf16))
                s = dot(q, k_s[keys, win], NT)
                top = jnp.max(s, axis=1, keepdims=True)
                p = jnp.exp2((s - top) * scale)
                total = jnp.sum(p, axis=1, keepdims=True)
                o = dot(p.astype(bf16), v_s[keys, win], NN) / total
                o_s[rows, win] = jnp.where(inside, o.astype(bf16), o_s[rows, win])
                stat[rows] = jnp.where(lane == head, top * scale + jnp.log2(total), stat[rows])
            return carry

        lax.fori_loop(0, heads, body, 0)

    one = flag_ref[0] == 1
    pl.when(one)(lambda: run(True))
    pl.when(jnp.logical_not(one))(lambda: run(False))
    for i in range(count):
        o_mine[128 * i : 128 * i + 128] = o_s[256 * i : 256 * i + 128]
        o_sib[128 * i : 128 * i + 128] = o_s[256 * i + 128 : 256 * i + 256]


def attend(flag, mine, sib, far, heads, hd, count):
    pad = mine.shape[1] // 3
    keys = 256 * count + (0 if far is None else far.shape[0])
    tokens = 128 * count
    inputs = [flag, mine, sib] + ([] if far is None else [far])
    return pl.pallas_call(
        functools.partial(attend_kernel, heads, hd, count, far is not None),
        out_shape=(
            shaped((tokens, pad)),
            shaped((tokens, pad)),
            shaped((2 * tokens, 128), f32),
        ),
        in_specs=[SMEM] + [VMEM] * (len(inputs) - 1),
        out_specs=(VMEM,) * 3,
        scratch_shapes=[
            pltpu.VMEM((2 * tokens, pad), bf16),
            pltpu.VMEM((keys, pad), bf16),
            pltpu.VMEM((keys, pad), bf16),
            pltpu.VMEM((2 * tokens, pad), bf16),
        ],
        compiler_params=pltpu.CompilerParams(vmem_limit_bytes=VMEM_LIMIT),
        cost_estimate=pl.CostEstimate(
            flops=1024 * heads * tokens * keys,
            bytes_accessed=8 * 2**20,
            transcendentals=heads * 2 * tokens * keys,
        ),
        name="attend_far" if far is not None else "attend_near",
    )(*inputs)


def attend_back_kernel(heads, hd, count, shared, flag_ref, mine_ref, sib_ref, *rest):
    d_mine, d_sib, o_mine, o_sib, stat, *rest = rest
    if shared:
        far_ref, g_mine, g_sib, g_far, *rest = rest
    else:
        g_mine, g_sib, *rest = rest
    q_s, k_s, v_s, do_s, kt_s, dqt_s, dk_s, dv_s, p_s, ds_s, lse_s, dd_s = rest
    pad = q_s.shape[1]
    inv = 1.0 / math.sqrt(hd)
    scale = LOG2E * inv
    base = mine_ref.shape[0] - 128 * count if shared else 0
    pair = (mine_ref, sib_ref)
    gather_rows(q_s, 0, pair, base, count)
    gather_rows(k_s, pad, pair, base, count)
    gather_rows(v_s, 2 * pad, pair, base, count)
    gather_rows(do_s, 0, (d_mine, d_sib), 0, count)
    if shared:
        k_s[256 * count :] = far_ref[:, 0:pad]
        v_s[256 * count :] = far_ref[:, pad : 2 * pad]
    kt_s[...] = k_s[...].astype(f32).T
    dqt_s[...] = jnp.zeros_like(dqt_s)
    dk_s[...] = jnp.zeros_like(dk_s)
    dv_s[...] = jnp.zeros_like(dv_s)
    row = lax.broadcasted_iota(jnp.int32, (heads, pad), 0)
    col = lax.broadcasted_iota(jnp.int32, (heads, pad), 1)
    member = jnp.where(jnp.logical_and(col >= row * hd, col < row * hd + hd), 1.0, 0.0).astype(bf16)
    for i in range(count):
        rows = slice(256 * i, 256 * i + 256)
        lse_s[i] = stat[rows].T[0:heads]
        o = jnp.concatenate(
            [o_mine[128 * i : 128 * i + 128], o_sib[128 * i : 128 * i + 128]], axis=0
        )
        both = do_s[rows].astype(f32) * o.astype(f32)
        high = both.astype(bf16)
        low = (both - high.astype(f32)).astype(bf16)
        dd_s[i] = dot(member, high, NT) + dot(member, low, NT)

    def run(single):
        def body(head, carry):
            win, inside = head_window(head, hd)
            mine = pl.ds(pl.multiple_of(head * hd, 8), hd)
            zero = jnp.zeros((), bf16)
            for i in range(count):
                rows = slice(256 * i, 256 * i + 256)
                keys = slice(None) if single else rows
                q = jnp.where(inside, q_s[rows, win], zero)
                do = jnp.where(inside, do_s[rows, win], zero)
                lse = lse_s[i, pl.ds(head, 1)]
                dd = dd_s[i, pl.ds(head, 1)]
                s = dot(k_s[keys, win], q, NT)
                p = jnp.exp2(s * scale - lse)
                dp = dot(v_s[keys, win], do, NT)
                ds = (p * (dp - dd)).astype(bf16)
                p = p.astype(bf16)
                if single:
                    p_s[:, rows] = p
                    ds_s[:, rows] = ds
                else:
                    dv_s[rows, win] += dot(p, do, NN)
                    dk_s[rows, win] += dot(ds, q, NN)
                    dqt_s[mine, rows] = dot(kt_s[mine, rows].astype(bf16), ds, NN)
            if single:
                q = jnp.where(inside, q_s[:, win], zero)
                do = jnp.where(inside, do_s[:, win], zero)
                dv_s[:, win] += dot(p_s[...], do, NN)
                dk_s[:, win] += dot(ds_s[...], q, NN)
                dqt_s[mine, :] = dot(kt_s[mine, :].astype(bf16), ds_s[...], NN)
            return carry

        lax.fori_loop(0, heads, body, 0)

    one = flag_ref[0] == 1
    pl.when(one)(lambda: run(True))
    pl.when(jnp.logical_not(one))(lambda: run(False))
    for i in range(count):
        for j, dst in enumerate((g_mine, g_sib)):
            rows = slice(256 * i + 128 * j, 256 * i + 128 * j + 128)
            out = slice(128 * i, 128 * i + 128)
            dst[out, 0:pad] = (dqt_s[:, rows] * inv).T.astype(bf16)
            dst[out, pad : 2 * pad] = (dk_s[rows] * inv).astype(bf16)
            dst[out, 2 * pad : 3 * pad] = dv_s[rows].astype(bf16)
    if shared:
        g_far[:, 0:pad] = (dk_s[256 * count :] * inv).astype(bf16)
        g_far[:, pad : 2 * pad] = dv_s[256 * count :].astype(bf16)


def attend_back(flag, mine, sib, d_mine, d_sib, o_mine, o_sib, stat, far, heads, hd, count):
    pad = mine.shape[1] // 3
    tokens = 128 * count
    keys = 2 * tokens + (0 if far is None else far.shape[0])
    inputs = [flag, mine, sib, d_mine, d_sib, o_mine, o_sib, stat] + ([] if far is None else [far])
    outs = [shaped((tokens, 3 * pad)), shaped((tokens, 3 * pad))]
    if far is not None:
        outs.append(shaped((far.shape[0], 2 * pad)))
    return pl.pallas_call(
        functools.partial(attend_back_kernel, heads, hd, count, far is not None),
        out_shape=tuple(outs),
        in_specs=[SMEM] + [VMEM] * (len(inputs) - 1),
        out_specs=(VMEM,) * len(outs),
        scratch_shapes=[
            pltpu.VMEM((2 * tokens, pad), bf16),
            pltpu.VMEM((keys, pad), bf16),
            pltpu.VMEM((keys, pad), bf16),
            pltpu.VMEM((2 * tokens, pad), bf16),
            pltpu.VMEM((pad, keys), f32),
            pltpu.VMEM((pad, 2 * tokens), f32),
            pltpu.VMEM((keys, pad), f32),
            pltpu.VMEM((keys, pad), f32),
            pltpu.VMEM((keys, 2 * tokens), bf16),
            pltpu.VMEM((keys, 2 * tokens), bf16),
            pltpu.VMEM((count, heads, 256), f32),
            pltpu.VMEM((count, heads, 256), f32),
        ],
        compiler_params=pltpu.CompilerParams(vmem_limit_bytes=VMEM_LIMIT),
        cost_estimate=pl.CostEstimate(
            flops=2560 * heads * tokens * keys,
            bytes_accessed=12 * 2**20,
            transcendentals=heads * 2 * tokens * keys,
        ),
        name="attend_far_back" if far is not None else "attend_near_back",
    )(*inputs)


def flip(index):
    return index + 1 - 2 * (index % 2)


def partners():
    img, r, z = lax.axis_index("img"), lax.axis_index("row"), lax.axis_index("col")
    return (img, flip(r), z), (img, (r + 2) % 4, z), (flip(img), r, z)


def greet(devices):
    barrier = pltpu.get_barrier_semaphore()
    for device in devices:
        pl.semaphore_signal(
            barrier, inc=1, device_id=device, device_id_type=pl.DeviceIdType.MESH
        )
    pl.semaphore_wait(barrier, len(devices))


def send(src, dst, send_sem, recv_sem, device):
    return pltpu.make_async_remote_copy(
        src_ref=src,
        dst_ref=dst,
        send_sem=send_sem,
        recv_sem=recv_sem,
        device_id=device,
        device_id_type=pl.DeviceIdType.MESH,
    )


def middle_kernel(
    blk,
    chunks,
    x_ref,
    cot_ref,
    am_ref,
    ao_ref,
    mod_ref,
    wpm_ref,
    wpo_ref,
    bp_ref,
    bd_ref,
    wu_ref,
    bu_ref,
    wd_ref,
    out_ref,
    gmid_ref,
    dom_ref,
    doo_ref,
    sum_ref,
    dbu_ref,
    dwpm_ref,
    dwpo_ref,
    dmod_ref,
    dbp_ref,
    dbd_ref,
    mid_s,
    br1_s,
    n_s,
    nt_s,
    db2_s,
    db2t_s,
    br2_s,
    gn_s,
    db1_s,
    mine_s,
    other_s,
    in1_s,
    out2_s,
    keep2_s,
    in2_s,
    out3_s,
    keep3_s,
    in3_s,
    send1,
    recv1,
    send2,
    recv2,
    send3,
    recv3,
    done,
):
    step = pl.program_id(0)
    tokens, width = x_ref.shape
    blocks = tokens // blk
    part = width // 4
    row = lax.axis_index("row")
    x, core, y = row // 2, row % 2, lax.axis_index("img") % 2
    to_core, to_x, to_img = partners()

    @pl.when(step == 0)
    def _():
        greet((to_core, to_x, to_img))
        br1_s[...] = (
            dot(am_ref[...], wpm_ref[...], NN) + dot(ao_ref[...], wpo_ref[...], NN) + bp_ref[...]
        ).astype(bf16)
        for i in range(blocks):
            rows = slice(i * blk, (i + 1) * blk)
            mid = x_ref[rows].astype(f32) + mod_ref[i, 2:3] * br1_s[rows].astype(f32)
            mid_s[rows] = mid
            normed, _ = norm(mid)
            n_s[rows] = (normed * (1.0 + mod_ref[i, 4:5]) + mod_ref[i, 3:4]).astype(bf16)
            db2_s[rows] = (mod_ref[i, 5:6] * cot_ref[rows].astype(f32)).astype(bf16)
        for g in range(4):
            place_row = ((g + core) % 2) * (2 * part) + (g // 2) * part
            place_row = pl.ds(pl.multiple_of(place_row, 16), part)
            cols = slice(g * part, (g + 1) * part)
            nt_s[place_row] = n_s[:, cols].astype(f32).T.astype(bf16)
            db2t_s[place_row] = db2_s[:, cols].astype(f32).T.astype(bf16)
        br2_s[...] = jnp.zeros_like(br2_s)
        gn_s[...] = jnp.zeros_like(gn_s)

    @pl.when(step < chunks)
    def _():
        slot = step % 2
        pre = dot(n_s[...], wu_ref[...], NN) + bu_ref[...]
        square = pre * pre
        t = jnp.tanh(pre * (GELU_A + (GELU_A * GELU_B) * square))
        hidden = (0.5 * pre * (1.0 + t)).astype(bf16)
        slope = 0.5 * (1.0 + t) + 0.5 * pre * (1.0 - t * t) * (
            GELU_A + (3.0 * GELU_A * GELU_B) * square
        )
        br2_s[...] += dot(hidden, wd_ref[...], NN)
        gpre = dot(db2_s[...], wd_ref[...], NT) * slope
        gp = gpre.astype(bf16)
        gn_s[...] += dot(gp, wu_ref[...], NT)
        dbu_ref[...] = jnp.sum(gpre, axis=0, keepdims=True)
        for k, (left, right) in enumerate(((nt_s, gp), (db2t_s, hidden))):
            for half, dst in enumerate((mine_s, other_s)):
                term = dot(left[2 * part * half : 2 * part * (half + 1)], right, NN)
                dst[slot, k] = term.reshape(dst.shape[2:]).astype(bf16)

    def copy1(a):
        return send(other_s.at[a % 2], in1_s.at[a % 2], send1.at[a % 2], recv1.at[a % 2], to_core)

    def turn(a, even, odd):
        return tuple(e + (o - e) * (a % 2) for e, o in zip(even, odd))

    def copy2(a):
        return send(
            out2_s.at[a % 2], in2_s.at[a % 4], send2.at[a % 4], recv2.at[a % 4], turn(a, to_x, to_img)
        )

    def copy3(a):
        return send(
            out3_s.at[a % 2], in3_s.at[a % 4], send3.at[a % 4], recv3.at[a % 4], turn(a, to_img, to_x)
        )

    @pl.when(step >= 5)
    def _():
        a = step - 5
        copy3(a).wait()
        sum_ref[...] = plus(keep3_s[a % 2], in3_s[a % 4])

    @pl.when(jnp.logical_and(step >= 3, step < chunks + 3))
    def _():
        a = step - 3
        copy2(a).wait()
        side = y + (x - y) * (a % 2)
        out3_s[a % 2] = plus(keep2_s[a % 2, 1 - side], in2_s[a % 4, 1 - side])
        keep3_s[a % 2] = plus(keep2_s[a % 2, side], in2_s[a % 4, side])
        copy3(a).start()

    @pl.when(jnp.logical_and(step >= 1, step < chunks + 1))
    def _():
        a = step - 1
        s = a % 2
        copy1(a).wait()

        @pl.when(s == 0)
        def _():
            for k in range(2):
                out2_s[s, k] = plus(mine_s[s, k, 1 - x], in1_s[s, k, 1 - x])
                keep2_s[s, k] = plus(mine_s[s, k, x], in1_s[s, k, x])

        @pl.when(s == 1)
        def _():
            for k in range(2):
                out2_s[s, k] = plus(mine_s[s, 1 - y, k], in1_s[s, 1 - y, k])
                keep2_s[s, k] = plus(mine_s[s, y, k], in1_s[s, y, k])

        copy2(a).start()

    @pl.when(step < chunks)
    def _():
        copy1(step).start()

    @pl.when(step == chunks)
    def _():
        dbp = jnp.zeros((1, width), f32)
        dbd = jnp.zeros((1, width), f32)
        for i in range(blocks):
            rows = slice(i * blk, (i + 1) * blk)
            cot = cot_ref[rows].astype(f32)
            br2 = br2_s[rows] + bd_ref[...]
            mid = mid_s[rows]
            n_s[rows] = (mid + mod_ref[i, 5:6] * br2).astype(bf16)
            normed, rstd = norm(mid)
            gn = gn_s[rows]
            u = gn * (1.0 + mod_ref[i, 4:5])
            gmid = cot + rstd * (
                u
                - jnp.mean(u, axis=-1, keepdims=True)
                - normed * jnp.mean(u * normed, axis=-1, keepdims=True)
            )
            db1 = mod_ref[i, 2:3] * gmid
            db1_s[rows] = db1.astype(bf16)
            dbp += jnp.sum(db1, axis=0, keepdims=True)
            dbd += jnp.sum(db2_s[rows].astype(f32), axis=0, keepdims=True)
            db2_s[rows] = gmid.astype(bf16)
            dmod_ref[i, 0:1] = jnp.sum(gmid * br1_s[rows].astype(f32), axis=0, keepdims=True)
            dmod_ref[i, 1:2] = jnp.sum(gn, axis=0, keepdims=True)
            dmod_ref[i, 2:3] = jnp.sum(gn * normed, axis=0, keepdims=True)
            dmod_ref[i, 3:4] = jnp.sum(cot * br2, axis=0, keepdims=True)
        dbp_ref[...] = dbp
        dbd_ref[...] = dbd
        first = pltpu.make_async_copy(n_s, out_ref, done.at[0])
        second = pltpu.make_async_copy(db2_s, gmid_ref, done.at[1])
        first.start()
        second.start()
        dom_ref[...] = dot(db1_s[...], wpm_ref[...], NT).astype(bf16)
        doo_ref[...] = dot(db1_s[...], wpo_ref[...], NT).astype(bf16)
        dwpm_ref[...] = dot(am_ref[...], db1_s[...], TN).astype(bf16)
        dwpo_ref[...] = dot(ao_ref[...], db1_s[...], TN).astype(bf16)
        first.wait()
        second.wait()


def middle(x, cot, att_m, att_o, mod, wp_m, wp_o, b_proj, b_down, w_up, b_up, w_down, blk):
    tokens, width = x.shape
    pad = att_m.shape[1]
    hidden = w_up.shape[1]
    chunk = 512
    chunks = hidden // chunk
    n = width // 16
    any_ref = pl.BlockSpec(memory_space=pl.ANY)

    def at(j):
        return jnp.minimum(j, chunks - 1)

    return pl.pallas_call(
        functools.partial(middle_kernel, blk, chunks),
        grid=(chunks + 5,),
        in_specs=[VMEM] * 9
        + [
            pl.BlockSpec((width, chunk), lambda j: (0, at(j))),
            pl.BlockSpec((1, chunk), lambda j: (0, at(j))),
            pl.BlockSpec((chunk, width), lambda j: (at(j), 0)),
        ],
        out_specs=[any_ref, any_ref, VMEM, VMEM]
        + [
            pl.BlockSpec((4, n, chunk), lambda j: (0, 0, jnp.maximum(j - 5, 0))),
            pl.BlockSpec((1, chunk), lambda j: (0, at(j))),
        ]
        + [VMEM] * 5,
        scratch_shapes=[
            pltpu.VMEM((tokens, width), f32),
            pltpu.VMEM((tokens, width), bf16),
            pltpu.VMEM((tokens, width), bf16),
            pltpu.VMEM((width, tokens), bf16),
            pltpu.VMEM((tokens, width), bf16),
            pltpu.VMEM((width, tokens), bf16),
            pltpu.VMEM((tokens, width), f32),
            pltpu.VMEM((tokens, width), f32),
            pltpu.VMEM((tokens, width), bf16),
            pltpu.VMEM((2, 2, 2, 4, n, chunk), bf16),
            pltpu.VMEM((2, 2, 2, 4, n, chunk), bf16),
            pltpu.VMEM((2, 2, 2, 4, n, chunk), bf16),
            pltpu.VMEM((2, 2, 4, n, chunk), bf16),
            pltpu.VMEM((2, 2, 4, n, chunk), bf16),
            pltpu.VMEM((4, 2, 4, n, chunk), bf16),
            pltpu.VMEM((2, 4, n, chunk), bf16),
            pltpu.VMEM((2, 4, n, chunk), bf16),
            pltpu.VMEM((4, 4, n, chunk), bf16),
        ]
        + [pltpu.SemaphoreType.DMA((k,)) for k in (2, 2, 4, 4, 4, 4, 2)],
        out_shape=(
            shaped((tokens, width)),
            shaped((tokens, width)),
            shaped((tokens, pad)),
            shaped((tokens, pad)),
            shaped((4, n, hidden)),
            shaped((1, hidden), f32),
            shaped((pad, width)),
            shaped((pad, width)),
            shaped((tokens // blk, 4, width), f32),
            shaped((1, width), f32),
            shaped((1, width), f32),
        ),
        compiler_params=pltpu.CompilerParams(
            vmem_limit_bytes=62 * 2**20, collective_id=1, has_side_effects=True
        ),
        cost_estimate=pl.CostEstimate(
            flops=2 * tokens * width * (6 * hidden + 6 * pad),
            bytes_accessed=60 * 2**20,
            transcendentals=tokens * hidden,
        ),
        name="middle",
    )(x, cot, att_m, att_o, mod, wp_m, wp_o, b_proj, b_down, w_up, b_up, w_down)


def first_back_kernel(blk, x_ref, ga_ref, gb_ref, gmid_ref, mod_ref, out_ref, dmod_ref):
    for i in range(x_ref.shape[0] // blk):
        rows = slice(i * blk, (i + 1) * blk)
        y, rstd = norm(x_ref[rows].astype(f32))
        gn = ga_ref[rows].astype(f32) + gb_ref[rows].astype(f32)
        u = gn * (1.0 + mod_ref[i, 1:2])
        back = rstd * (
            u - jnp.mean(u, axis=-1, keepdims=True) - y * jnp.mean(u * y, axis=-1, keepdims=True)
        )
        out_ref[rows] = (gmid_ref[rows].astype(f32) + back).astype(bf16)
        dmod_ref[i, 0:1] = jnp.sum(gn, axis=0, keepdims=True)
        dmod_ref[i, 1:2] = jnp.sum(gn * y, axis=0, keepdims=True)


def first_back(x, part_a, part_b, gmid, mod, blk):
    tokens, width = x.shape
    steps = 3
    rows = tokens // steps
    each = pl.BlockSpec((rows, width), lambda s: (s, 0))
    return pl.pallas_call(
        functools.partial(first_back_kernel, blk),
        grid=(steps,),
        in_specs=[each] * 4 + [pl.BlockSpec((rows // blk, 6, width), lambda s: (s, 0, 0))],
        out_specs=[each, pl.BlockSpec((rows // blk, 2, width), lambda s: (s, 0, 0))],
        out_shape=(shaped((tokens, width)), shaped((tokens // blk, 2, width), f32)),
        compiler_params=pltpu.CompilerParams(vmem_limit_bytes=VMEM_LIMIT),
        cost_estimate=pl.CostEstimate(
            flops=20 * tokens * width, bytes_accessed=10 * tokens * width, transcendentals=tokens
        ),
        name="first_back",
    )(x, part_a, part_b, gmid, mod)


def place_kernel(order_ref, in_ref, out_ref):
    out_ref[...] = in_ref[...].astype(out_ref.dtype)


def place(order, tiles, dtype):
    count = tiles.shape[0]
    block = (1,) + tiles.shape[1:]
    return pl.pallas_call(
        place_kernel,
        grid_spec=pltpu.PrefetchScalarGridSpec(
            num_scalar_prefetch=1,
            grid=(count,),
            in_specs=[pl.BlockSpec(block, lambda i, o: (o[i], 0, 0))],
            out_specs=pl.BlockSpec(block, lambda i, o: (i, 0, 0)),
        ),
        out_shape=shaped(tiles.shape, dtype),
        cost_estimate=pl.CostEstimate(
            flops=0, bytes_accessed=6 * math.prod(tiles.shape), transcendentals=0
        ),
        name="place",
    )(order, tiles)


def pick(values, index, axis=0):
    return lax.dynamic_index_in_dim(values, index, axis, keepdims=False)


def over_core(v):
    return lax.ppermute(v, "row", [(r, r ^ 1) for r in range(4)])


def over_x(v):
    return lax.ppermute(v, "row", [(r, r ^ 2) for r in range(4)])


def over_col(v, far):
    return lax.ppermute(v, "col", [(i, i ^ far) for i in range(4)])


def over_plane(v, dx, dz):
    swap = [(i, ((i // 4) ^ (2 * dx)) * 4 + ((i % 4) ^ dz)) for i in range(16)]
    return lax.ppermute(v, ("row", "col"), swap)


def over_img(v):
    if lax.axis_size("img") == 2:
        return v.astype(f32) + lax.ppermute(v, "img", [(0, 1), (1, 0)]).astype(f32)
    return lax.psum(v, "img").astype(f32)


def shards(
    tokens,
    conditioning,
    images_in_slot,
    w_qkv,
    b_qv,
    w_proj,
    b_proj,
    w_up,
    b_up,
    w_down,
    b_down,
    w_ada,
    b_ada,
    cotangent,
):
    slots, rows_tile, cols_tile, width = tokens.shape
    tile = rows_tile * cols_tile
    blk = 2 * tile
    count = slots * tile
    main = 8 * tile
    hd = width // HEADS
    heads = HEADS // 2
    half = width // 2
    pad = -(-half // 128) * 128
    hidden = w_up.shape[1]
    r, z = lax.axis_index("row"), lax.axis_index("col")
    x, core = r // 2, r % 2
    core_arr = core.reshape(1).astype(jnp.int32)
    assert lax.axis_size("row") == 4 and lax.axis_size("col") == 4 and slots == 12

    def spread(values):
        grouped = values.reshape(4, 3, tile, width)
        near, far, shared = [], [], []
        for dz in range(4):
            group = pick(grouped, z ^ dz)
            own = jnp.stack([pick(group, x), group[2]])
            other = pick(group, 1 - x)
            if dz:
                own = over_plane(own, 0, dz)
            near.append(own[0])
            shared.append(own[1])
            far.append(over_plane(other, 1, dz))
        return jnp.concatenate(near + far + shared, axis=0)

    def collect(values, dtype):
        tiles = values.reshape(12, tile, width)
        near, far, shared = [], [], []
        for dz in range(4):
            own = jnp.stack([tiles[dz], tiles[8 + dz]])
            if dz:
                own = over_plane(own, 0, dz)
            near.append(own[0])
            shared.append(own[1])
            far.append(over_plane(tiles[4 + dz], 1, dz))
        stacked = jnp.stack(near + far + shared)
        slot = jnp.arange(12, dtype=jnp.int32)
        kind = slot % 3
        dz = (slot // 3) ^ z
        order = jnp.where(kind == 2, 8 + dz, ((kind ^ x) & 1) * 4 + dz)
        return place(order, stacked, dtype).reshape(tokens.shape)

    inputs = spread(tokens)
    upstream = spread(cotangent)

    four_way = images_in_slot == 4
    kinds = pick(four_way.reshape(4, 3), z)
    main_four, shared_four = pick(kinds, x), kinds[2]
    quarter = jnp.stack([2 * (x ^ dx) + ((z // 2) ^ dz) for dx in range(2) for dz in range(2)])
    picks = jnp.concatenate(
        [jnp.where(main_four, quarter, 0), jnp.where(shared_four, quarter[:2], 0)]
    )
    places = jnp.concatenate([jnp.full((4,), x, jnp.int32), jnp.full((2,), 2, jnp.int32)]) * 4 + picks
    flag_main = jnp.where(main_four, 0, 1).reshape(1).astype(jnp.int32)
    flag_shared = jnp.where(shared_four, 0, 1).reshape(1).astype(jnp.int32)
    cond = conditioning.astype(f32)
    silu = jax.nn.silu(cond).astype(bf16)
    silu_groups = silu.reshape(4, 12, width)
    chosen = jnp.take(pick(silu_groups, z), places, axis=0)
    mod = (jnp.dot(chosen, w_ada, preferred_element_type=f32) + b_ada).reshape(6, 6, width)

    def widen(v, axis):
        return jnp.pad(v, [(0, pad - half) if a == axis else (0, 0) for a in range(v.ndim)])

    w_half = widen(w_qkv.reshape(width, 3, 2, half), 3).transpose(2, 0, 1, 3)
    w_half = w_half.reshape(2, width, 3 * pad)
    b_three = jnp.stack([b_qv[:width], jnp.zeros_like(b_qv[:width]), b_qv[width:]])
    b_half = widen(b_three.reshape(3, 2, half).astype(f32), 2).transpose(1, 0, 2)
    b_half = b_half.reshape(2, 1, 3 * pad)
    w_proj_half = widen(w_proj.reshape(2, half, width), 1)
    wp_mine, wp_other = pick(w_proj_half, core), pick(w_proj_half, 1 - core)

    qkv_other, qkv_mine, normed_t = qkv(core_arr, inputs, mod, w_half, b_half, blk)
    qkv_sib = over_core(qkv_other)
    normed_sib = over_core(normed_t)
    far_kv = over_x(jnp.concatenate([qkv_mine[main:, pad:], qkv_sib[main:, pad:]], axis=0))
    om_near, os_near, stat_near = attend(flag_main, qkv_mine, qkv_sib, None, heads, hd, 4)
    back_near = over_core(os_near)
    om_far, os_far, stat_far = attend(flag_shared, qkv_mine, qkv_sib, far_kv, heads, hd, 2)
    back_far = over_core(os_far)
    att_mine = jnp.concatenate([om_near, om_far], axis=0)
    att_other = jnp.concatenate([back_near, back_far], axis=0)

    (
        out,
        gmid,
        do_mine,
        do_other,
        dw_sum,
        dbu,
        dwp_mine,
        dwp_other,
        dmod_mid,
        dbp,
        dbd,
    ) = middle(
        inputs,
        upstream,
        att_mine,
        att_other,
        mod,
        wp_mine,
        wp_other,
        b_proj.astype(f32).reshape(1, width),
        b_down.astype(f32).reshape(1, width),
        w_up,
        b_up.astype(f32).reshape(1, hidden),
        w_down,
        blk,
    )
    output = collect(out, bf16)
    do_sib = over_core(do_other)

    def reduce_plane(mine):
        got = over_x(pick(mine, 1 - x))
        mine = plus(pick(mine, x), got)
        return over_img(reduce_col(mine))

    def reduce_col(mine):
        split = mine.reshape((2, 2) + mine.shape[1:])
        got = over_col(pick(split, 1 - z % 2, 1), 1)
        mine = plus(pick(split, z % 2, 1), got)
        got = over_col(pick(mine, 1 - z // 2), 2)
        return plus(pick(mine, z // 2), got)

    size = lax.axis_size("img")
    side = lax.axis_index("img") % 2
    dw = reduce_col(dw_sum)
    step = 2
    while step < size:
        dw = plus(dw, lax.ppermute(dw, "img", [(i, i ^ step) for i in range(size)]))
        step *= 2
    dw_there = lax.ppermute(dw, "img", [(i, i ^ 1) for i in range(size)])
    grad_w_up = jnp.where(side == 0, dw, dw_there).astype(f32)
    dwd = jnp.where(side == 0, dw_there, dw).reshape(width // 16, 16, hidden // 16)
    dwd = lax.all_to_all(dwd.transpose(1, 0, 2), ("row", "col"), 0, 0, tiled=True)
    grad_w_down = dwd.reshape(width, hidden // 16).T.astype(f32)
    dwp = jnp.stack([dwp_mine, dwp_other])
    dwp = jnp.stack([pick(dwp, core), pick(dwp, 1 - core)])[:, :half]
    dwp = dwp.reshape(2, 2, half // 2, width)
    dwp_sum = plus(pick(dwp, core, 1), over_core(pick(dwp, 1 - core, 1)))
    grad_w_proj = reduce_plane(dwp_sum.reshape(2, 4, width // 16, width))

    gm_far, gs_far, g_far = attend_back(
        flag_shared,
        qkv_mine,
        qkv_sib,
        do_mine[main:],
        do_sib[main:],
        om_far,
        os_far,
        stat_far,
        far_kv,
        heads,
        hd,
        2,
    )
    far_back = over_x(g_far)
    gm_near, gs_near = attend_back(
        flag_main, qkv_mine, qkv_sib, do_mine, do_sib, om_near, os_near, stat_near, None, heads, hd, 4
    )
    gm_far = jnp.concatenate([gm_far[:, :pad], plus(gm_far[:, pad:], far_back[: count - main])], 1)
    gs_far = jnp.concatenate([gs_far[:, :pad], plus(gs_far[:, pad:], far_back[count - main :])], 1)
    g_mine = jnp.concatenate([gm_near, gm_far], axis=0)
    g_sib = jnp.concatenate([gs_near, gs_far], axis=0)
    w_half_mine = pick(w_half, core)
    gn_other = over_core(dot(g_sib, w_half_mine, NT).astype(bf16))
    gn_mine = dot(g_mine, w_half_mine, NT).astype(bf16)
    dwq = (dot(normed_t, g_mine, NN) + dot(normed_sib, g_sib, NN)).astype(bf16)
    dwq = reduce_plane(
        dwq.reshape(2, 2, 4, width // 16, 3 * pad).transpose(0, 2, 1, 3, 4)
    )
    swap = over_core(pick(dwq, 1 - core).astype(bf16))
    parts = jnp.stack([pick(dwq, core), swap.astype(f32)])
    parts = jnp.stack([pick(parts, core), pick(parts, 1 - core)])
    parts = parts.reshape(2, width // 16, 3, pad)[..., :half]
    grad_w_qkv = parts.transpose(1, 2, 0, 3).reshape(width // 16, 3 * width)

    grad_x, dmod_first = first_back(inputs, gn_mine, gn_other, gmid, mod, blk)
    grad_tokens = collect(grad_x, f32)

    one_hot = (jnp.arange(12, dtype=jnp.int32)[:, None] == places[None, :]).astype(f32)
    silu_rel = jnp.concatenate([pick(silu_groups, z ^ dz) for dz in range(4)], axis=0)
    rank = r * 4 + z
    silu_rows = lax.dynamic_slice_in_dim(silu_rel, rank * (width // 16), width // 16, 1)

    def modulation_grads(dmod, columns):
        values = jnp.sum(one_hot[:, :, None] * dmod.reshape(1, 6, -1), axis=1).astype(bf16)
        values = plus(values, over_core(values))
        values = plus(values, over_x(values))
        every = jnp.concatenate(
            [values] + [over_col(values, dz) for dz in range(1, 4)], axis=0
        )
        d_w = over_img(dot(silu_rows, every, TN).astype(bf16))
        d_b = jnp.sum(every.astype(f32), axis=0)
        d_s = dot(every, w_ada[:, columns], NT)
        return d_w, d_b, d_s

    late = modulation_grads(dmod_first, slice(0, 2 * width))
    early = modulation_grads(dmod_mid, slice(2 * width, 6 * width))
    grad_w_ada = jnp.concatenate([late[0], early[0]], axis=1)
    d_s = (late[2] + early[2]).reshape(4, 12, width)
    d_s = jnp.stack([pick(d_s, z ^ g) for g in range(4)]).reshape(slots, 4, width)
    sig = jax.nn.sigmoid(cond)
    grad_conditioning = d_s * (sig * (1.0 + cond * (1.0 - sig)))

    db_three = jnp.sum(g_mine.astype(f32), axis=0) + jnp.sum(g_sib.astype(f32), axis=0)
    db_three = db_three.reshape(3, pad)[:, :half]
    db_three = jnp.where(
        (jnp.arange(2) == core)[None, :, None], db_three[:, None, :], 0.0
    ).reshape(3, width)
    small = jnp.concatenate([db_three[0], db_three[2], dbp[0], dbu[0], dbd[0]])
    small = lax.psum(small, ("row", "col", "img"))
    d_ada = jnp.concatenate([late[1], early[1]])
    d_ada = lax.dynamic_slice_in_dim(d_ada, rank * (6 * width // 16), 6 * width // 16, 0)
    grad_b_ada = over_img(d_ada)

    def own(start, size):
        return lax.dynamic_slice_in_dim(small, start + rank * (size // 16), size // 16, 0)

    return (
        output,
        grad_tokens,
        grad_conditioning,
        grad_w_qkv,
        own(0, 2 * width),
        grad_w_proj,
        own(2 * width, width),
        grad_w_up,
        own(3 * width, hidden),
        grad_w_down,
        own(3 * width + hidden, width),
        grad_w_ada,
        grad_b_ada,
    )


def solution(mesh):
    grid = P("img", "row", "col", None)
    plane = ("row", "col")
    return jax.shard_map(
        shards,
        mesh=mesh,
        in_specs=(grid, P("img", None, None), P("img")) + (P(),) * 10 + (grid,),
        out_specs=(grid, grid, P("img", None, None))
        + (P(plane, None), P(plane)) * 5,
        check_vma=False,
    )
```

```python
import functools
import math

import jax
import jax.numpy as jnp
from jax import lax
from jax.experimental import pallas as pl
from jax.experimental.pallas import tpu as pltpu
from jax.sharding import PartitionSpec as P

HEADS = 16
EPS = 1e-06
LOG2E = math.log2(math.e)
GELU_A = math.sqrt(2.0 / math.pi)
GELU_B = 0.044715
VMEM_LIMIT = 60 * 2**20

f32 = jnp.float32
bf16 = jnp.bfloat16
NT = (((1,), (1,)), ((), ()))
NN = (((1,), (0,)), ((), ()))
TN = (((0,), (0,)), ((), ()))

VMEM = pl.BlockSpec(memory_space=pltpu.VMEM)
SMEM = pl.BlockSpec(memory_space=pltpu.SMEM)


def dot(left, right, dims):
    return lax.dot_general(left, right, dims, preferred_element_type=f32)


def shaped(shape, dtype=bf16):
    return jax.ShapeDtypeStruct(shape, dtype)


def norm(values):
    center = values - jnp.mean(values, axis=-1, keepdims=True)
    rstd = lax.rsqrt(jnp.mean(center * center, axis=-1, keepdims=True) + EPS)
    return center * rstd, rstd


def plus(a, b):
    return (a.astype(f32) + b.astype(f32)).astype(bf16)


def flip(index):
    return index + 1 - 2 * (index % 2)


def partners():
    img, r, z = lax.axis_index("img"), lax.axis_index("row"), lax.axis_index("col")
    return (img, flip(r), z), (img, (r + 2) % 4, z), (flip(img), r, z)


def plane_device(dx, dz):
    img, r, z = lax.axis_index("img"), lax.axis_index("row"), lax.axis_index("col")
    return img, (r + 2 * dx) % 4, hop(z, dz)


def hop(z, dz):
    return (z, flip(z), (z + 2) % 4, 3 - z)[dz]


def greet(devices):
    barrier = pltpu.get_barrier_semaphore()
    for device in devices:
        pl.semaphore_signal(
            barrier, inc=1, device_id=device, device_id_type=pl.DeviceIdType.MESH
        )
    pl.semaphore_wait(barrier, len(devices))


def send(src, dst, send_sem, recv_sem, device):
    return pltpu.make_async_remote_copy(
        src_ref=src,
        dst_ref=dst,
        send_sem=send_sem,
        recv_sem=recv_sem,
        device_id=device,
        device_id_type=pl.DeviceIdType.MESH,
    )


def tile_moves(src, dst, send_sem, recv_sem, local_sem):
    r, z = lax.axis_index("row"), lax.axis_index("col")
    x = r // 2
    shared, near, far, local = [], [], [], []
    for dz in range(4):
        first = 3 * hop(z, dz)
        moves = (
            (shared, 0, first + 2, 8 + dz),
            (near, 0, first + x, dz),
            (far, 1, first + 1 - x, 4 + dz),
        )
        for group, dx, slot, place_at in moves:
            if dx == 0 and dz == 0:
                sem = local_sem.at[0 if place_at else 1]
                local.append(pltpu.make_async_copy(src.at[slot], dst.at[place_at], sem))
            else:
                sems = send_sem.at[place_at], recv_sem.at[place_at]
                group.append(
                    send(src.at[slot], dst.at[place_at], *sems, plane_device(dx, dz))
                )
    return local, shared, near, far


def head_window(head, hd):
    first = head * hd
    start = pl.multiple_of((first // 128) * 128, 128)
    lane = lax.broadcasted_iota(jnp.int32, (1, 256), 1) + start
    inside = jnp.logical_and(lane >= first, lane < first + hd)
    return pl.ds(start, 256), inside


def gather_rows(dst, col, sources, base, count):
    pad = dst.shape[1]
    for i in range(count):
        for j, src in enumerate(sources):
            row = 256 * i + 128 * j
            dst[row : row + 128] = src[base + 128 * i : base + 128 * i + 128, col : col + pad]


def attend(heads, hd, count, base, bias, mine, sib, far, o_mine, o_sib, stat, q_s, k_s, v_s, o_s):
    pad = q_s.shape[1]
    scale = LOG2E / math.sqrt(hd)
    gather_rows(q_s, 0, (mine, sib), base, count)
    gather_rows(k_s, pad, (mine, sib), base, count)
    gather_rows(v_s, 2 * pad, (mine, sib), base, count)
    if far is not None:
        k_s[256 * count :] = far[:, 0:pad]
        v_s[256 * count :] = far[:, pad : 2 * pad]
    blocks = k_s.shape[0] // 256
    lane = lax.broadcasted_iota(jnp.int32, (1, 128), 1)

    def body(head, carry):
        win, inside = head_window(head, hd)
        for i in range(count):
            rows = slice(256 * i, 256 * i + 256)
            q = jnp.where(inside, q_s[rows, win], jnp.zeros((), bf16))
            s = dot(q, k_s[:, win], NT)
            cols = [s[:, 256 * j : 256 * j + 256] for j in range(blocks)]
            best = [jnp.max(col, axis=1, keepdims=True) for col in cols]
            own = best[i]
            rest = best[:i] + best[i + 1 :]
            top = jnp.maximum(own, functools.reduce(jnp.maximum, rest) + bias)
            near = -scale * top
            away = near + bias
            cols = [
                jnp.exp2(col * scale + (near if j == i else away)) for j, col in enumerate(cols)
            ]
            total = functools.reduce(
                jnp.add, [jnp.sum(col, axis=1, keepdims=True) for col in cols]
            )
            p = jnp.concatenate([col.astype(bf16) for col in cols], axis=1)
            o = dot(p, v_s[:, win], NN) / total
            o_s[rows, win] = jnp.where(inside, o.astype(bf16), o_s[rows, win])
            at = slice(2 * base + 256 * i, 2 * base + 256 * i + 256)
            stat[at] = jnp.where(lane == head, top * scale + jnp.log2(total), stat[at])
        return carry

    lax.fori_loop(0, heads, body, 0)
    for i in range(count):
        at = slice(base + 128 * i, base + 128 * i + 128)
        o_mine[at] = o_s[256 * i : 256 * i + 128]
        o_sib[at] = o_s[256 * i + 128 : 256 * i + 256]


def forward_kernel(
    heads,
    hd,
    tok_ref,
    cot_ref,
    wq_ref,
    wa_ref,
    chosen_ref,
    bh_ref,
    ba_ref,
    bias_ref,
    x_out,
    cot_out,
    mine_out,
    sib_out,
    nt_out,
    ntsib_out,
    far_out,
    om_out,
    os_out,
    ao_out,
    stat_out,
    mod_out,
    wh_out,
    x_s,
    raw_s,
    w_s,
    wa_s,
    mod_s,
    nt_s,
    ntsib_s,
    other_s,
    mine_s,
    sib_s,
    far_s,
    q_s,
    k_s,
    v_s,
    o_s,
    om_s,
    os_s,
    ao_s,
    stat_s,
    tok_send,
    tok_recv,
    cot_send,
    cot_recv,
    local_sem,
    raw_sem,
    wa_sem,
    side_send,
    side_recv,
    out_sem,
):
    tile, width = x_s.shape[1:]
    tokens = 12 * tile
    main = 8 * tile
    half = width // 2
    pad = w_s.shape[2] // 3
    rows_step = raw_s.shape[1]
    core = lax.axis_index("row") % 2
    to_core, to_x, _ = partners()

    raw = [
        pltpu.make_async_copy(
            wq_ref.at[pl.ds(i * rows_step, rows_step)], raw_s.at[i % 2], raw_sem.at[i % 2]
        )
        for i in range(width // rows_step)
    ]
    ada = [
        pltpu.make_async_copy(
            wa_ref.at[:, pl.ds(i * width, width)], wa_s.at[i % 2], wa_sem.at[i % 2]
        )
        for i in range(6)
    ]
    for copy in raw[:2] + ada[:2]:
        copy.start()
    greet([to_core] + [plane_device(dx, dz) for dx in range(2) for dz in range(4) if dx or dz])
    local, shared, near, far = tile_moves(tok_ref, x_s, tok_send, tok_recv, local_sem)
    for copy in local + shared + near + far:
        copy.start()

    w_s[...] = jnp.zeros_like(w_s)
    for i, copy in enumerate(raw):
        copy.wait()
        rows = slice(i * rows_step, (i + 1) * rows_step)
        for h in range(2):
            for p in range(3):
                start = half * (2 * p + h)
                w_s[h, rows, p * pad : p * pad + half] = raw_s[i % 2, :, start : start + half]
        if i + 2 < len(raw):
            raw[i + 2].start()
    for i, copy in enumerate(ada):
        copy.wait()
        mod_s[i] = dot(chosen_ref[...], wa_s[i % 2], NN) + ba_ref[i]
        if i + 2 < len(ada):
            ada[i + 2].start()
    outs = []

    def put(src, dst):
        copy = pltpu.make_async_copy(src, dst, out_sem.at[len(outs)])
        copy.start()
        outs.append(copy)

    put(w_s, wh_out)
    put(mod_s, mod_out)

    sides = []

    def side(src, dst, device):
        k = len(sides)
        copy = send(src, dst, side_send.at[k], side_recv.at[k], device)
        copy.start()
        sides.append(copy)
        return copy

    moves = None
    from_core = []
    for first, waits in ((8, local[:1] + shared), (0, local[1:] + near), (4, far)):
        for copy in waits:
            copy.wait()
        if first == 4:
            moves = tile_moves(cot_ref, cot_out, cot_send, cot_recv, local_sem)
            for group in moves:
                for copy in group:
                    copy.start()
        parts = []
        for i in range(2):
            at = first // 2 + i
            values = x_s[first + 2 * i : first + 2 * i + 2].reshape(2 * tile, width)
            normed, _ = norm(values.astype(f32))
            parts.append((normed * (1.0 + mod_s[1, at : at + 1]) + mod_s[0, at : at + 1]).astype(bf16))
        normed = jnp.concatenate(parts, axis=0)
        rows = slice(first * tile, (first + 4) * tile)
        other_s[rows] = (dot(normed, w_s[1 - core], NN) + bh_ref[1 - core]).astype(bf16)
        at = pl.ds(first * tile, 4 * tile)
        from_core.append(side(other_s.at[at], sib_s.at[at], to_core))
        mine_s[rows] = (dot(normed, w_s[core], NN) + bh_ref[core]).astype(bf16)
        nt_s[:, rows] = normed.T
        if first == 0:
            from_core[0].wait_recv()
            at, cols = pl.ds(main, tokens - main), pl.ds(pad, 2 * pad)
            size = tokens - main
            from_x = [
                side(src.at[at, cols], far_s.at[pl.ds(size * k, size)], to_x)
                for k, src in enumerate((mine_s, sib_s))
            ]
    put(x_s, x_out)
    put(mine_s, mine_out)
    put(nt_s, nt_out)
    nt_copy = side(nt_s, ntsib_s, to_core)

    o_s[...] = jnp.zeros_like(o_s)
    stat_s[...] = jnp.zeros_like(stat_s)
    for copy in from_core[1:]:
        copy.wait_recv()
    put(sib_s, sib_out)
    scratch = (om_s, os_s, stat_s, q_s, k_s, v_s, o_s)
    attend(heads, hd, 4, 0, bias_ref[0], mine_s, sib_s, None, *scratch)
    back = [side(os_s.at[pl.ds(0, main)], ao_s.at[pl.ds(0, main)], to_core)]
    for copy in from_x:
        copy.wait_recv()
    put(far_s, far_out)
    attend(heads, hd, 2, main, bias_ref[1], mine_s, sib_s, far_s, *scratch)
    at = pl.ds(main, tokens - main)
    back.append(side(os_s.at[at], ao_s.at[at], to_core))
    put(om_s, om_out)
    put(os_s, os_out)
    put(stat_s, stat_out)
    nt_copy.wait_recv()
    put(ntsib_s, ntsib_out)
    for copy in back:
        copy.wait_recv()
    put(ao_s, ao_out)
    for copy in sides:
        copy.wait_send()
    for group in moves:
        for copy in group:
            copy.wait()
    for copy in outs:
        copy.wait()


def forward(tok, cot, w_qkv, w_ada, chosen, b_half, b_ada, bias, heads, hd):
    _, tile, width = tok.shape
    tokens = 12 * tile
    pad = b_half.shape[2] // 3
    any_ref = pl.BlockSpec(memory_space=pl.ANY)
    outs = (
        shaped((12, tile, width)),
        shaped((12, tile, width)),
        shaped((tokens, 3 * pad)),
        shaped((tokens, 3 * pad)),
        shaped((width, tokens)),
        shaped((width, tokens)),
        shaped((8 * tile, 2 * pad)),
        shaped((tokens, pad)),
        shaped((tokens, pad)),
        shaped((tokens, pad)),
        shaped((2 * tokens, 128), f32),
        shaped((6, 8, width), f32),
        shaped((2, width, 3 * pad)),
    )
    scratch = [
        outs[0],
        shaped((2, width // 4, 3 * width)),
        outs[12],
        shaped((2, width, width)),
        outs[11],
        outs[4],
        outs[4],
        outs[2],
        outs[2],
        outs[2],
        outs[6],
        shaped((16 * tile, pad)),
        shaped((16 * tile, pad)),
        shaped((16 * tile, pad)),
        shaped((16 * tile, pad)),
        outs[7],
        outs[7],
        outs[7],
        outs[10],
    ]
    return pl.pallas_call(
        functools.partial(forward_kernel, heads, hd),
        in_specs=[any_ref] * 4 + [VMEM] * 3 + [SMEM],
        out_specs=(any_ref,) * len(outs),
        scratch_shapes=[pltpu.VMEM(s.shape, s.dtype) for s in scratch]
        + [pltpu.SemaphoreType.DMA((k,)) for k in (12, 12, 12, 12, 2, 2, 2, 10, 10, 12)],
        out_shape=outs,
        compiler_params=pltpu.CompilerParams(
            vmem_limit_bytes=62 * 2**20, collective_id=2, has_side_effects=True
        ),
        cost_estimate=pl.CostEstimate(
            flops=4 * tokens * width * 3 * pad + 4096 * heads * tokens * 16 * tile,
            bytes_accessed=70 * 2**20,
            transcendentals=heads * 2 * tokens * 16 * tile,
        ),
        name="forward",
    )(tok, cot, w_qkv, w_ada, chosen, b_half, b_ada, bias)


def attend_back_kernel(heads, hd, count, shared, flag_ref, mine_ref, sib_ref, *rest):
    d_mine, d_sib, o_mine, o_sib, stat, *rest = rest
    if shared:
        far_ref, g_mine, g_sib, g_far, *rest = rest
    else:
        g_mine, g_sib, *rest = rest
    q_s, k_s, v_s, do_s, kt_s, dqt_s, dk_s, dv_s, p_s, ds_s, lse_s, dd_s = rest
    pad = q_s.shape[1]
    inv = 1.0 / math.sqrt(hd)
    scale = LOG2E * inv
    base = mine_ref.shape[0] - 128 * count if shared else 0
    pair = (mine_ref, sib_ref)
    gather_rows(q_s, 0, pair, base, count)
    gather_rows(k_s, pad, pair, base, count)
    gather_rows(v_s, 2 * pad, pair, base, count)
    gather_rows(do_s, 0, (d_mine, d_sib), base, count)
    if shared:
        k_s[256 * count :] = far_ref[:, 0:pad]
        v_s[256 * count :] = far_ref[:, pad : 2 * pad]
    kt_s[...] = k_s[...].astype(f32).T
    dqt_s[...] = jnp.zeros_like(dqt_s)
    dk_s[...] = jnp.zeros_like(dk_s)
    dv_s[...] = jnp.zeros_like(dv_s)
    row = lax.broadcasted_iota(jnp.int32, (heads, pad), 0)
    col = lax.broadcasted_iota(jnp.int32, (heads, pad), 1)
    member = jnp.where(jnp.logical_and(col >= row * hd, col < row * hd + hd), 1.0, 0.0).astype(bf16)
    for i in range(count):
        rows = slice(256 * i, 256 * i + 256)
        lse_s[i] = stat[2 * base + 256 * i : 2 * base + 256 * i + 256].T[0:heads]
        o = jnp.concatenate(
            [ref[base + 128 * i : base + 128 * i + 128] for ref in (o_mine, o_sib)], axis=0
        )
        both = do_s[rows].astype(f32) * o.astype(f32)
        high = both.astype(bf16)
        low = (both - high.astype(f32)).astype(bf16)
        dd_s[i] = dot(member, high, NT) + dot(member, low, NT)

    def run(single):
        def body(head, carry):
            win, inside = head_window(head, hd)
            mine = pl.ds(pl.multiple_of(head * hd, 8), hd)
            zero = jnp.zeros((), bf16)
            for i in range(count):
                rows = slice(256 * i, 256 * i + 256)
                keys = slice(None) if single else rows
                q = jnp.where(inside, q_s[rows, win], zero)
                do = jnp.where(inside, do_s[rows, win], zero)
                lse = lse_s[i, pl.ds(head, 1)]
                dd = dd_s[i, pl.ds(head, 1)]
                s = dot(k_s[keys, win], q, NT)
                p = jnp.exp2(s * scale - lse)
                dp = dot(v_s[keys, win], do, NT)
                ds = (p * (dp - dd)).astype(bf16)
                p = p.astype(bf16)
                if single:
                    p_s[:, rows] = p
                    ds_s[:, rows] = ds
                else:
                    dv_s[rows, win] += dot(p, do, NN)
                    dk_s[rows, win] += dot(ds, q, NN)
                    dqt_s[mine, rows] = dot(kt_s[mine, rows].astype(bf16), ds, NN)
            if single:
                q = jnp.where(inside, q_s[:, win], zero)
                do = jnp.where(inside, do_s[:, win], zero)
                dv_s[:, win] += dot(p_s[...], do, NN)
                dk_s[:, win] += dot(ds_s[...], q, NN)
                dqt_s[mine, :] = dot(kt_s[mine, :].astype(bf16), ds_s[...], NN)
            return carry

        lax.fori_loop(0, heads, body, 0)

    one = flag_ref[0] == 1
    pl.when(one)(lambda: run(True))
    pl.when(jnp.logical_not(one))(lambda: run(False))
    for i in range(count):
        for j, dst in enumerate((g_mine, g_sib)):
            rows = slice(256 * i + 128 * j, 256 * i + 128 * j + 128)
            out = slice(128 * i, 128 * i + 128)
            dst[out, 0:pad] = (dqt_s[:, rows] * inv).T.astype(bf16)
            dst[out, pad : 2 * pad] = (dk_s[rows] * inv).astype(bf16)
            dst[out, 2 * pad : 3 * pad] = dv_s[rows].astype(bf16)
    if shared:
        g_far[:, 0:pad] = (dk_s[256 * count :] * inv).astype(bf16)
        g_far[:, pad : 2 * pad] = dv_s[256 * count :].astype(bf16)


def attend_back(flag, mine, sib, d_mine, d_sib, o_mine, o_sib, stat, far, heads, hd, count):
    pad = mine.shape[1] // 3
    tokens = 128 * count
    keys = 2 * tokens + (0 if far is None else far.shape[0])
    inputs = [flag, mine, sib, d_mine, d_sib, o_mine, o_sib, stat] + ([] if far is None else [far])
    outs = [shaped((tokens, 3 * pad)), shaped((tokens, 3 * pad))]
    if far is not None:
        outs.append(shaped((far.shape[0], 2 * pad)))
    return pl.pallas_call(
        functools.partial(attend_back_kernel, heads, hd, count, far is not None),
        out_shape=tuple(outs),
        in_specs=[SMEM] + [VMEM] * (len(inputs) - 1),
        out_specs=(VMEM,) * len(outs),
        scratch_shapes=[
            pltpu.VMEM((2 * tokens, pad), bf16),
            pltpu.VMEM((keys, pad), bf16),
            pltpu.VMEM((keys, pad), bf16),
            pltpu.VMEM((2 * tokens, pad), bf16),
            pltpu.VMEM((pad, keys), f32),
            pltpu.VMEM((pad, 2 * tokens), f32),
            pltpu.VMEM((keys, pad), f32),
            pltpu.VMEM((keys, pad), f32),
            pltpu.VMEM((keys, 2 * tokens), bf16),
            pltpu.VMEM((keys, 2 * tokens), bf16),
            pltpu.VMEM((count, heads, 256), f32),
            pltpu.VMEM((count, heads, 256), f32),
        ],
        compiler_params=pltpu.CompilerParams(vmem_limit_bytes=VMEM_LIMIT),
        cost_estimate=pl.CostEstimate(
            flops=2560 * heads * tokens * keys,
            bytes_accessed=12 * 2**20,
            transcendentals=heads * 2 * tokens * keys,
        ),
        name="attend_far_back" if far is not None else "attend_near_back",
    )(*inputs)


def middle_kernel(
    blk,
    chunks,
    x_ref,
    cot_ref,
    am_ref,
    ao_ref,
    mod_ref,
    wpm_ref,
    wpo_ref,
    bp_ref,
    bd_ref,
    wu_ref,
    bu_ref,
    wd_ref,
    out_ref,
    gmid_ref,
    dom_ref,
    doo_ref,
    sum_ref,
    dbu_ref,
    dwpm_ref,
    dwpo_ref,
    dmod_ref,
    dbp_ref,
    dbd_ref,
    mid_s,
    br1_s,
    n_s,
    nt_s,
    db2_s,
    db2t_s,
    br2_s,
    gn_s,
    db1_s,
    mine_s,
    other_s,
    in1_s,
    out2_s,
    keep2_s,
    in2_s,
    out3_s,
    keep3_s,
    in3_s,
    send1,
    recv1,
    send2,
    recv2,
    send3,
    recv3,
    done,
):
    step = pl.program_id(0)
    tokens, width = x_ref.shape
    blocks = tokens // blk
    part = width // 4
    row = lax.axis_index("row")
    x, core, y = row // 2, row % 2, lax.axis_index("img") % 2
    to_core, to_x, to_img = partners()

    @pl.when(step == 0)
    def _():
        greet((to_core, to_x, to_img))
        br1_s[...] = (
            dot(am_ref[...], wpm_ref[...], NN) + dot(ao_ref[...], wpo_ref[...], NN) + bp_ref[...]
        ).astype(bf16)
        for i in range(blocks):
            rows = slice(i * blk, (i + 1) * blk)
            mid = x_ref[rows].astype(f32) + mod_ref[2, i : i + 1] * br1_s[rows].astype(f32)
            mid_s[rows] = mid
            normed, _ = norm(mid)
            n_s[rows] = (normed * (1.0 + mod_ref[4, i : i + 1]) + mod_ref[3, i : i + 1]).astype(bf16)
            db2_s[rows] = (mod_ref[5, i : i + 1] * cot_ref[rows].astype(f32)).astype(bf16)
        for g in range(4):
            place_row = ((g + core) % 2) * (2 * part) + (g // 2) * part
            place_row = pl.ds(pl.multiple_of(place_row, 16), part)
            cols = slice(g * part, (g + 1) * part)
            nt_s[place_row] = n_s[:, cols].astype(f32).T.astype(bf16)
            db2t_s[place_row] = db2_s[:, cols].astype(f32).T.astype(bf16)
        br2_s[...] = jnp.zeros_like(br2_s)
        gn_s[...] = jnp.zeros_like(gn_s)

    @pl.when(step < chunks)
    def _():
        slot = step % 2
        pre = dot(n_s[...], wu_ref[...], NN) + bu_ref[...]
        square = pre * pre
        t = jnp.tanh(pre * (GELU_A + (GELU_A * GELU_B) * square))
        hidden = (0.5 * pre * (1.0 + t)).astype(bf16)
        slope = 0.5 * (1.0 + t) + 0.5 * pre * (1.0 - t * t) * (
            GELU_A + (3.0 * GELU_A * GELU_B) * square
        )
        br2_s[...] += dot(hidden, wd_ref[...], NN)
        gpre = dot(db2_s[...], wd_ref[...], NT) * slope
        gp = gpre.astype(bf16)
        gn_s[...] += dot(gp, wu_ref[...], NT)
        dbu_ref[...] = jnp.sum(gpre, axis=0, keepdims=True)
        for k, (left, right) in enumerate(((nt_s, gp), (db2t_s, hidden))):
            for half, dst in enumerate((mine_s, other_s)):
                term = dot(left[2 * part * half : 2 * part * (half + 1)], right, NN)
                dst[slot, k] = term.reshape(dst.shape[2:]).astype(bf16)

    def copy1(a):
        return send(other_s.at[a % 2], in1_s.at[a % 2], send1.at[a % 2], recv1.at[a % 2], to_core)

    def turn(a, even, odd):
        return tuple(e + (o - e) * (a % 2) for e, o in zip(even, odd))

    def copy2(a):
        return send(
            out2_s.at[a % 2], in2_s.at[a % 4], send2.at[a % 4], recv2.at[a % 4], turn(a, to_x, to_img)
        )

    def copy3(a):
        return send(
            out3_s.at[a % 2], in3_s.at[a % 4], send3.at[a % 4], recv3.at[a % 4], turn(a, to_img, to_x)
        )

    @pl.when(step >= 5)
    def _():
        a = step - 5
        copy3(a).wait()
        sum_ref[...] = plus(keep3_s[a % 2], in3_s[a % 4])

    @pl.when(jnp.logical_and(step >= 3, step < chunks + 3))
    def _():
        a = step - 3
        copy2(a).wait()
        side = y + (x - y) * (a % 2)
        out3_s[a % 2] = plus(keep2_s[a % 2, 1 - side], in2_s[a % 4, 1 - side])
        keep3_s[a % 2] = plus(keep2_s[a % 2, side], in2_s[a % 4, side])
        copy3(a).start()

    @pl.when(jnp.logical_and(step >= 1, step < chunks + 1))
    def _():
        a = step - 1
        s = a % 2
        copy1(a).wait()

        @pl.when(s == 0)
        def _():
            for k in range(2):
                out2_s[s, k] = plus(mine_s[s, k, 1 - x], in1_s[s, k, 1 - x])
                keep2_s[s, k] = plus(mine_s[s, k, x], in1_s[s, k, x])

        @pl.when(s == 1)
        def _():
            for k in range(2):
                out2_s[s, k] = plus(mine_s[s, 1 - y, k], in1_s[s, 1 - y, k])
                keep2_s[s, k] = plus(mine_s[s, y, k], in1_s[s, y, k])

        copy2(a).start()

    @pl.when(step < chunks)
    def _():
        copy1(step).start()

    @pl.when(step == chunks)
    def _():
        dbp = jnp.zeros((1, width), f32)
        dbd = jnp.zeros((1, width), f32)
        for i in range(blocks):
            rows = slice(i * blk, (i + 1) * blk)
            cot = cot_ref[rows].astype(f32)
            br2 = br2_s[rows] + bd_ref[...]
            mid = mid_s[rows]
            n_s[rows] = (mid + mod_ref[5, i : i + 1] * br2).astype(bf16)
            normed, rstd = norm(mid)
            gn = gn_s[rows]
            u = gn * (1.0 + mod_ref[4, i : i + 1])
            gmid = cot + rstd * (
                u
                - jnp.mean(u, axis=-1, keepdims=True)
                - normed * jnp.mean(u * normed, axis=-1, keepdims=True)
            )
            db1 = mod_ref[2, i : i + 1] * gmid
            db1_s[rows] = db1.astype(bf16)
            dbp += jnp.sum(db1, axis=0, keepdims=True)
            dbd += jnp.sum(db2_s[rows].astype(f32), axis=0, keepdims=True)
            db2_s[rows] = gmid.astype(bf16)
            dmod_ref[i, 0:1] = jnp.sum(gmid * br1_s[rows].astype(f32), axis=0, keepdims=True)
            dmod_ref[i, 1:2] = jnp.sum(gn, axis=0, keepdims=True)
            dmod_ref[i, 2:3] = jnp.sum(gn * normed, axis=0, keepdims=True)
            dmod_ref[i, 3:4] = jnp.sum(cot * br2, axis=0, keepdims=True)
        dbp_ref[...] = dbp
        dbd_ref[...] = dbd
        first = pltpu.make_async_copy(n_s, out_ref, done.at[0])
        second = pltpu.make_async_copy(db2_s, gmid_ref, done.at[1])
        first.start()
        second.start()
        dom_ref[...] = dot(db1_s[...], wpm_ref[...], NT).astype(bf16)
        doo_ref[...] = dot(db1_s[...], wpo_ref[...], NT).astype(bf16)
        dwpm_ref[...] = dot(am_ref[...], db1_s[...], TN).astype(bf16)
        dwpo_ref[...] = dot(ao_ref[...], db1_s[...], TN).astype(bf16)
        first.wait()
        second.wait()


def middle(x, cot, att_m, att_o, mod, wp_m, wp_o, b_proj, b_down, w_up, b_up, w_down, blk):
    tokens, width = x.shape
    pad = att_m.shape[1]
    hidden = w_up.shape[1]
    chunk = 512
    chunks = hidden // chunk
    n = width // 16
    any_ref = pl.BlockSpec(memory_space=pl.ANY)

    def at(j):
        return jnp.minimum(j, chunks - 1)

    return pl.pallas_call(
        functools.partial(middle_kernel, blk, chunks),
        grid=(chunks + 5,),
        in_specs=[VMEM] * 9
        + [
            pl.BlockSpec((width, chunk), lambda j: (0, at(j))),
            pl.BlockSpec((1, chunk), lambda j: (0, at(j))),
            pl.BlockSpec((chunk, width), lambda j: (at(j), 0)),
        ],
        out_specs=[any_ref, any_ref, VMEM, VMEM]
        + [
            pl.BlockSpec((4, n, chunk), lambda j: (0, 0, jnp.maximum(j - 5, 0))),
            pl.BlockSpec((1, chunk), lambda j: (0, at(j))),
        ]
        + [VMEM] * 5,
        scratch_shapes=[
            pltpu.VMEM((tokens, width), f32),
            pltpu.VMEM((tokens, width), bf16),
            pltpu.VMEM((tokens, width), bf16),
            pltpu.VMEM((width, tokens), bf16),
            pltpu.VMEM((tokens, width), bf16),
            pltpu.VMEM((width, tokens), bf16),
            pltpu.VMEM((tokens, width), f32),
            pltpu.VMEM((tokens, width), f32),
            pltpu.VMEM((tokens, width), bf16),
            pltpu.VMEM((2, 2, 2, 4, n, chunk), bf16),
            pltpu.VMEM((2, 2, 2, 4, n, chunk), bf16),
            pltpu.VMEM((2, 2, 2, 4, n, chunk), bf16),
            pltpu.VMEM((2, 2, 4, n, chunk), bf16),
            pltpu.VMEM((2, 2, 4, n, chunk), bf16),
            pltpu.VMEM((4, 2, 4, n, chunk), bf16),
            pltpu.VMEM((2, 4, n, chunk), bf16),
            pltpu.VMEM((2, 4, n, chunk), bf16),
            pltpu.VMEM((4, 4, n, chunk), bf16),
        ]
        + [pltpu.SemaphoreType.DMA((k,)) for k in (2, 2, 4, 4, 4, 4, 2)],
        out_shape=(
            shaped((tokens, width)),
            shaped((tokens, width)),
            shaped((tokens, pad)),
            shaped((tokens, pad)),
            shaped((4, n, hidden)),
            shaped((1, hidden), f32),
            shaped((pad, width)),
            shaped((pad, width)),
            shaped((tokens // blk, 4, width), f32),
            shaped((1, width), f32),
            shaped((1, width), f32),
        ),
        compiler_params=pltpu.CompilerParams(
            vmem_limit_bytes=62 * 2**20, collective_id=1, has_side_effects=True
        ),
        cost_estimate=pl.CostEstimate(
            flops=2 * tokens * width * (6 * hidden + 6 * pad),
            bytes_accessed=60 * 2**20,
            transcendentals=tokens * hidden,
        ),
        name="middle",
    )(x, cot, att_m, att_o, mod, wp_m, wp_o, b_proj, b_down, w_up, b_up, w_down)


def first_back_kernel(blk, x_ref, ga_ref, gb_ref, gmid_ref, mod_ref, out_ref, dmod_ref):
    for i in range(x_ref.shape[0] // blk):
        rows = slice(i * blk, (i + 1) * blk)
        y, rstd = norm(x_ref[rows].astype(f32))
        gn = ga_ref[rows].astype(f32) + gb_ref[rows].astype(f32)
        u = gn * (1.0 + mod_ref[1, pl.ds(2 * pl.program_id(0) + i, 1)])
        back = rstd * (
            u - jnp.mean(u, axis=-1, keepdims=True) - y * jnp.mean(u * y, axis=-1, keepdims=True)
        )
        out_ref[rows] = (gmid_ref[rows].astype(f32) + back).astype(bf16)
        dmod_ref[i, 0:1] = jnp.sum(gn, axis=0, keepdims=True)
        dmod_ref[i, 1:2] = jnp.sum(gn * y, axis=0, keepdims=True)


def first_back(x, part_a, part_b, gmid, mod, blk):
    tokens, width = x.shape
    steps = 3
    rows = tokens // steps
    each = pl.BlockSpec((rows, width), lambda s: (s, 0))
    return pl.pallas_call(
        functools.partial(first_back_kernel, blk),
        grid=(steps,),
        in_specs=[each] * 4 + [VMEM],
        out_specs=[each, pl.BlockSpec((rows // blk, 2, width), lambda s: (s, 0, 0))],
        out_shape=(shaped((tokens, width)), shaped((tokens // blk, 2, width), f32)),
        compiler_params=pltpu.CompilerParams(vmem_limit_bytes=VMEM_LIMIT),
        cost_estimate=pl.CostEstimate(
            flops=20 * tokens * width, bytes_accessed=10 * tokens * width, transcendentals=tokens
        ),
        name="first_back",
    )(x, part_a, part_b, gmid, mod)


def place_kernel(order_ref, in_ref, out_ref):
    out_ref[...] = in_ref[...].astype(out_ref.dtype)


def place(order, tiles, dtype):
    count = tiles.shape[0]
    block = (1,) + tiles.shape[1:]
    return pl.pallas_call(
        place_kernel,
        grid_spec=pltpu.PrefetchScalarGridSpec(
            num_scalar_prefetch=1,
            grid=(count,),
            in_specs=[pl.BlockSpec(block, lambda i, o: (o[i], 0, 0))],
            out_specs=pl.BlockSpec(block, lambda i, o: (i, 0, 0)),
        ),
        out_shape=shaped(tiles.shape, dtype),
        cost_estimate=pl.CostEstimate(
            flops=0, bytes_accessed=6 * math.prod(tiles.shape), transcendentals=0
        ),
        name="place",
    )(order, tiles)


def pick(values, index, axis=0):
    return lax.dynamic_index_in_dim(values, index, axis, keepdims=False)


def over_core(v):
    return lax.ppermute(v, "row", [(r, r ^ 1) for r in range(4)])


def over_x(v):
    return lax.ppermute(v, "row", [(r, r ^ 2) for r in range(4)])


def over_col(v, far):
    return lax.ppermute(v, "col", [(i, i ^ far) for i in range(4)])


def over_plane(v, dx, dz):
    swap = [(i, ((i // 4) ^ (2 * dx)) * 4 + ((i % 4) ^ dz)) for i in range(16)]
    return lax.ppermute(v, ("row", "col"), swap)


def over_img(v):
    if lax.axis_size("img") == 2:
        return v.astype(f32) + lax.ppermute(v, "img", [(0, 1), (1, 0)]).astype(f32)
    return lax.psum(v, "img").astype(f32)


def shards(
    tokens,
    conditioning,
    images_in_slot,
    w_qkv,
    b_qv,
    w_proj,
    b_proj,
    w_up,
    b_up,
    w_down,
    b_down,
    w_ada,
    b_ada,
    cotangent,
):
    slots, rows_tile, cols_tile, width = tokens.shape
    tile = rows_tile * cols_tile
    blk = 2 * tile
    count = slots * tile
    main = 8 * tile
    hd = width // HEADS
    heads = HEADS // 2
    half = width // 2
    pad = -(-half // 128) * 128
    hidden = w_up.shape[1]
    r, z = lax.axis_index("row"), lax.axis_index("col")
    x, core = r // 2, r % 2
    assert lax.axis_size("row") == 4 and lax.axis_size("col") == 4 and slots == 12

    def collect(values, dtype):
        tiles = values.reshape(12, tile, width)
        near, far, shared = [], [], []
        for dz in range(4):
            own = jnp.stack([tiles[dz], tiles[8 + dz]])
            if dz:
                own = over_plane(own, 0, dz)
            near.append(own[0])
            shared.append(own[1])
            far.append(over_plane(tiles[4 + dz], 1, dz))
        stacked = jnp.stack(near + far + shared)
        slot = jnp.arange(12, dtype=jnp.int32)
        kind = slot % 3
        dz = (slot // 3) ^ z
        order = jnp.where(kind == 2, 8 + dz, ((kind ^ x) & 1) * 4 + dz)
        return place(order, stacked, dtype).reshape(tokens.shape)

    four_way = images_in_slot == 4
    kinds = pick(four_way.reshape(4, 3), z)
    main_four, shared_four = pick(kinds, x), kinds[2]
    quarter = jnp.stack([2 * (x ^ dx) + ((z // 2) ^ dz) for dx in range(2) for dz in range(2)])
    picks = jnp.concatenate(
        [jnp.where(main_four, quarter, 0), jnp.where(shared_four, quarter[:2], 0)]
    )
    places = jnp.concatenate([jnp.full((4,), x, jnp.int32), jnp.full((2,), 2, jnp.int32)]) * 4 + picks
    flag_main = jnp.where(main_four, 0, 1).reshape(1).astype(jnp.int32)
    flag_shared = jnp.where(shared_four, 0, 1).reshape(1).astype(jnp.int32)
    bias = jnp.where(jnp.stack([main_four, shared_four]), -1e30, 0.0).astype(f32)
    cond = conditioning.astype(f32)
    silu = jax.nn.silu(cond).astype(bf16)
    silu_groups = silu.reshape(4, 12, width)
    chosen = jnp.take(pick(silu_groups, z), places, axis=0)
    chosen = jnp.pad(chosen, ((0, 2), (0, 0)))

    def widen(v, axis):
        return jnp.pad(v, [(0, pad - half) if a == axis else (0, 0) for a in range(v.ndim)])

    b_three = jnp.stack([b_qv[:width], jnp.zeros_like(b_qv[:width]), b_qv[width:]])
    b_half = widen(b_three.reshape(3, 2, half).astype(f32), 2).transpose(1, 0, 2)
    b_half = b_half.reshape(2, 1, 3 * pad)
    w_proj_half = widen(w_proj.reshape(2, half, width), 1)
    wp_mine, wp_other = pick(w_proj_half, core), pick(w_proj_half, 1 - core)

    (
        inputs,
        upstream,
        qkv_mine,
        qkv_sib,
        normed_t,
        normed_sib,
        far_kv,
        om,
        os,
        att_other,
        stat,
        mod,
        w_half,
    ) = forward(
        tokens.reshape(slots, tile, width),
        cotangent.reshape(slots, tile, width),
        w_qkv,
        w_ada,
        chosen,
        b_half,
        b_ada.astype(f32).reshape(6, 1, width),
        bias,
        heads,
        hd,
    )
    inputs = inputs.reshape(count, width)
    upstream = upstream.reshape(count, width)

    (
        out,
        gmid,
        do_mine,
        do_other,
        dw_sum,
        dbu,
        dwp_mine,
        dwp_other,
        dmod_mid,
        dbp,
        dbd,
    ) = middle(
        inputs,
        upstream,
        om,
        att_other,
        mod,
        wp_mine,
        wp_other,
        b_proj.astype(f32).reshape(1, width),
        b_down.astype(f32).reshape(1, width),
        w_up,
        b_up.astype(f32).reshape(1, hidden),
        w_down,
        blk,
    )
    output = collect(out, bf16)
    do_sib = over_core(do_other)

    def reduce_plane(mine):
        got = over_x(pick(mine, 1 - x))
        mine = plus(pick(mine, x), got)
        return over_img(reduce_col(mine))

    def reduce_col(mine):
        split = mine.reshape((2, 2) + mine.shape[1:])
        got = over_col(pick(split, 1 - z % 2, 1), 1)
        mine = plus(pick(split, z % 2, 1), got)
        got = over_col(pick(mine, 1 - z // 2), 2)
        return plus(pick(mine, z // 2), got)

    size = lax.axis_size("img")
    side = lax.axis_index("img") % 2
    dw = reduce_col(dw_sum)
    step = 2
    while step < size:
        dw = plus(dw, lax.ppermute(dw, "img", [(i, i ^ step) for i in range(size)]))
        step *= 2
    dw_there = lax.ppermute(dw, "img", [(i, i ^ 1) for i in range(size)])
    grad_w_up = jnp.where(side == 0, dw, dw_there).astype(f32)
    dwd = jnp.where(side == 0, dw_there, dw).reshape(width // 16, 16, hidden // 16)
    dwd = lax.all_to_all(dwd.transpose(1, 0, 2), ("row", "col"), 0, 0, tiled=True)
    grad_w_down = dwd.reshape(width, hidden // 16).T.astype(f32)
    dwp = jnp.stack([dwp_mine, dwp_other])
    dwp = jnp.stack([pick(dwp, core), pick(dwp, 1 - core)])[:, :half]
    dwp = dwp.reshape(2, 2, half // 2, width)
    dwp_sum = plus(pick(dwp, core, 1), over_core(pick(dwp, 1 - core, 1)))
    grad_w_proj = reduce_plane(dwp_sum.reshape(2, 4, width // 16, width))

    gm_far, gs_far, g_far = attend_back(
        flag_shared,
        qkv_mine,
        qkv_sib,
        do_mine,
        do_sib,
        om,
        os,
        stat,
        far_kv,
        heads,
        hd,
        2,
    )
    far_back = over_x(g_far)
    gm_near, gs_near = attend_back(
        flag_main, qkv_mine, qkv_sib, do_mine, do_sib, om, os, stat, None, heads, hd, 4
    )
    gm_far = jnp.concatenate([gm_far[:, :pad], plus(gm_far[:, pad:], far_back[: count - main])], 1)
    gs_far = jnp.concatenate([gs_far[:, :pad], plus(gs_far[:, pad:], far_back[count - main :])], 1)
    g_mine = jnp.concatenate([gm_near, gm_far], axis=0)
    g_sib = jnp.concatenate([gs_near, gs_far], axis=0)
    w_half_mine = pick(w_half, core)
    gn_other = over_core(dot(g_sib, w_half_mine, NT).astype(bf16))
    gn_mine = dot(g_mine, w_half_mine, NT).astype(bf16)
    dwq = (dot(normed_t, g_mine, NN) + dot(normed_sib, g_sib, NN)).astype(bf16)
    dwq = reduce_plane(
        dwq.reshape(2, 2, 4, width // 16, 3 * pad).transpose(0, 2, 1, 3, 4)
    )
    swap = over_core(pick(dwq, 1 - core).astype(bf16))
    parts = jnp.stack([pick(dwq, core), swap.astype(f32)])
    parts = jnp.stack([pick(parts, core), pick(parts, 1 - core)])
    parts = parts.reshape(2, width // 16, 3, pad)[..., :half]
    grad_w_qkv = parts.transpose(1, 2, 0, 3).reshape(width // 16, 3 * width)

    grad_x, dmod_first = first_back(inputs, gn_mine, gn_other, gmid, mod, blk)
    grad_tokens = collect(grad_x, f32)

    one_hot = (jnp.arange(12, dtype=jnp.int32)[:, None] == places[None, :]).astype(f32)
    silu_rel = jnp.concatenate([pick(silu_groups, z ^ dz) for dz in range(4)], axis=0)
    rank = r * 4 + z
    silu_rows = lax.dynamic_slice_in_dim(silu_rel, rank * (width // 16), width // 16, 1)

    def modulation_grads(dmod, columns):
        values = jnp.sum(one_hot[:, :, None] * dmod.reshape(1, 6, -1), axis=1).astype(bf16)
        values = plus(values, over_core(values))
        values = plus(values, over_x(values))
        every = jnp.concatenate(
            [values] + [over_col(values, dz) for dz in range(1, 4)], axis=0
        )
        d_w = over_img(dot(silu_rows, every, TN).astype(bf16))
        d_b = jnp.sum(every.astype(f32), axis=0)
        d_s = dot(every, w_ada[:, columns], NT)
        return d_w, d_b, d_s

    late = modulation_grads(dmod_first, slice(0, 2 * width))
    early = modulation_grads(dmod_mid, slice(2 * width, 6 * width))
    grad_w_ada = jnp.concatenate([late[0], early[0]], axis=1)
    d_s = (late[2] + early[2]).reshape(4, 12, width)
    d_s = jnp.stack([pick(d_s, z ^ g) for g in range(4)]).reshape(slots, 4, width)
    sig = jax.nn.sigmoid(cond)
    grad_conditioning = d_s * (sig * (1.0 + cond * (1.0 - sig)))

    db_three = jnp.sum(g_mine.astype(f32), axis=0) + jnp.sum(g_sib.astype(f32), axis=0)
    db_three = db_three.reshape(3, pad)[:, :half]
    db_three = jnp.where(
        (jnp.arange(2) == core)[None, :, None], db_three[:, None, :], 0.0
    ).reshape(3, width)
    small = jnp.concatenate([db_three[0], db_three[2], dbp[0], dbu[0], dbd[0]])
    small = lax.psum(small, ("row", "col", "img"))
    d_ada = jnp.concatenate([late[1], early[1]])
    d_ada = lax.dynamic_slice_in_dim(d_ada, rank * (6 * width // 16), 6 * width // 16, 0)
    grad_b_ada = over_img(d_ada)

    def own(start, size):
        return lax.dynamic_slice_in_dim(small, start + rank * (size // 16), size // 16, 0)

    return (
        output,
        grad_tokens,
        grad_conditioning,
        grad_w_qkv,
        own(0, 2 * width),
        grad_w_proj,
        own(2 * width, width),
        grad_w_up,
        own(3 * width, hidden),
        grad_w_down,
        own(3 * width + hidden, width),
        grad_w_ada,
        grad_b_ada,
    )


def solution(mesh):
    grid = P("img", "row", "col", None)
    plane = ("row", "col")
    return jax.shard_map(
        shards,
        mesh=mesh,
        in_specs=(grid, P("img", None, None), P("img")) + (P(),) * 10 + (grid,),
        out_specs=(grid, grid, P("img", None, None))
        + (P(plane, None), P(plane)) * 5,
        check_vma=False,
    )
```

```python
import functools
import math

import jax
import jax.numpy as jnp
from jax import lax
from jax.experimental import pallas as pl
from jax.experimental.pallas import tpu as pltpu
from jax.sharding import PartitionSpec as P

HEADS = 16
EPS = 1e-06
LOG2E = math.log2(math.e)
GELU_A = math.sqrt(2.0 / math.pi)
GELU_B = 0.044715
VMEM_LIMIT = 60 * 2**20

f32 = jnp.float32
bf16 = jnp.bfloat16
NT = (((1,), (1,)), ((), ()))
NN = (((1,), (0,)), ((), ()))
TN = (((0,), (0,)), ((), ()))

VMEM = pl.BlockSpec(memory_space=pltpu.VMEM)
SMEM = pl.BlockSpec(memory_space=pltpu.SMEM)


def dot(left, right, dims):
    return lax.dot_general(left, right, dims, preferred_element_type=f32)


def shaped(shape, dtype=bf16):
    return jax.ShapeDtypeStruct(shape, dtype)


def norm(values):
    center = values - jnp.mean(values, axis=-1, keepdims=True)
    rstd = lax.rsqrt(jnp.mean(center * center, axis=-1, keepdims=True) + EPS)
    return center * rstd, rstd


def plus(a, b):
    return (a.astype(f32) + b.astype(f32)).astype(bf16)


def flip(index):
    return index + 1 - 2 * (index % 2)


def partners():
    img, r, z = lax.axis_index("img"), lax.axis_index("row"), lax.axis_index("col")
    return (img, flip(r), z), (img, (r + 2) % 4, z), (flip(img), r, z)


def plane_device(dx, dz):
    img, r, z = lax.axis_index("img"), lax.axis_index("row"), lax.axis_index("col")
    return img, (r + 2 * dx) % 4, hop(z, dz)


def hop(z, dz):
    return (z, flip(z), (z + 2) % 4, 3 - z)[dz]


def greet(devices):
    barrier = pltpu.get_barrier_semaphore()
    for device in devices:
        pl.semaphore_signal(
            barrier, inc=1, device_id=device, device_id_type=pl.DeviceIdType.MESH
        )
    pl.semaphore_wait(barrier, len(devices))


def send(src, dst, send_sem, recv_sem, device):
    return pltpu.make_async_remote_copy(
        src_ref=src,
        dst_ref=dst,
        send_sem=send_sem,
        recv_sem=recv_sem,
        device_id=device,
        device_id_type=pl.DeviceIdType.MESH,
    )


def tile_moves(src, dst, send_sem, recv_sem, local_sem):
    r, z = lax.axis_index("row"), lax.axis_index("col")
    x = r // 2
    shared, near, far, local = [], [], [], []
    for dz in range(4):
        first = 3 * hop(z, dz)
        moves = (
            (shared, 0, first + 2, 8 + dz),
            (near, 0, first + x, dz),
            (far, 1, first + 1 - x, 4 + dz),
        )
        for group, dx, slot, place_at in moves:
            if dx == 0 and dz == 0:
                sem = local_sem.at[0 if place_at else 1]
                local.append(pltpu.make_async_copy(src.at[slot], dst.at[place_at], sem))
            else:
                sems = send_sem.at[place_at], recv_sem.at[place_at]
                group.append(
                    send(src.at[slot], dst.at[place_at], *sems, plane_device(dx, dz))
                )
    return local, shared, near, far


def head_window(head, hd):
    first = head * hd
    start = pl.multiple_of((first // 128) * 128, 128)
    lane = lax.broadcasted_iota(jnp.int32, (1, 256), 1) + start
    inside = jnp.logical_and(lane >= first, lane < first + hd)
    return pl.ds(start, 256), inside


def gather_rows(dst, col, sources, base, count):
    pad = dst.shape[1]
    for i in range(count):
        for j, src in enumerate(sources):
            row = 256 * i + 128 * j
            dst[row : row + 128] = src[base + 128 * i : base + 128 * i + 128, col : col + pad]


def attend(heads, hd, count, base, bias, mine, sib, far, o_mine, o_sib, stat, q_s, k_s, v_s, o_s):
    pad = q_s.shape[1]
    scale = LOG2E / math.sqrt(hd)
    gather_rows(q_s, 0, (mine, sib), base, count)
    gather_rows(k_s, pad, (mine, sib), base, count)
    gather_rows(v_s, 2 * pad, (mine, sib), base, count)
    if far is not None:
        k_s[256 * count :] = far[:, 0:pad]
        v_s[256 * count :] = far[:, pad : 2 * pad]
    blocks = k_s.shape[0] // 256
    lane = lax.broadcasted_iota(jnp.int32, (1, 128), 1)

    def body(head, carry):
        win, inside = head_window(head, hd)
        for i in range(count):
            rows = slice(256 * i, 256 * i + 256)
            q = jnp.where(inside, q_s[rows, win], jnp.zeros((), bf16))
            s = dot(q, k_s[:, win], NT)
            cols = [s[:, 256 * j : 256 * j + 256] for j in range(blocks)]
            best = [jnp.max(col, axis=1, keepdims=True) for col in cols]
            own = best[i]
            rest = best[:i] + best[i + 1 :]
            top = jnp.maximum(own, functools.reduce(jnp.maximum, rest) + bias)
            near = -scale * top
            away = near + bias
            cols = [
                jnp.exp2(col * scale + (near if j == i else away)) for j, col in enumerate(cols)
            ]
            total = functools.reduce(
                jnp.add, [jnp.sum(col, axis=1, keepdims=True) for col in cols]
            )
            p = jnp.concatenate([col.astype(bf16) for col in cols], axis=1)
            o = dot(p, v_s[:, win], NN) / total
            o_s[rows, win] = jnp.where(inside, o.astype(bf16), o_s[rows, win])
            at = slice(2 * base + 256 * i, 2 * base + 256 * i + 256)
            stat[at] = jnp.where(lane == head, top * scale + jnp.log2(total), stat[at])
        return carry

    lax.fori_loop(0, heads, body, 0)
    for i in range(count):
        at = slice(base + 128 * i, base + 128 * i + 128)
        o_mine[at] = o_s[256 * i : 256 * i + 128]
        o_sib[at] = o_s[256 * i + 128 : 256 * i + 256]


def forward_kernel(
    heads,
    hd,
    tok_ref,
    cot_ref,
    wq_ref,
    wa_ref,
    chosen_ref,
    bh_ref,
    ba_ref,
    bias_ref,
    x_out,
    cot_out,
    mine_out,
    sib_out,
    nt_out,
    ntsib_out,
    far_out,
    om_out,
    os_out,
    ao_out,
    stat_out,
    mod_out,
    wh_out,
    x_s,
    raw_s,
    w_s,
    wa_s,
    mod_s,
    nt_s,
    ntsib_s,
    other_s,
    mine_s,
    sib_s,
    far_s,
    q_s,
    k_s,
    v_s,
    o_s,
    om_s,
    os_s,
    ao_s,
    stat_s,
    tok_send,
    tok_recv,
    cot_send,
    cot_recv,
    local_sem,
    raw_sem,
    wa_sem,
    side_send,
    side_recv,
    out_sem,
):
    tile, width = x_s.shape[1:]
    tokens = 12 * tile
    main = 8 * tile
    half = width // 2
    pad = w_s.shape[2] // 3
    rows_step = raw_s.shape[1]
    core = lax.axis_index("row") % 2
    to_core, to_x, _ = partners()

    raw = [
        pltpu.make_async_copy(
            wq_ref.at[pl.ds(i * rows_step, rows_step)], raw_s.at[i % 2], raw_sem.at[i % 2]
        )
        for i in range(width // rows_step)
    ]
    ada = [
        pltpu.make_async_copy(
            wa_ref.at[:, pl.ds(i * width, width)], wa_s.at[i % 2], wa_sem.at[i % 2]
        )
        for i in range(6)
    ]
    for copy in raw[:2] + ada[:2]:
        copy.start()
    greet([to_core] + [plane_device(dx, dz) for dx in range(2) for dz in range(4) if dx or dz])
    local, shared, near, far = tile_moves(tok_ref, x_s, tok_send, tok_recv, local_sem)
    for copy in local + shared + near + far:
        copy.start()

    w_s[...] = jnp.zeros_like(w_s)
    for i, copy in enumerate(raw):
        copy.wait()
        rows = slice(i * rows_step, (i + 1) * rows_step)
        for h in range(2):
            for p in range(3):
                start = half * (2 * p + h)
                w_s[h, rows, p * pad : p * pad + half] = raw_s[i % 2, :, start : start + half]
        if i + 2 < len(raw):
            raw[i + 2].start()
    for i, copy in enumerate(ada):
        copy.wait()
        mod_s[i] = dot(chosen_ref[...], wa_s[i % 2], NN) + ba_ref[i]
        if i + 2 < len(ada):
            ada[i + 2].start()
    outs = []

    def put(src, dst):
        copy = pltpu.make_async_copy(src, dst, out_sem.at[len(outs)])
        copy.start()
        outs.append(copy)

    put(w_s, wh_out)
    put(mod_s, mod_out)

    sides = []

    def side(src, dst, device):
        k = len(sides)
        copy = send(src, dst, side_send.at[k], side_recv.at[k], device)
        copy.start()
        sides.append(copy)
        return copy

    moves = None
    from_core = []
    for first, waits in ((8, local[:1] + shared), (0, local[1:] + near), (4, far)):
        for copy in waits:
            copy.wait()
        if first == 4:
            moves = tile_moves(cot_ref, cot_out, cot_send, cot_recv, local_sem)
            for group in moves:
                for copy in group:
                    copy.start()
        parts = []
        for i in range(2):
            at = first // 2 + i
            values = x_s[first + 2 * i : first + 2 * i + 2].reshape(2 * tile, width)
            normed, _ = norm(values.astype(f32))
            parts.append((normed * (1.0 + mod_s[1, at : at + 1]) + mod_s[0, at : at + 1]).astype(bf16))
        normed = jnp.concatenate(parts, axis=0)
        rows = slice(first * tile, (first + 4) * tile)
        other_s[rows] = (dot(normed, w_s[1 - core], NN) + bh_ref[1 - core]).astype(bf16)
        at = pl.ds(first * tile, 4 * tile)
        from_core.append(side(other_s.at[at], sib_s.at[at], to_core))
        mine_s[rows] = (dot(normed, w_s[core], NN) + bh_ref[core]).astype(bf16)
        nt_s[:, rows] = normed.T
        if first == 0:
            from_core[0].wait_recv()
            at, cols = pl.ds(main, tokens - main), pl.ds(pad, 2 * pad)
            size = tokens - main
            from_x = [
                side(src.at[at, cols], far_s.at[pl.ds(size * k, size)], to_x)
                for k, src in enumerate((mine_s, sib_s))
            ]
    put(x_s, x_out)
    put(mine_s, mine_out)
    put(nt_s, nt_out)
    nt_copy = side(nt_s, ntsib_s, to_core)

    o_s[...] = jnp.zeros_like(o_s)
    stat_s[...] = jnp.zeros_like(stat_s)
    for copy in from_core[1:]:
        copy.wait_recv()
    put(sib_s, sib_out)
    scratch = (om_s, os_s, stat_s, q_s, k_s, v_s, o_s)
    attend(heads, hd, 4, 0, bias_ref[0], mine_s, sib_s, None, *scratch)
    back = [side(os_s.at[pl.ds(0, main)], ao_s.at[pl.ds(0, main)], to_core)]
    for copy in from_x:
        copy.wait_recv()
    put(far_s, far_out)
    attend(heads, hd, 2, main, bias_ref[1], mine_s, sib_s, far_s, *scratch)
    at = pl.ds(main, tokens - main)
    back.append(side(os_s.at[at], ao_s.at[at], to_core))
    put(om_s, om_out)
    put(os_s, os_out)
    put(stat_s, stat_out)
    nt_copy.wait_recv()
    put(ntsib_s, ntsib_out)
    for copy in back:
        copy.wait_recv()
    put(ao_s, ao_out)
    for copy in sides:
        copy.wait_send()
    for group in moves:
        for copy in group:
            copy.wait()
    for copy in outs:
        copy.wait()


def forward(tok, cot, w_qkv, w_ada, chosen, b_half, b_ada, bias, heads, hd):
    _, tile, width = tok.shape
    tokens = 12 * tile
    pad = b_half.shape[2] // 3
    any_ref = pl.BlockSpec(memory_space=pl.ANY)
    outs = (
        shaped((12, tile, width)),
        shaped((12, tile, width)),
        shaped((tokens, 3 * pad)),
        shaped((tokens, 3 * pad)),
        shaped((width, tokens)),
        shaped((width, tokens)),
        shaped((8 * tile, 2 * pad)),
        shaped((tokens, pad)),
        shaped((tokens, pad)),
        shaped((tokens, pad)),
        shaped((2 * tokens, 128), f32),
        shaped((6, 8, width), f32),
        shaped((2, width, 3 * pad)),
    )
    scratch = [
        outs[0],
        shaped((2, width // 4, 3 * width)),
        outs[12],
        shaped((2, width, width)),
        outs[11],
        outs[4],
        outs[4],
        outs[2],
        outs[2],
        outs[2],
        outs[6],
        shaped((16 * tile, pad)),
        shaped((16 * tile, pad)),
        shaped((16 * tile, pad)),
        shaped((16 * tile, pad)),
        outs[7],
        outs[7],
        outs[7],
        outs[10],
    ]
    return pl.pallas_call(
        functools.partial(forward_kernel, heads, hd),
        in_specs=[any_ref] * 4 + [VMEM] * 3 + [SMEM],
        out_specs=(any_ref,) * len(outs),
        scratch_shapes=[pltpu.VMEM(s.shape, s.dtype) for s in scratch]
        + [pltpu.SemaphoreType.DMA((k,)) for k in (12, 12, 12, 12, 2, 2, 2, 10, 10, 12)],
        out_shape=outs,
        compiler_params=pltpu.CompilerParams(
            vmem_limit_bytes=62 * 2**20, collective_id=2, has_side_effects=True
        ),
        cost_estimate=pl.CostEstimate(
            flops=4 * tokens * width * 3 * pad + 4096 * heads * tokens * 16 * tile,
            bytes_accessed=70 * 2**20,
            transcendentals=heads * 2 * tokens * 16 * tile,
        ),
        name="forward",
    )(tok, cot, w_qkv, w_ada, chosen, b_half, b_ada, bias)


def middle_kernel(
    blk,
    chunks,
    x_ref,
    cot_ref,
    am_ref,
    ao_ref,
    mod_ref,
    wpm_ref,
    wpo_ref,
    bp_ref,
    bd_ref,
    wu_ref,
    bu_ref,
    wd_ref,
    out_ref,
    gmid_ref,
    dom_ref,
    doo_ref,
    sum_ref,
    dbu_ref,
    dwp_ref,
    dmod_ref,
    dbp_ref,
    dbd_ref,
    mid_s,
    br1_s,
    n_s,
    nt_s,
    db2_s,
    db2t_s,
    br2_s,
    gn_s,
    db1_s,
    mine_s,
    other_s,
    in1_s,
    out2_s,
    keep2_s,
    in2_s,
    out3_s,
    keep3_s,
    in3_s,
    out4_s,
    keep4_s,
    in4_s,
    out5_s,
    keep5_s,
    in5_s,
    sems,
    done,
):
    step = pl.program_id(0)
    tokens, width = x_ref.shape
    pad = am_ref.shape[1]
    blocks = tokens // blk
    part = width // 4
    row = lax.axis_index("row")
    x, core, y = row // 2, row % 2, lax.axis_index("img") % 2
    z = lax.axis_index("col")
    zh, zl = z // 2, z % 2
    to_core, to_x, to_img = partners()
    to_near, to_far = plane_device(0, 1), plane_device(0, 2)

    @pl.when(step == 0)
    def _():
        greet((to_core, to_x, to_img, to_near, to_far))
        br1_s[...] = (
            dot(am_ref[...], wpm_ref[...], NN) + dot(ao_ref[...], wpo_ref[...], NN) + bp_ref[...]
        ).astype(bf16)
        for i in range(blocks):
            rows = slice(i * blk, (i + 1) * blk)
            mid = x_ref[rows].astype(f32) + mod_ref[2, i : i + 1] * br1_s[rows].astype(f32)
            mid_s[rows] = mid
            normed, _ = norm(mid)
            n_s[rows] = (normed * (1.0 + mod_ref[4, i : i + 1]) + mod_ref[3, i : i + 1]).astype(bf16)
            db2_s[rows] = (mod_ref[5, i : i + 1] * cot_ref[rows].astype(f32)).astype(bf16)
        for g in range(4):
            place_row = ((g + core) % 2) * (2 * part) + (g // 2) * part
            place_row = pl.ds(pl.multiple_of(place_row, 16), part)
            cols = slice(g * part, (g + 1) * part)
            nt_s[place_row] = n_s[:, cols].astype(f32).T.astype(bf16)
            db2t_s[place_row] = db2_s[:, cols].astype(f32).T.astype(bf16)
        br2_s[...] = jnp.zeros_like(br2_s)
        gn_s[...] = jnp.zeros_like(gn_s)

    @pl.when(step < chunks)
    def _():
        slot = step % 2
        pre = dot(n_s[...], wu_ref[...], NN) + bu_ref[...]
        square = pre * pre
        t = jnp.tanh(pre * (GELU_A + (GELU_A * GELU_B) * square))
        hidden = (0.5 * pre * (1.0 + t)).astype(bf16)
        slope = 0.5 * (1.0 + t) + 0.5 * pre * (1.0 - t * t) * (
            GELU_A + (3.0 * GELU_A * GELU_B) * square
        )
        br2_s[...] += dot(hidden, wd_ref[...], NN)
        gpre = dot(db2_s[...], wd_ref[...], NT) * slope
        gp = gpre.astype(bf16)
        gn_s[...] += dot(gp, wu_ref[...], NT)
        dbu_ref[...] = jnp.sum(gpre, axis=0, keepdims=True)
        for k, (left, right) in enumerate(((nt_s, gp), (db2t_s, hidden))):
            for half, dst in enumerate((mine_s, other_s)):
                term = dot(left[2 * part * half : 2 * part * (half + 1)], right, NN)
                dst[slot, k] = term.reshape(dst.shape[2:]).astype(bf16)

    def copy(k, a, src, dst, device):
        return send(src, dst, sems.at[0, k, a % 4], sems.at[1, k, a % 4], device)

    def stage1(a):
        return [copy(0, a, other_s.at[a % 2], in1_s.at[a % 2], to_core)]

    def stage2(a):
        return [
            copy(1 + h, a, out2_s.at[a % 2, h], in2_s.at[a % 4, h], (to_x, to_img)[h]) for h in range(2)
        ]

    def stage3(a):
        return [
            copy(3 + h, a, out3_s.at[a % 2, h], in3_s.at[a % 4, h], (to_img, to_x)[h]) for h in range(2)
        ]

    def stage4(a):
        return [copy(5, a, out4_s, in4_s.at[a % 2], to_near)]

    def stage5(a):
        return [copy(6, a, out5_s, in5_s.at[a % 2], to_far)]

    def when(lag):
        return pl.when(jnp.logical_and(step >= lag, step < chunks + lag))

    def go(copies):
        for c in copies:
            c.start()

    def settle(copies):
        for c in copies:
            c.wait()

    @when(7)
    def _():
        a = step - 7
        settle(stage5(a))
        sum_ref[...] = plus(keep5_s[...], in5_s[a % 2])

    @when(6)
    def _():
        a = step - 6
        settle(stage4(a))
        out5_s[...] = plus(keep4_s[1 - zh], in4_s[a % 2, 1 - zh])
        keep5_s[...] = plus(keep4_s[zh], in4_s[a % 2, zh])
        go(stage5(a))

    @when(5)
    def _():
        a = step - 5
        settle(stage3(a))
        t = a % 2
        for h in range(2):
            out4_s[h] = plus(keep3_s[t, h, 1 - zl], in3_s[a % 4, h, 1 - zl])
            keep4_s[h] = plus(keep3_s[t, h, zl], in3_s[a % 4, h, zl])
        go(stage4(a))

    @when(3)
    def _():
        a = step - 3
        t = a % 2
        settle(stage2(a))
        for h, side in enumerate((y, x)):
            out3_s[t, h] = plus(keep2_s[t, h, 1 - side], in2_s[a % 4, h, 1 - side])
            keep3_s[t, h] = plus(keep2_s[t, h, side], in2_s[a % 4, h, side])
        go(stage3(a))

    @when(1)
    def _():
        a = step - 1
        s = a % 2
        settle(stage1(a))
        for k in range(2):
            low, high = slice(0, 2), slice(2, 4)
            out2_s[s, 0, k] = plus(mine_s[s, k, 1 - x, low], in1_s[s, k, 1 - x, low])
            keep2_s[s, 0, k] = plus(mine_s[s, k, x, low], in1_s[s, k, x, low])
            out2_s[s, 1, k] = plus(mine_s[s, 1 - y, k, high], in1_s[s, 1 - y, k, high])
            keep2_s[s, 1, k] = plus(mine_s[s, y, k, high], in1_s[s, y, k, high])
        go(stage2(a))

    @pl.when(step < chunks)
    def _():
        go(stage1(step))

    @pl.when(step == chunks)
    def _():
        dbp = jnp.zeros((1, width), f32)
        dbd = jnp.zeros((1, width), f32)
        for i in range(blocks):
            rows = slice(i * blk, (i + 1) * blk)
            cot = cot_ref[rows].astype(f32)
            br2 = br2_s[rows] + bd_ref[...]
            mid = mid_s[rows]
            n_s[rows] = (mid + mod_ref[5, i : i + 1] * br2).astype(bf16)
            normed, rstd = norm(mid)
            gn = gn_s[rows]
            u = gn * (1.0 + mod_ref[4, i : i + 1])
            gmid = cot + rstd * (
                u
                - jnp.mean(u, axis=-1, keepdims=True)
                - normed * jnp.mean(u * normed, axis=-1, keepdims=True)
            )
            db1 = mod_ref[2, i : i + 1] * gmid
            db1_s[rows] = db1.astype(bf16)
            dbp += jnp.sum(db1, axis=0, keepdims=True)
            dbd += jnp.sum(db2_s[rows].astype(f32), axis=0, keepdims=True)
            db2_s[rows] = gmid.astype(bf16)
            dmod_ref[i, 0:1] = jnp.sum(gmid * br1_s[rows].astype(f32), axis=0, keepdims=True)
            dmod_ref[i, 1:2] = jnp.sum(gn, axis=0, keepdims=True)
            dmod_ref[i, 2:3] = jnp.sum(gn * normed, axis=0, keepdims=True)
            dmod_ref[i, 3:4] = jnp.sum(cot * br2, axis=0, keepdims=True)
        dbp_ref[...] = dbp
        dbd_ref[...] = dbd
        first = pltpu.make_async_copy(n_s, out_ref, done.at[0])
        second = pltpu.make_async_copy(db2_s, gmid_ref, done.at[1])
        first.start()
        second.start()
        dom_ref[...] = dot(db1_s[...], wpm_ref[...], NT).astype(bf16)
        doo_ref[...] = dot(db1_s[...], wpo_ref[...], NT).astype(bf16)
        for side, ref in ((core, am_ref), (1 - core, ao_ref)):
            term = dot(ref[...], db1_s[...], TN)
            for c in range(2):
                rows = term[2 * part * c // 2 : 2 * part * (c + 1) // 2]
                for k, at in enumerate((0, width - pad)):
                    dwp_ref[(c + core) % 2, k, side] = rows[:, at : at + pad].astype(bf16)
        first.wait()
        second.wait()


def middle(x, cot, att_m, att_o, mod, wp_m, wp_o, b_proj, b_down, w_up, b_up, w_down, blk):
    tokens, width = x.shape
    pad = att_m.shape[1]
    hidden = w_up.shape[1]
    chunk = 512
    chunks = hidden // chunk
    n = width // 16
    any_ref = pl.BlockSpec(memory_space=pl.ANY)

    def at(j):
        return jnp.minimum(j, chunks - 1)

    return pl.pallas_call(
        functools.partial(middle_kernel, blk, chunks),
        grid=(chunks + 7,),
        in_specs=[VMEM] * 9
        + [
            pl.BlockSpec((width, chunk), lambda j: (0, at(j))),
            pl.BlockSpec((1, chunk), lambda j: (0, at(j))),
            pl.BlockSpec((chunk, width), lambda j: (at(j), 0)),
        ],
        out_specs=[any_ref, any_ref, VMEM, VMEM]
        + [
            pl.BlockSpec((n, chunk), lambda j: (0, jnp.maximum(j - 7, 0))),
            pl.BlockSpec((1, chunk), lambda j: (0, at(j))),
        ]
        + [VMEM] * 4,
        scratch_shapes=[
            pltpu.VMEM((tokens, width), f32),
            pltpu.VMEM((tokens, width), bf16),
            pltpu.VMEM((tokens, width), bf16),
            pltpu.VMEM((width, tokens), bf16),
            pltpu.VMEM((tokens, width), bf16),
            pltpu.VMEM((width, tokens), bf16),
            pltpu.VMEM((tokens, width), f32),
            pltpu.VMEM((tokens, width), f32),
            pltpu.VMEM((tokens, width), bf16),
            pltpu.VMEM((2, 2, 2, 4, n, chunk), bf16),
            pltpu.VMEM((2, 2, 2, 4, n, chunk), bf16),
            pltpu.VMEM((2, 2, 2, 4, n, chunk), bf16),
            pltpu.VMEM((2, 2, 2, 2, n, chunk), bf16),
            pltpu.VMEM((2, 2, 2, 2, n, chunk), bf16),
            pltpu.VMEM((4, 2, 2, 2, n, chunk), bf16),
            pltpu.VMEM((2, 2, 2, n, chunk), bf16),
            pltpu.VMEM((2, 2, 2, n, chunk), bf16),
            pltpu.VMEM((4, 2, 2, n, chunk), bf16),
            pltpu.VMEM((2, n, chunk), bf16),
            pltpu.VMEM((2, n, chunk), bf16),
            pltpu.VMEM((2, 2, n, chunk), bf16),
            pltpu.VMEM((n, chunk), bf16),
            pltpu.VMEM((n, chunk), bf16),
            pltpu.VMEM((2, n, chunk), bf16),
            pltpu.SemaphoreType.DMA((2, 7, 4)),
            pltpu.SemaphoreType.DMA((2,)),
        ],
        out_shape=(
            shaped((tokens, width)),
            shaped((tokens, width)),
            shaped((tokens, pad)),
            shaped((tokens, pad)),
            shaped((n, hidden)),
            shaped((1, hidden), f32),
            shaped((2, 2, 2, 4 * n, pad)),
            shaped((tokens // blk, 4, width), f32),
            shaped((1, width), f32),
            shaped((1, width), f32),
        ),
        compiler_params=pltpu.CompilerParams(
            vmem_limit_bytes=62 * 2**20, collective_id=1, has_side_effects=True
        ),
        cost_estimate=pl.CostEstimate(
            flops=2 * tokens * width * (6 * hidden + 6 * pad),
            bytes_accessed=60 * 2**20,
            transcendentals=tokens * hidden,
        ),
        name="middle",
    )(x, cot, att_m, att_o, mod, wp_m, wp_o, b_proj, b_down, w_up, b_up, w_down)


def attend_back(heads, hd, count, base, bias, mine, sib, far, d_mine, d_sib, o_mine, o_sib, stat,
                g_mine, g_sib, g_far, q_s, k_s, v_s, do_s, kt_s, dqt_s, dk_s, dv_s, p_s, ds_s,
                lse_s, dd_s):
    pad = q_s.shape[1]
    inv = 1.0 / math.sqrt(hd)
    scale = LOG2E * inv
    pair = (mine, sib)
    gather_rows(q_s, 0, pair, base, count)
    gather_rows(k_s, pad, pair, base, count)
    gather_rows(v_s, 2 * pad, pair, base, count)
    gather_rows(do_s, 0, (d_mine, d_sib), base, count)
    if far is not None:
        k_s[256 * count :] = far[:, 0:pad]
        v_s[256 * count :] = far[:, pad : 2 * pad]
    kt_s[...] = k_s[...].astype(f32).T
    dqt_s[...] = jnp.zeros_like(dqt_s)
    dk_s[...] = jnp.zeros_like(dk_s)
    dv_s[...] = jnp.zeros_like(dv_s)
    blocks = k_s.shape[0] // 256
    used = 256 * count
    row = lax.broadcasted_iota(jnp.int32, (heads, pad), 0)
    col = lax.broadcasted_iota(jnp.int32, (heads, pad), 1)
    member = jnp.where(jnp.logical_and(col >= row * hd, col < row * hd + hd), 1.0, 0.0).astype(bf16)
    for i in range(count):
        rows = slice(256 * i, 256 * i + 256)
        at = 2 * base + 256 * i
        lse_s[i] = stat[at : at + 256].T[0:heads]
        o = jnp.concatenate(
            [ref[base + 128 * i : base + 128 * i + 128] for ref in (o_mine, o_sib)], axis=0
        )
        both = do_s[rows].astype(f32) * o.astype(f32)
        high = both.astype(bf16)
        low = (both - high.astype(f32)).astype(bf16)
        dd_s[i] = dot(member, high, NT) + dot(member, low, NT)

    def body(head, carry):
        win, inside = head_window(head, hd)
        own = pl.ds(pl.multiple_of(head * hd, 8), hd)
        zero = jnp.zeros((), bf16)
        for i in range(count):
            rows = slice(256 * i, 256 * i + 256)
            q = jnp.where(inside, q_s[rows, win], zero)
            do = jnp.where(inside, do_s[rows, win], zero)
            near = -lse_s[i, pl.ds(head, 1)]
            away = near + bias
            dd = dd_s[i, pl.ds(head, 1)]
            s = dot(k_s[:, win], q, NT)
            dp = dot(v_s[:, win], do, NT)
            for j in range(blocks):
                keys = slice(256 * j, 256 * j + 256)
                p = jnp.exp2(s[keys] * scale + (near if j == i else away))
                ds_s[keys, rows] = (p * (dp[keys] - dd)).astype(bf16)
                p_s[keys, rows] = p.astype(bf16)
        q = jnp.where(inside, q_s[0:used, win], zero)
        do = jnp.where(inside, do_s[0:used, win], zero)
        dv_s[:, win] += dot(p_s[:, 0:used], do, NN)
        dk_s[:, win] += dot(ds_s[:, 0:used], q, NN)
        dqt_s[own, 0:used] = dot(kt_s[own, :].astype(bf16), ds_s[:, 0:used], NN)
        return carry

    lax.fori_loop(0, heads, body, 0)
    for i in range(count):
        for j, dst in enumerate((g_mine, g_sib)):
            rows = slice(256 * i + 128 * j, 256 * i + 128 * j + 128)
            out = slice(base + 128 * i, base + 128 * i + 128)
            dst[out, 0:pad] = (dqt_s[:, rows] * inv).T.astype(bf16)
            dst[out, pad : 2 * pad] = (dk_s[rows] * inv).astype(bf16)
            dst[out, 2 * pad : 3 * pad] = dv_s[rows].astype(bf16)
    if far is not None:
        g_far[:, 0:pad] = (dk_s[used:] * inv).astype(bf16)
        g_far[:, pad : 2 * pad] = dv_s[used:].astype(bf16)


def return_moves(src, dst, send_sem, recv_sem, local_sem):
    r, z = lax.axis_index("row"), lax.axis_index("col")
    local, near, far, shared = [], [], [], []
    for dz in range(4):
        for group, dx, slot, at in (
            (near, 0, 3 * z + r // 2, dz),
            (far, 1, 3 * z + r // 2, 4 + dz),
            (shared, 0, 3 * z + 2, 8 + dz),
        ):
            if dx == 0 and dz == 0:
                sem = local_sem.at[0 if at else 1]
                local.append((at, pltpu.make_async_copy(src.at[at], dst.at[slot], sem)))
            else:
                sems = send_sem.at[at], recv_sem.at[at]
                copy = send(src.at[at], dst.at[slot], *sems, plane_device(dx, dz))
                group.append((at, copy))
    return local + near + far + shared


def back_kernel(
    heads,
    hd,
    mine_ref,
    sib_ref,
    far_ref,
    dom_ref,
    doo_ref,
    om_ref,
    os_ref,
    stat_ref,
    out_ref,
    sum_ref,
    bias_ref,
    gm_out,
    gs_out,
    tiles_out,
    dwu_out,
    dwd_out,
    mine_s,
    sib_s,
    far_s,
    dom_s,
    dos_s,
    om_s,
    os_s,
    stat_s,
    gm_s,
    gs_s,
    gfar_s,
    back_s,
    q_s,
    k_s,
    v_s,
    do_s,
    kt_s,
    dqt_s,
    dk_s,
    dv_s,
    p_s,
    ds_s,
    lse_s,
    dd_s,
    sum_s,
    piece_s,
    here_s,
    there_s,
    turn_s,
    dwd_s,
    dwu_s,
    tile_send,
    tile_recv,
    local_sem,
    side_send,
    side_recv,
    piece_send,
    piece_recv,
    load_sem,
    out_sem,
):
    row, z = lax.axis_index("row"), lax.axis_index("col")
    x, core, side = row // 2, row % 2, lax.axis_index("img") % 2
    to_core, to_x, to_img = partners()
    tokens = mine_s.shape[0]
    pad = om_s.shape[1]
    main = 2 * tokens // 3
    n = sum_s.shape[1]
    wide = piece_s.shape[4]

    loads = []

    def load(src, dst):
        copy = pltpu.make_async_copy(src, dst, load_sem.at[len(loads)])
        copy.start()
        loads.append(copy)

    sides = []

    def start(src, dst, device):
        k = len(sides)
        copy = send(src, dst, side_send.at[k], side_recv.at[k], device)
        copy.start()
        sides.append(copy)
        return copy

    for src, dst in (
        (mine_ref, mine_s),
        (sib_ref, sib_s),
        (far_ref, far_s),
        (dom_ref, dom_s),
        (om_ref, om_s),
        (os_ref, os_s),
        (stat_ref, stat_s),
    ):
        load(src, dst)
    load(sum_ref, sum_s.at[side])
    greet(
        [to_core, to_img] + [plane_device(dx, dz) for dx in range(2) for dz in range(4) if dx or dz]
    )
    from_core = start(doo_ref, dos_s, to_core)
    from_img = start(sum_ref, sum_s.at[side], to_img)
    moves = return_moves(out_ref, tiles_out, tile_send, tile_recv, local_sem)
    for _, copy in moves:
        copy.start()
    for copy in loads:
        copy.wait()
    from_core.wait_recv()
    scratch = (q_s, k_s, v_s, do_s, kt_s, dqt_s, dk_s, dv_s, p_s, ds_s, lse_s, dd_s)
    inputs = (dom_s, dos_s, om_s, os_s, stat_s, gm_s, gs_s, gfar_s)
    attend_back(heads, hd, 2, main, bias_ref[1], mine_s, sib_s, far_s, *inputs, *scratch)
    from_x = start(gfar_s, back_s, to_x)

    from_img.wait_recv()
    dwu_s[...] = sum_s[0].astype(f32)
    for a in range(2):
        for b in range(4):
            for c in range(2):
                first = ((2 * a + c) * 4 + b) * wide
                piece_s[a, b, c] = sum_s[1, :, first : first + wide]
    pieces = []
    for dx in range(2):
        for dz in range(4):
            src, dst = piece_s.at[(x + dx) % 2, hop(z, dz)], here_s.at[x, z]
            k = 4 * dx + dz
            if k:
                pieces.append(
                    send(src, dst, piece_send.at[k], piece_recv.at[k], plane_device(dx, dz))
                )
            else:
                pieces.append(pltpu.make_async_copy(src, dst, local_sem.at[2]))
    for copy in pieces:
        copy.start()

    attend_back(heads, hd, 4, 0, bias_ref[0], mine_s, sib_s, None, *inputs, *scratch)
    for copy in pieces:
        copy.wait()
    swap = start(here_s.at[:, :, 1 - core], there_s, to_core)
    from_x.wait_recv()
    size = tokens - main
    gm_s[main:, pad:] = plus(gm_s[main:, pad:], back_s[0:size])
    gs_s[main:, pad:] = plus(gs_s[main:, pad:], back_s[size:])
    outs = [
        pltpu.make_async_copy(src, dst, out_sem.at[k])
        for k, (src, dst) in enumerate(
            ((gm_s, gm_out), (gs_s, gs_out), (dwu_s, dwu_out), (dwd_s, dwd_out))
        )
    ]
    for copy in outs[:3]:
        copy.start()
    swap.wait_recv()
    for a in range(2):
        turn_s[a, core] = here_s[a, :, core].astype(f32)
        turn_s[a, 1 - core] = there_s[a].astype(f32)
    dwd_s[...] = turn_s[...].reshape(16 * n, wide).T
    outs[3].start()
    for copy in sides:
        copy.wait_send()
    for _, copy in moves:
        copy.wait()
    for copy in outs:
        copy.wait()


def back(mine, sib, far, dom, doo, om, os, stat, out, dw_sum, bias, heads, hd):
    tokens, pad = om.shape
    tile = tokens // 12
    n, hidden = dw_sum.shape
    width = 16 * n
    wide = hidden // 16
    any_ref = pl.BlockSpec(memory_space=pl.ANY)
    outs = (
        shaped((tokens, 3 * pad)),
        shaped((tokens, 3 * pad)),
        shaped((12, tile, width)),
        shaped((n, hidden), f32),
        shaped((wide, width), f32),
    )
    scratch = [
        shaped(mine.shape),
        shaped(sib.shape),
        shaped(far.shape),
        shaped(om.shape),
        shaped(om.shape),
        shaped(om.shape),
        shaped(om.shape),
        shaped(stat.shape, f32),
        outs[0],
        outs[1],
        shaped(far.shape),
        shaped(far.shape),
    ]
    scratch += [shaped((16 * tile, pad))] * 4
    scratch += [shaped((pad, 16 * tile), f32)] * 2
    scratch += [shaped((16 * tile, pad), f32)] * 2
    scratch += [shaped((16 * tile, 16 * tile))] * 2
    scratch += [shaped((4, heads, 256), f32)] * 2
    scratch += [
        shaped((2, n, hidden)),
        shaped((2, 4, 2, n, wide)),
        shaped((2, 4, 2, n, wide)),
        shaped((2, 4, n, wide)),
        shaped((2, 2, 4, n, wide), f32),
        outs[4],
        outs[3],
    ]
    return pl.pallas_call(
        functools.partial(back_kernel, heads, hd),
        in_specs=[any_ref] * 10 + [SMEM],
        out_specs=(any_ref,) * len(outs),
        scratch_shapes=[pltpu.VMEM(s.shape, s.dtype) for s in scratch]
        + [pltpu.SemaphoreType.DMA((k,)) for k in (12, 12, 3, 4, 4, 8, 8, 8, 4)],
        out_shape=outs,
        compiler_params=pltpu.CompilerParams(
            vmem_limit_bytes=62 * 2**20, collective_id=3, has_side_effects=True
        ),
        cost_estimate=pl.CostEstimate(
            flops=10240 * heads * tokens * 16 * tile,
            bytes_accessed=40 * 2**20,
            transcendentals=heads * 2 * tokens * 16 * tile,
        ),
        name="back",
    )(mine, sib, far, dom, doo, om, os, stat, out.reshape(12, tile, width), dw_sum, bias)


class Sum:
    def __init__(self, a, in2, out3, keep3, in3, c4, in4, d5, in5, all6, sems):
        self.refs = a, in2, out3, keep3, in3, c4, in4, d5, in5, all6
        self.sems = sems
        row, z = lax.axis_index("row"), lax.axis_index("col")
        self.x, self.y = row // 2, lax.axis_index("img") % 2
        self.zh, self.zl = z // 2, z % 2
        _, self.to_x, self.to_img = partners()
        self.waits = []

    def go(self, *copies):
        self.waits = [
            send(src, dst, self.sems.at[0, k], self.sems.at[1, k], device)
            for k, src, dst, device in copies
        ]
        for copy in self.waits:
            copy.start()

    def settle(self):
        for copy in self.waits:
            copy.wait()

    def step2(self):
        a, in2 = self.refs[:2]
        half = a.shape[2] // 2
        self.go(
            (0, a.at[:, 1 - self.x, pl.ds(0, half)], in2.at[0], self.to_x),
            (1, a.at[1 - self.y, :, pl.ds(half, half)], in2.at[1], self.to_img),
        )

    def step3(self):
        a, in2, out3, keep3, in3 = self.refs[:5]
        x, y = self.x, self.y
        half = a.shape[2] // 2
        low, high = slice(0, half), slice(half, 2 * half)
        self.settle()
        out3[0] = a[1 - y, x, low] + in2[0, 1 - y]
        out3[1] = a[y, 1 - x, high] + in2[1, 1 - x]
        self.go((2, out3.at[0], in3.at[0], self.to_img), (3, out3.at[1], in3.at[1], self.to_x))
        keep3[0] = a[y, x, low] + in2[0, y]
        keep3[1] = a[y, x, high] + in2[1, x]

    def step4(self):
        _, _, _, keep3, in3, c4, in4 = self.refs[:7]
        n = c4.shape[2]
        self.settle()
        for h in range(2):
            term = keep3[h].astype(f32) + in3[h].astype(f32)
            for k in range(2):
                c4[h, k] = term[k * n : (k + 1) * n].astype(bf16)
        self.go((4, c4.at[:, 1 - self.zl], in4, plane_device(0, 1)))

    def step5(self):
        c4, in4, d5, in5 = self.refs[5:9]
        self.settle()
        for h in range(2):
            d5[h] = c4[h, self.zl] + in4[h]
        self.go((5, d5.at[1 - self.zh], in5, plane_device(0, 2)))

    def step6(self):
        d5, in5, all6 = self.refs[7:]
        self.settle()
        all6[self.y] = d5[self.zh] + in5[...]
        self.go((6, all6.at[self.y], all6.at[self.y], self.to_img))


def sum_scratch(count, n, wide):
    return [
        shaped((count, 2, 2, 4 * n, wide)),
        shaped((count, 2, 2, 2 * n, wide)),
        shaped((count, 2, 2 * n, wide)),
        shaped((count, 2, 2 * n, wide)),
        shaped((count, 2, 2 * n, wide)),
        shaped((count, 2, 2, n, wide)),
        shaped((count, 2, n, wide)),
        shaped((count, 2, n, wide)),
        shaped((count, n, wide)),
        shaped((count, 2, n, wide)),
    ]


def last_kernel(
    blk,
    gm_ref,
    gs_ref,
    nt_ref,
    ntsib_ref,
    wh_ref,
    x_ref,
    gmid_ref,
    dwp_ref,
    wa_ref,
    mod_ref,
    dmod_ref,
    hot_ref,
    silu_ref,
    dbu_ref,
    dbp_ref,
    dbd_ref,
    tiles_out,
    dwp_out,
    dwq_out,
    dwa_out,
    dba_out,
    dsilu_out,
    small_out,
    gm_s,
    gs_s,
    nt_s,
    ntsib_s,
    w_s,
    x_s,
    gmid_s,
    tile_s,
    gnout_s,
    gnin_s,
    in1_s,
    a_s,
    in2_s,
    out3_s,
    keep3_s,
    in3_s,
    c4_s,
    in4_s,
    d5_s,
    in5_s,
    all6_s,
    swap_s,
    dwq_s,
    place_s,
    pcore_s,
    pmid_s,
    px_s,
    psum_s,
    every_s,
    wa_s,
    dwa_s,
    dwain_s,
    dwaf_s,
    dba_s,
    dbain_s,
    dbaf_s,
    small_s,
    smallin_s,
    sum_sem,
    gn_sem,
    tile_send,
    tile_recv,
    local_sem,
    small_sem,
    p_sem,
    ada_sem,
    swap_sem,
    load_sem,
    wa_sem,
    out_sem,
):
    row = lax.axis_index("row")
    core, side = row % 2, lax.axis_index("img") % 2
    to_core, to_x, to_img = partners()
    tokens, width = x_s.shape
    tile = tokens // 12
    pad = w_s.shape[1] // 3
    part = width // 4
    ones = jnp.ones((16, tokens), bf16)

    loads = [
        pltpu.make_async_copy(src, dst, load_sem.at[k])
        for k, (src, dst) in enumerate(
            (
                (gs_ref, gs_s),
                (wh_ref.at[core], w_s),
                (gm_ref, gm_s),
                (dwp_ref.at[0], a_s.at[0]),
                (nt_ref, nt_s),
                (ntsib_ref, ntsib_s),
                (gmid_ref, gmid_s),
                (x_ref, x_s),
            )
        )
    ]
    for copy in loads:
        copy.start()
    ada = [
        pltpu.make_async_copy(
            wa_ref.at[:, pl.ds(k * width, width)], wa_s.at[i % 2], wa_sem.at[i % 2]
        )
        for i, k in enumerate((2, 3, 4, 5, 0, 1))
    ]
    for copy in ada[:2]:
        copy.start()
    greet(
        [to_core, to_img] + [plane_device(dx, dz) for dx in range(2) for dz in range(4) if dx or dz]
    )
    pending = []

    def start(src, dst, sems, k, device):
        copy = send(src, dst, sems.at[0, k], sems.at[1, k], device)
        copy.start()
        pending.append(copy)
        return copy

    sums = [
        Sum(
            *[
                ref.at[k]
                for ref in (a_s, in2_s, out3_s, keep3_s, in3_s, c4_s, in4_s, d5_s, in5_s, all6_s)
            ],
            sum_sem.at[k],
        )
        for k in range(4)
    ]
    proj = start(dwp_ref.at[1], in1_s, gn_sem, 3, to_core)

    def place(first, rows):
        for k, values in enumerate(rows):
            place_s[first + k] = functools.reduce(
                jnp.add, [hot_ref[:, i : i + 1] * values[i] for i in range(len(values))]
            ).astype(bf16)

    def p_core(k, first, count):
        at = pl.ds(first, count)
        return start(place_s.at[at], pcore_s.at[at], p_sem, k, to_core)

    def p_x(k, first, count, before):
        before.wait_recv()
        at = pl.ds(first, count)
        for c in range(first, first + count):
            pmid_s[c] = place_s[c] + pcore_s[c]
        return start(pmid_s.at[at], px_s.at[at], p_sem, k, to_x)

    def p_col(k, first, count, before):
        before.wait_recv()
        at = pl.ds(first, count)
        for c in range(first, first + count):
            psum_s[c] = pmid_s[c] + px_s[c]
            every_s[c, 0:16] = psum_s[c]
        return [
            start(
                psum_s.at[at],
                every_s.at[at, pl.ds(16 * dz, 16)],
                p_sem,
                k + dz - 1,
                plane_device(0, dz),
            )
            for dz in range(1, 4)
        ]

    def p_ada(k, first, count, before):
        for copy in before:
            copy.wait_recv()
        at = pl.ds(first, count)
        for c in range(first, first + count):
            dwaf_s[c] = dot(silu_ref[...], every_s[c], NN)
            dwa_s[c] = dwaf_s[c].astype(bf16)
            dba_s[c : c + 1] = jnp.sum(every_s[c].astype(f32), axis=0, keepdims=True)
        return start(dwa_s.at[at], dwain_s.at[at], ada_sem, k, to_img)

    def p_silu(i, first):
        ada[i].wait()
        term = dot(every_s[first], wa_s[i % 2], NT)
        if i:
            dsilu_out[...] += term
        else:
            dsilu_out[...] = term
        if i + 2 < 6:
            ada[i + 2].start()

    dba_s[...] = jnp.zeros_like(dba_s)
    place(2, [[dmod_ref[i, k : k + 1] for i in range(6)] for k in range(4)])
    early = p_core(0, 2, 4)

    loads[0].wait()
    loads[2].wait()
    total = dot(ones, gs_s[...], NN)[0:1] + dot(ones, gm_s[...], NN)[0:1]
    small_s[0] = jnp.zeros(small_s.shape[1:], f32)
    for c in range(2):
        mask = jnp.where(core == c, 1.0, 0.0)
        small_s[0, c : c + 1, 0:pad] = total[:, 0:pad] * mask
        small_s[0, c : c + 1, pad : 2 * pad] = total[:, 2 * pad :] * mask
    small_s[0, 2:3, 0:width] = dbp_ref[...]
    small_s[0, 3:4, 0:width] = dbd_ref[...]
    for k in range(4):
        small_s[0, 4 + k : 5 + k, 0:width] = dbu_ref[:, k * width : (k + 1) * width]
    route = (to_core, to_x, plane_device(0, 1), plane_device(0, 2), to_img)
    small_copies = []

    def small_step():
        k = len(small_copies)
        if k:
            small_copies[-1].wait_recv()
            small_s[k] = small_s[k - 1] + smallin_s[k - 1]
        if k < 5:
            small_copies.append(start(small_s.at[k], smallin_s.at[k], small_sem, k, route[k]))

    small_step()

    loads[1].wait()
    gn_copies = {}
    for first in (8, 0, 4):
        rows, at = slice(first * tile, (first + 4) * tile), pl.ds(first * tile, 4 * tile)
        gnout_s[rows] = dot(gs_s[rows], w_s[...], NT).astype(bf16)
        gn_copies[first] = start(gnout_s.at[at], gnin_s.at[at], gn_sem, first // 4, to_core)

    loads[3].wait()
    proj.wait_recv()
    for k in range(2):
        for h in range(2):
            a_s[0, k, h] = a_s[0, k, h] + in1_s[k, h]
    sums[0].step2()
    early = p_x(1, 2, 4, early)
    small_step()
    loads[4].wait()
    loads[5].wait()
    loads[6].wait()
    loads[7].wait()
    tile_moves_back = dict(return_moves(tile_s, tiles_out, tile_send, tile_recv, local_sem))
    late_rows = [[None] * 6, [None] * 6]

    def product(k, p):
        cols = slice(p * pad, (p + 1) * pad)
        for h in range(2):
            for c in range(2):
                rows = slice((2 * h + c) * part, (2 * h + c + 1) * part)
                term = dot(nt_s[rows], gm_s[:, cols], NN) + dot(ntsib_s[rows], gs_s[:, cols], NN)
                a_s[k, c, h] = term.astype(bf16)
        sums[k].step2()

    def first_norm(first):
        rows = slice(first * tile, (first + 4) * tile)
        gn_copies[first].wait_recv()
        both = dot(gm_s[rows], w_s[...], NT) + gnin_s[rows].astype(f32)
        for h in range(2):
            i = first // 2 + h
            rows = slice((first + 2 * h) * tile, (first + 2 * h + 2) * tile)
            y, rstd = norm(x_s[rows].astype(f32))
            gn = both[h * blk : (h + 1) * blk]
            u = gn * (1.0 + mod_ref[1, i : i + 1])
            back_term = rstd * (
                u
                - jnp.mean(u, axis=-1, keepdims=True)
                - y * jnp.mean(u * y, axis=-1, keepdims=True)
            )
            value = (gmid_s[rows].astype(f32) + back_term).astype(bf16)
            for t in range(2):
                tile_s[first + 2 * h + t] = value[t * tile : (t + 1) * tile]
            late_rows[0][i] = jnp.sum(gn, axis=0, keepdims=True)
            late_rows[1][i] = jnp.sum(gn * y, axis=0, keepdims=True)
        for t in range(first, first + 4):
            tile_moves_back[t].start()

    product(1, 2)
    first_norm(8)
    early = p_col(2, 2, 4, early)
    small_step()
    sums[0].step3()
    product(2, 1)
    first_norm(0)
    small_step()
    sums[1].step3()
    product(3, 0)
    first_norm(4)
    place(0, late_rows)
    late = p_core(5, 0, 2)
    sums[0].step4()
    small_step()
    early = p_ada(0, 2, 4, early)
    late = p_x(6, 0, 2, late)
    sums[2].step3()
    sums[1].step4()
    sums[0].step5()
    for i in range(2):
        p_silu(i, 2 + i)
    late = p_col(7, 0, 2, late)
    sums[3].step3()
    sums[2].step4()
    sums[1].step5()
    sums[0].step6()
    small_step()
    for i in range(2, 4):
        p_silu(i, 2 + i)
    late = p_ada(1, 0, 2, late)
    dba_copy = start(dba_s, dbain_s, ada_sem, 2, to_img)
    sums[3].step4()
    sums[2].step5()
    sums[1].step6()
    for i in range(4, 6):
        p_silu(i, i - 4)
    sums[3].step5()
    sums[2].step6()
    early.wait_recv()
    for c in range(2, 6):
        dwaf_s[c] = dwaf_s[c] + dwain_s[c].astype(f32)
    sums[3].step6()
    sums[0].settle()
    outs = [pltpu.make_async_copy(all6_s.at[0], dwp_out, out_sem.at[0])]
    outs[0].start()
    swaps = []
    for k in range(1, 4):
        sums[k].settle()
        swaps.append(start(all6_s.at[k, 1 - core], swap_s.at[3 - k], swap_sem, k - 1, to_core))
        dwq_s[core, 3 - k] = all6_s[k, core]
    late.wait_recv()
    dba_copy.wait_recv()
    for c in range(2):
        dwaf_s[c] = dwaf_s[c] + dwain_s[c].astype(f32)
    dbaf_s[...] = dba_s[...] + dbain_s[...]
    for copy in swaps:
        copy.wait_recv()
    for p in range(3):
        dwq_s[1 - core, p] = swap_s[p]
    for k, (src, dst) in enumerate(
        ((dwq_s, dwq_out), (dwaf_s, dwa_out), (dbaf_s, dba_out), (small_s.at[5], small_out))
    ):
        outs.append(pltpu.make_async_copy(src, dst, out_sem.at[k + 1]))
        outs[-1].start()
    for copy in pending:
        copy.wait_send()
    for copy in tile_moves_back.values():
        copy.wait()
    for copy in outs:
        copy.wait()


def last(gm, gs, nt, ntsib, w_half, x, gmid, dwp, w_ada, mod, dmod, hot, silu_t, dbu, dbp, dbd, blk):
    tokens, width = x.shape
    tile = tokens // 12
    wide = gm.shape[1]
    pad = wide // 3
    n = width // 16
    any_ref = pl.BlockSpec(memory_space=pl.ANY)
    outs = (
        shaped((12, tile, width)),
        shaped((2, n, pad)),
        shaped((2, 3, n, pad)),
        shaped((6, n, width), f32),
        shaped((8, width), f32),
        shaped((64, width), f32),
        shaped((8, 2 * pad), f32),
    )
    scratch = [
        shaped(gm.shape),
        shaped(gs.shape),
        shaped(nt.shape),
        shaped(nt.shape),
        shaped((width, wide)),
        shaped(x.shape),
        shaped(x.shape),
        outs[0],
        shaped(x.shape),
        shaped(x.shape),
        shaped(dwp.shape[1:]),
    ]
    scratch += sum_scratch(4, n, pad)
    scratch += [shaped((3, n, pad)), outs[2]]
    scratch += [shaped((6, 16, width))] * 5
    scratch += [
        shaped((6, 64, width)),
        shaped((2, width, width)),
        shaped((6, n, width)),
        shaped((6, n, width)),
        outs[3],
        outs[4],
        outs[4],
        outs[4],
        shaped((6, 8, 2 * pad), f32),
        shaped((5, 8, 2 * pad), f32),
    ]
    sems = [(4, 2, 7), (2, 4), (12,), (12,), (3,), (2, 5), (2, 10), (2, 3), (2, 3), (8,), (2,), (5,)]
    return pl.pallas_call(
        functools.partial(last_kernel, blk),
        in_specs=[any_ref] * 9 + [VMEM] * 7,
        out_specs=(any_ref,) * 5 + (VMEM, any_ref),
        scratch_shapes=[pltpu.VMEM(s.shape, s.dtype) for s in scratch]
        + [pltpu.SemaphoreType.DMA(s) for s in sems],
        out_shape=outs,
        compiler_params=pltpu.CompilerParams(
            vmem_limit_bytes=62 * 2**20, collective_id=4, has_side_effects=True
        ),
        cost_estimate=pl.CostEstimate(
            flops=8 * tokens * width * wide, bytes_accessed=60 * 2**20, transcendentals=tokens
        ),
        name="last",
    )(gm, gs, nt, ntsib, w_half, x, gmid, dwp, w_ada, mod, dmod, hot, silu_t, dbu, dbp, dbd)


def pick(values, index, axis=0):
    return lax.dynamic_index_in_dim(values, index, axis, keepdims=False)


def over_rest(v):
    size = lax.axis_size("img")
    step = 2
    while step < size:
        v = v + lax.ppermute(v, "img", [(i, i ^ step) for i in range(size)])
        step *= 2
    return v


def shards(
    tokens,
    conditioning,
    images_in_slot,
    w_qkv,
    b_qv,
    w_proj,
    b_proj,
    w_up,
    b_up,
    w_down,
    b_down,
    w_ada,
    b_ada,
    cotangent,
):
    slots, rows_tile, cols_tile, width = tokens.shape
    tile = rows_tile * cols_tile
    blk = 2 * tile
    count = slots * tile
    main = 8 * tile
    hd = width // HEADS
    heads = HEADS // 2
    half = width // 2
    pad = -(-half // 128) * 128
    hidden = w_up.shape[1]
    r, z = lax.axis_index("row"), lax.axis_index("col")
    x, core = r // 2, r % 2
    assert lax.axis_size("row") == 4 and lax.axis_size("col") == 4 and slots == 12

    four_way = images_in_slot == 4
    kinds = pick(four_way.reshape(4, 3), z)
    main_four, shared_four = pick(kinds, x), kinds[2]
    quarter = jnp.stack([2 * (x ^ dx) + ((z // 2) ^ dz) for dx in range(2) for dz in range(2)])
    picks = jnp.concatenate(
        [jnp.where(main_four, quarter, 0), jnp.where(shared_four, quarter[:2], 0)]
    )
    places = jnp.concatenate([jnp.full((4,), x, jnp.int32), jnp.full((2,), 2, jnp.int32)]) * 4 + picks
    bias = jnp.where(jnp.stack([main_four, shared_four]), -1e30, 0.0).astype(f32)
    cond = conditioning.astype(f32)
    silu = jax.nn.silu(cond).astype(bf16)
    silu_groups = silu.reshape(4, 12, width)
    chosen = jnp.take(pick(silu_groups, z), places, axis=0)
    chosen = jnp.pad(chosen, ((0, 2), (0, 0)))

    def widen(v, axis):
        return jnp.pad(v, [(0, pad - half) if a == axis else (0, 0) for a in range(v.ndim)])

    b_three = jnp.stack([b_qv[:width], jnp.zeros_like(b_qv[:width]), b_qv[width:]])
    b_half = widen(b_three.reshape(3, 2, half).astype(f32), 2).transpose(1, 0, 2)
    b_half = b_half.reshape(2, 1, 3 * pad)
    w_proj_half = widen(w_proj.reshape(2, half, width), 1)
    wp_mine, wp_other = pick(w_proj_half, core), pick(w_proj_half, 1 - core)

    (
        inputs,
        upstream,
        qkv_mine,
        qkv_sib,
        normed_t,
        normed_sib,
        far_kv,
        om,
        os,
        att_other,
        stat,
        mod,
        w_half,
    ) = forward(
        tokens.reshape(slots, tile, width),
        cotangent.reshape(slots, tile, width),
        w_qkv,
        w_ada,
        chosen,
        b_half,
        b_ada.astype(f32).reshape(6, 1, width),
        bias,
        heads,
        hd,
    )
    inputs = inputs.reshape(count, width)
    upstream = upstream.reshape(count, width)

    (
        out,
        gmid,
        do_mine,
        do_other,
        dw_sum,
        dbu,
        dwp,
        dmod_mid,
        dbp,
        dbd,
    ) = middle(
        inputs,
        upstream,
        om,
        att_other,
        mod,
        wp_mine,
        wp_other,
        b_proj.astype(f32).reshape(1, width),
        b_down.astype(f32).reshape(1, width),
        w_up,
        b_up.astype(f32).reshape(1, hidden),
        w_down,
        blk,
    )
    g_mine, g_sib, output, grad_w_up, grad_w_down = back(
        qkv_mine, qkv_sib, far_kv, do_mine, do_other, om, os, stat, out, dw_sum, bias, heads, hd
    )
    output = output.reshape(tokens.shape)
    hot = (jnp.arange(16, dtype=jnp.int32)[:, None] == places[None, :]).astype(f32)
    hot = jnp.pad(hot, ((0, 0), (0, 2)))
    rank = r * 4 + z
    n = width // 16
    silu_t = jnp.stack([pick(silu_groups, z ^ dz) for dz in range(4)])
    silu_t = lax.dynamic_slice_in_dim(silu_t, rank * n, n, 2)
    silu_t = jnp.pad(silu_t, ((0, 0), (0, 4), (0, 0))).reshape(64, n).T
    grad_x, dwp_sum, dwq_sum, dwa, dba, dsilu, small = last(
        g_mine,
        g_sib,
        normed_t,
        normed_sib,
        w_half,
        inputs,
        gmid,
        dwp,
        w_ada,
        mod,
        dmod_mid,
        hot,
        silu_t,
        dbu,
        dbp,
        dbd,
        blk,
    )
    grad_tokens = grad_x.reshape(tokens.shape).astype(f32)
    dwp_sum, dwq_sum, dwa, dba, small, grad_w_up, grad_w_down = (
        over_rest(v) for v in (dwp_sum, dwq_sum, dwa, dba, small, grad_w_up, grad_w_down)
    )
    grad_w_proj = jnp.concatenate([dwp_sum[0], dwp_sum[1, :, 2 * pad - width :]], axis=1)
    grad_w_proj = grad_w_proj.astype(f32)
    grad_w_qkv = dwq_sum[..., :half].astype(f32).transpose(2, 1, 0, 3).reshape(n, 3 * width)
    grad_w_ada = dwa.transpose(1, 0, 2).reshape(n, 6 * width)
    grad_b_ada = lax.dynamic_slice_in_dim(dba[:6].reshape(6 * width), rank * 6 * n, 6 * n, 0)
    d_s = dsilu.reshape(4, 16, width)[:, :12]
    d_s = jnp.stack([pick(d_s, z ^ g) for g in range(4)]).reshape(slots, 4, width)
    sig = jax.nn.sigmoid(cond)
    grad_conditioning = d_s * (sig * (1.0 + cond * (1.0 - sig)))
    db_qv = small[:2].reshape(2, 2, pad)[..., :half].transpose(1, 0, 2).reshape(2 * width)

    def own(values):
        size = values.shape[0] // 16
        return lax.dynamic_slice_in_dim(values, rank * size, size, 0)

    return (
        output,
        grad_tokens,
        grad_conditioning,
        grad_w_qkv,
        own(db_qv),
        grad_w_proj,
        own(small[2, :width]),
        grad_w_up,
        own(small[4:, :width].reshape(hidden)),
        grad_w_down,
        own(small[3, :width]),
        grad_w_ada,
        grad_b_ada,
    )


def solution(mesh):
    grid = P("img", "row", "col", None)
    plane = ("row", "col")
    return jax.shard_map(
        shards,
        mesh=mesh,
        in_specs=(grid, P("img", None, None), P("img")) + (P(),) * 10 + (grid,),
        out_specs=(grid, grid, P("img", None, None))
        + (P(plane, None), P(plane)) * 5,
        check_vma=False,
    )
```

```python
import functools
import math

import jax
import jax.numpy as jnp
from jax import lax
from jax.experimental import pallas as pl
from jax.experimental.pallas import tpu as pltpu
from jax.sharding import PartitionSpec as P

HEADS = 16
EPS = 1e-06
LOG2E = math.log2(math.e)
GELU_A = math.sqrt(2.0 / math.pi)
GELU_B = 0.044715
VMEM_LIMIT = 60 * 2**20

f32 = jnp.float32
bf16 = jnp.bfloat16
NT = (((1,), (1,)), ((), ()))
NN = (((1,), (0,)), ((), ()))
TN = (((0,), (0,)), ((), ()))

VMEM = pl.BlockSpec(memory_space=pltpu.VMEM)
SMEM = pl.BlockSpec(memory_space=pltpu.SMEM)


def dot(left, right, dims):
    return lax.dot_general(left, right, dims, preferred_element_type=f32)


def shaped(shape, dtype=bf16):
    return jax.ShapeDtypeStruct(shape, dtype)


def norm(values):
    center = values - jnp.mean(values, axis=-1, keepdims=True)
    rstd = lax.rsqrt(jnp.mean(center * center, axis=-1, keepdims=True) + EPS)
    return center * rstd, rstd


def plus(a, b):
    return (a.astype(f32) + b.astype(f32)).astype(bf16)


def flip(index):
    return index + 1 - 2 * (index % 2)


def partners():
    img, r, z = lax.axis_index("img"), lax.axis_index("row"), lax.axis_index("col")
    return (img, flip(r), z), (img, (r + 2) % 4, z), (flip(img), r, z)


def plane_device(dx, dz):
    img, r, z = lax.axis_index("img"), lax.axis_index("row"), lax.axis_index("col")
    return img, (r + 2 * dx) % 4, hop(z, dz)


def hop(z, dz):
    return (z, flip(z), (z + 2) % 4, 3 - z)[dz]


def signal(devices):
    barrier = pltpu.get_barrier_semaphore()
    for device in devices:
        pl.semaphore_signal(
            barrier, inc=1, device_id=device, device_id_type=pl.DeviceIdType.MESH
        )


def await_signals(devices):
    pl.semaphore_wait(pltpu.get_barrier_semaphore(), len(devices))


def greet(devices):
    signal(devices)
    await_signals(devices)


def send(src, dst, send_sem, recv_sem, device):
    return pltpu.make_async_remote_copy(
        src_ref=src,
        dst_ref=dst,
        send_sem=send_sem,
        recv_sem=recv_sem,
        device_id=device,
        device_id_type=pl.DeviceIdType.MESH,
    )


def tile_moves(src, dst, send_sem, recv_sem, local_sem):
    r, z = lax.axis_index("row"), lax.axis_index("col")
    x = r // 2
    shared, near, far, local = [], [], [], []
    for dz in range(4):
        first = 3 * hop(z, dz)
        moves = (
            (shared, 0, first + 2, 8 + dz),
            (near, 0, first + x, dz),
            (far, 1, first + 1 - x, 4 + dz),
        )
        for group, dx, slot, place_at in moves:
            if dx == 0 and dz == 0:
                sem = local_sem.at[0 if place_at else 1]
                local.append(pltpu.make_async_copy(src.at[slot], dst.at[place_at], sem))
            else:
                sems = send_sem.at[place_at], recv_sem.at[place_at]
                group.append(
                    send(src.at[slot], dst.at[place_at], *sems, plane_device(dx, dz))
                )
    return local, shared, near, far


def head_window(head, hd):
    first = head * hd
    start = pl.multiple_of((first // 128) * 128, 128)
    lane = lax.broadcasted_iota(jnp.int32, (1, 256), 1) + start
    inside = jnp.logical_and(lane >= first, lane < first + hd)
    return pl.ds(start, 256), inside


def gather_rows(dst, col, sources, base, count):
    pad = dst.shape[1]
    for i in range(count):
        for j, src in enumerate(sources):
            row = 256 * i + 128 * j
            dst[row : row + 128] = src[base + 128 * i : base + 128 * i + 128, col : col + pad]


def attend(heads, hd, count, base, bias, mine, sib, far, o_mine, o_sib, stat, q_s, k_s, v_s, o_s):
    pad = q_s.shape[1]
    scale = LOG2E / math.sqrt(hd)
    gather_rows(q_s, 0, (mine, sib), base, count)
    gather_rows(k_s, pad, (mine, sib), base, count)
    gather_rows(v_s, 2 * pad, (mine, sib), base, count)
    if far is not None:
        k_s[256 * count :] = far[:, 0:pad]
        v_s[256 * count :] = far[:, pad : 2 * pad]
    blocks = k_s.shape[0] // 256
    lane = lax.broadcasted_iota(jnp.int32, (1, 128), 1)

    def body(head, carry):
        win, inside = head_window(head, hd)
        for i in range(count):
            rows = slice(256 * i, 256 * i + 256)
            q = jnp.where(inside, q_s[rows, win], jnp.zeros((), bf16))
            s = dot(q, k_s[:, win], NT)
            cols = [s[:, 256 * j : 256 * j + 256] for j in range(blocks)]
            best = [jnp.max(col, axis=1, keepdims=True) for col in cols]
            own = best[i]
            rest = best[:i] + best[i + 1 :]
            top = jnp.maximum(own, functools.reduce(jnp.maximum, rest) + bias)
            near = -scale * top
            away = near + bias
            cols = [
                jnp.exp2(col * scale + (near if j == i else away)) for j, col in enumerate(cols)
            ]
            total = functools.reduce(
                jnp.add, [jnp.sum(col, axis=1, keepdims=True) for col in cols]
            )
            p = jnp.concatenate([col.astype(bf16) for col in cols], axis=1)
            o = dot(p, v_s[:, win], NN) / total
            o_s[rows, win] = jnp.where(inside, o.astype(bf16), o_s[rows, win])
            at = slice(2 * base + 256 * i, 2 * base + 256 * i + 256)
            stat[at] = jnp.where(lane == head, top * scale + jnp.log2(total), stat[at])
        return carry

    lax.fori_loop(0, heads, body, 0)
    for i in range(count):
        at = slice(base + 128 * i, base + 128 * i + 128)
        o_mine[at] = o_s[256 * i : 256 * i + 128]
        o_sib[at] = o_s[256 * i + 128 : 256 * i + 256]


def forward_kernel(
    heads,
    hd,
    tok_ref,
    cot_ref,
    wq_ref,
    wa_ref,
    chosen_ref,
    bh_ref,
    ba_ref,
    bias_ref,
    x_out,
    cot_out,
    mine_out,
    sib_out,
    nt_out,
    ntsib_out,
    far_out,
    om_out,
    os_out,
    ao_out,
    stat_out,
    mod_out,
    wh_out,
    x_s,
    raw_s,
    w_s,
    wa_s,
    mod_s,
    nt_s,
    ntsib_s,
    other_s,
    mine_s,
    sib_s,
    far_s,
    q_s,
    k_s,
    v_s,
    o_s,
    om_s,
    os_s,
    ao_s,
    stat_s,
    tok_send,
    tok_recv,
    cot_send,
    cot_recv,
    local_sem,
    raw_sem,
    wa_sem,
    side_send,
    side_recv,
    out_sem,
):
    tile, width = x_s.shape[1:]
    tokens = 12 * tile
    main = 8 * tile
    half = width // 2
    pad = w_s.shape[2] // 3
    rows_step = raw_s.shape[1]
    core = lax.axis_index("row") % 2
    to_core, to_x, _ = partners()

    raw = [
        pltpu.make_async_copy(
            wq_ref.at[pl.ds(i * rows_step, rows_step)], raw_s.at[i % 2], raw_sem.at[i % 2]
        )
        for i in range(width // rows_step)
    ]
    ada = [
        pltpu.make_async_copy(
            wa_ref.at[:, pl.ds(i * width, width)], wa_s.at[i % 2], wa_sem.at[i % 2]
        )
        for i in range(6)
    ]
    for copy in raw[:2] + ada[:2]:
        copy.start()
    greet([to_core] + [plane_device(dx, dz) for dx in range(2) for dz in range(4) if dx or dz])
    local, shared, near, far = tile_moves(tok_ref, x_s, tok_send, tok_recv, local_sem)
    for copy in local + shared + near + far:
        copy.start()

    w_s[...] = jnp.zeros_like(w_s)
    for i, copy in enumerate(raw):
        copy.wait()
        rows = slice(i * rows_step, (i + 1) * rows_step)
        for h in range(2):
            for p in range(3):
                start = half * (2 * p + h)
                w_s[h, rows, p * pad : p * pad + half] = raw_s[i % 2, :, start : start + half]
        if i + 2 < len(raw):
            raw[i + 2].start()
    for i, copy in enumerate(ada):
        copy.wait()
        bias = ba_ref[i * width : (i + 1) * width].astype(f32).reshape(1, width)
        mod_s[i] = dot(chosen_ref[...], wa_s[i % 2], NN) + bias
        if i + 2 < len(ada):
            ada[i + 2].start()
    outs = []

    def put(src, dst):
        copy = pltpu.make_async_copy(src, dst, out_sem.at[len(outs)])
        copy.start()
        outs.append(copy)

    put(w_s, wh_out)
    put(mod_s, mod_out)

    sides = []

    def side(src, dst, device):
        k = len(sides)
        copy = send(src, dst, side_send.at[k], side_recv.at[k], device)
        copy.start()
        sides.append(copy)
        return copy

    moves = None
    from_core = []
    for first, waits in ((8, local[:1] + shared), (0, local[1:] + near), (4, far)):
        for copy in waits:
            copy.wait()
        if first == 4:
            moves = tile_moves(cot_ref, cot_out, cot_send, cot_recv, local_sem)
            for group in moves:
                for copy in group:
                    copy.start()
        parts = []
        for i in range(2):
            at = first // 2 + i
            values = x_s[first + 2 * i : first + 2 * i + 2].reshape(2 * tile, width)
            normed, _ = norm(values.astype(f32))
            parts.append((normed * (1.0 + mod_s[1, at : at + 1]) + mod_s[0, at : at + 1]).astype(bf16))
        normed = jnp.concatenate(parts, axis=0)
        rows = slice(first * tile, (first + 4) * tile)
        other_s[rows] = (dot(normed, w_s[1 - core], NN) + bh_ref[1 - core]).astype(bf16)
        at = pl.ds(first * tile, 4 * tile)
        from_core.append(side(other_s.at[at], sib_s.at[at], to_core))
        mine_s[rows] = (dot(normed, w_s[core], NN) + bh_ref[core]).astype(bf16)
        nt_s[:, rows] = normed.T
        if first == 0:
            from_core[0].wait_recv()
            at, cols = pl.ds(main, tokens - main), pl.ds(pad, 2 * pad)
            size = tokens - main
            from_x = [
                side(src.at[at, cols], far_s.at[pl.ds(size * k, size)], to_x)
                for k, src in enumerate((mine_s, sib_s))
            ]
    put(x_s, x_out)
    put(mine_s, mine_out)
    put(nt_s, nt_out)
    nt_copy = side(nt_s, ntsib_s, to_core)

    o_s[...] = jnp.zeros_like(o_s)
    stat_s[...] = jnp.zeros_like(stat_s)
    for copy in from_core[1:]:
        copy.wait_recv()
    put(sib_s, sib_out)
    scratch = (om_s, os_s, stat_s, q_s, k_s, v_s, o_s)
    attend(heads, hd, 4, 0, bias_ref[0], mine_s, sib_s, None, *scratch)
    back = [side(os_s.at[pl.ds(0, main)], ao_s.at[pl.ds(0, main)], to_core)]
    for copy in from_x:
        copy.wait_recv()
    put(far_s, far_out)
    attend(heads, hd, 2, main, bias_ref[1], mine_s, sib_s, far_s, *scratch)
    at = pl.ds(main, tokens - main)
    back.append(side(os_s.at[at], ao_s.at[at], to_core))
    put(om_s, om_out)
    put(os_s, os_out)
    put(stat_s, stat_out)
    nt_copy.wait_recv()
    put(ntsib_s, ntsib_out)
    for copy in back:
        copy.wait_recv()
    put(ao_s, ao_out)
    for copy in sides:
        copy.wait_send()
    for group in moves:
        for copy in group:
            copy.wait()
    for copy in outs:
        copy.wait()


def forward(tok, cot, w_qkv, w_ada, chosen, b_half, b_ada, bias, heads, hd):
    _, tile, width = tok.shape
    tokens = 12 * tile
    pad = b_half.shape[2] // 3
    any_ref = pl.BlockSpec(memory_space=pl.ANY)
    outs = (
        shaped((12, tile, width)),
        shaped((12, tile, width)),
        shaped((tokens, 3 * pad)),
        shaped((tokens, 3 * pad)),
        shaped((width, tokens)),
        shaped((width, tokens)),
        shaped((8 * tile, 2 * pad)),
        shaped((tokens, pad)),
        shaped((tokens, pad)),
        shaped((tokens, pad)),
        shaped((2 * tokens, 128), f32),
        shaped((6, 8, width), f32),
        shaped((2, width, 3 * pad)),
    )
    scratch = [
        outs[0],
        shaped((2, width // 4, 3 * width)),
        outs[12],
        shaped((2, width, width)),
        outs[11],
        outs[4],
        outs[4],
        outs[2],
        outs[2],
        outs[2],
        outs[6],
        shaped((16 * tile, pad)),
        shaped((16 * tile, pad)),
        shaped((16 * tile, pad)),
        shaped((16 * tile, pad)),
        outs[7],
        outs[7],
        outs[7],
        outs[10],
    ]
    return pl.pallas_call(
        functools.partial(forward_kernel, heads, hd),
        in_specs=[any_ref] * 4 + [VMEM] * 3 + [SMEM],
        out_specs=(any_ref,) * len(outs),
        scratch_shapes=[pltpu.VMEM(s.shape, s.dtype) for s in scratch]
        + [pltpu.SemaphoreType.DMA((k,)) for k in (12, 12, 12, 12, 2, 2, 2, 10, 10, 12)],
        out_shape=outs,
        compiler_params=pltpu.CompilerParams(
            vmem_limit_bytes=62 * 2**20, collective_id=2, has_side_effects=True
        ),
        cost_estimate=pl.CostEstimate(
            flops=4 * tokens * width * 3 * pad + 4096 * heads * tokens * 16 * tile,
            bytes_accessed=70 * 2**20,
            transcendentals=heads * 2 * tokens * 16 * tile,
        ),
        name="forward",
    )(tok, cot, w_qkv, w_ada, chosen, b_half, b_ada, bias)


def middle_kernel(
    blk,
    chunks,
    x_ref,
    cot_ref,
    am_ref,
    ao_ref,
    mod_ref,
    wp_ref,
    bp_ref,
    bd_ref,
    wu_ref,
    bu_ref,
    wd_ref,
    out_ref,
    gmid_ref,
    dom_ref,
    doo_ref,
    sum_ref,
    dbu_ref,
    dwp_ref,
    dmod_ref,
    dbp_ref,
    dbd_ref,
    mid_s,
    br1_s,
    n_s,
    nt_s,
    db2_s,
    db2t_s,
    br2_s,
    gn_s,
    db1_s,
    mine_s,
    other_s,
    in1_s,
    in2_s,
    out3_s,
    keep3_s,
    in3_s,
    sum4_s,
    in4_s,
    sum5_s,
    in5_s,
    sems,
    done,
    wpm_ref,
    wpo_ref,
):
    step = pl.program_id(0)
    tokens, width = x_ref.shape
    pad = am_ref.shape[1]
    blocks = tokens // blk
    part = width // 4
    row = lax.axis_index("row")
    x, core, y = row // 2, row % 2, lax.axis_index("img") % 2
    z = lax.axis_index("col")
    zh, zl = z // 2, z % 2
    to_core, to_x, to_img = partners()
    to_near, to_far = plane_device(0, 1), plane_device(0, 2)
    neighbours = to_core, to_x, to_img, to_near, to_far
    halves = [
        pltpu.make_async_copy(
            wp_ref.at[pl.ds(pl.multiple_of(2 * part * c, 16), 2 * part)],
            dst.at[pl.ds(0, 2 * part)],
            done.at[k],
        )
        for k, (c, dst) in enumerate(((core, wpm_ref), (1 - core, wpo_ref)))
    ]

    half = mine_s.shape[3] // 2
    low, high = slice(0, half), slice(half, 2 * half)

    def copy(k, a, src, dst, device):
        return send(src, dst, sems.at[0, k, a % 4], sems.at[1, k, a % 4], device)

    def stage1(a):
        return [copy(0, a, other_s.at[a % 2], in1_s.at[a % 2], to_core)]

    def stage2(a):
        t = a % 4
        return [
            copy(1, a, mine_s.at[t, :, 1 - x, pl.ds(0, half)], in2_s.at[t, 0], to_x),
            copy(2, a, mine_s.at[t, 1 - y, :, pl.ds(half, half)], in2_s.at[t, 1], to_img),
        ]

    def stage3(a):
        return [
            copy(3 + h, a, out3_s.at[a % 2, h], in3_s.at[a % 4, h], (to_img, to_x)[h])
            for h in range(2)
        ]

    def stage4(a):
        return [copy(5, a, sum4_s.at[:, 1 - zl], in4_s.at[a % 2], to_near)]

    def stage5(a):
        return [copy(6, a, sum5_s.at[1 - zh], in5_s.at[a % 2], to_far)]

    def when(lag):
        return pl.when(jnp.logical_and(step >= lag, step < chunks + lag))

    def go(copies):
        for c in copies:
            c.start()

    def settle(copies):
        for c in copies:
            c.wait()

    @pl.when(step == 0)
    def _():
        signal(neighbours)
        for c in halves:
            c.start()
        pad_rows = jnp.zeros((pad - 2 * part, width), bf16)
        wpm_ref[2 * part :] = pad_rows
        wpo_ref[2 * part :] = pad_rows
        for c in halves:
            c.wait()
        br1_s[...] = (
            dot(am_ref[...], wpm_ref[...], NN) + dot(ao_ref[...], wpo_ref[...], NN) + bp_ref[...].astype(f32).reshape(1, width)
        ).astype(bf16)
        for i in range(blocks):
            rows = slice(i * blk, (i + 1) * blk)
            mid = x_ref[rows].astype(f32) + mod_ref[2, i : i + 1] * br1_s[rows].astype(f32)
            mid_s[rows] = mid
            normed, _ = norm(mid)
            n_s[rows] = (normed * (1.0 + mod_ref[4, i : i + 1]) + mod_ref[3, i : i + 1]).astype(bf16)
            db2_s[rows] = (mod_ref[5, i : i + 1] * cot_ref[rows].astype(f32)).astype(bf16)
        for b in range(width // 128):
            for src, dst in ((n_s, nt_s), (db2_s, db2t_s)):
                turned = src[:, 128 * b : 128 * b + 128].T
                for q in range(4):
                    first = 128 * b + 32 * q
                    g = first // part
                    to = ((g + core) % 2) * (2 * part) + (g // 2) * part + first % part
                    dst[pl.ds(pl.multiple_of(to, 16), 32)] = turned[32 * q : 32 * q + 32]
        br2_s[...] = jnp.zeros_like(br2_s)
        gn_s[...] = jnp.zeros_like(gn_s)

    @pl.when(step < chunks)
    def _():
        pre = dot(n_s[...], wu_ref[...], NN) + bu_ref[...].astype(f32).reshape(1, -1)
        square = pre * pre
        t = jnp.tanh(pre * (GELU_A + (GELU_A * GELU_B) * square))
        hidden = (0.5 * pre * (1.0 + t)).astype(bf16)
        slope = 0.5 * (1.0 + t) + 0.5 * pre * (1.0 - t * t) * (
            GELU_A + (3.0 * GELU_A * GELU_B) * square
        )
        gpre = dot(db2_s[...], wd_ref[...], NT) * slope
        gp = gpre.astype(bf16)
        for k, (left, right) in enumerate(((nt_s, gp), (db2t_s, hidden))):
            for own, dst in enumerate((mine_s.at[step % 4, k], other_s.at[step % 2, k])):
                for h in range(2):
                    rows = slice((2 * own + h) * part, (2 * own + h + 1) * part)
                    dst[h] = dot(left[rows], right, NN).astype(bf16)

        @pl.when(step == 0)
        def _():
            await_signals(neighbours)

        go(stage1(step))
        br2_s[...] += dot(hidden, wd_ref[...], NN)
        gn_s[...] += dot(gp, wu_ref[...], NT)
        dbu_ref[...] = jnp.sum(gpre, axis=0, keepdims=True)

    @when(6)
    def _():
        a = step - 6
        settle(stage5(a))
        sum_ref[...] = sum5_s[zh] + in5_s[a % 2]

    @when(5)
    def _():
        a = step - 5
        settle(stage4(a))
        for h in range(2):
            sum5_s[h] = sum4_s[h, zl] + in4_s[a % 2, h]
        go(stage5(a))

    @when(4)
    def _():
        a = step - 4
        settle(stage3(a))
        for h in range(2):
            term = keep3_s[a % 2, h].astype(f32) + in3_s[a % 4, h].astype(f32)
            for k in range(2):
                sum4_s[h, k] = term[k * half // 2 : (k + 1) * half // 2].astype(bf16)
        go(stage4(a))

    @when(2)
    def _():
        a = step - 2
        s, t = a % 2, a % 4
        settle(stage2(a))
        out3_s[s, 0] = mine_s[t, 1 - y, x, low] + in2_s[t, 0, 1 - y]
        out3_s[s, 1] = mine_s[t, y, 1 - x, high] + in2_s[t, 1, 1 - x]
        go(stage3(a))
        keep3_s[s, 0] = mine_s[t, y, x, low] + in2_s[t, 0, y]
        keep3_s[s, 1] = mine_s[t, y, x, high] + in2_s[t, 1, x]

    @when(0)
    def _():
        a = step - 0
        settle(stage1(a))
        for k in range(2):
            for h in range(2):
                mine_s[a % 4, k, h] = mine_s[a % 4, k, h] + in1_s[a % 2, k, h]
        go(stage2(a))

    outs = [
        pltpu.make_async_copy(n_s, out_ref, done.at[0]),
        pltpu.make_async_copy(db2_s, gmid_ref, done.at[1]),
    ]

    def finish(i):
        rows = slice(i * blk, (i + 1) * blk)
        cot = cot_ref[rows].astype(f32)
        br2 = br2_s[rows] + bd_ref[...].astype(f32).reshape(1, width)
        mid = mid_s[rows]
        n_s[rows] = (mid + mod_ref[5, i : i + 1] * br2).astype(bf16)
        normed, rstd = norm(mid)
        gn = gn_s[rows]
        u = gn * (1.0 + mod_ref[4, i : i + 1])
        gmid = cot + rstd * (
            u
            - jnp.mean(u, axis=-1, keepdims=True)
            - normed * jnp.mean(u * normed, axis=-1, keepdims=True)
        )
        db1 = mod_ref[2, i : i + 1] * gmid
        db1_s[rows] = db1.astype(bf16)
        dbp = jnp.sum(db1, axis=0, keepdims=True)
        dbd = jnp.sum(db2_s[rows].astype(f32), axis=0, keepdims=True)
        dbp_ref[...] = dbp if i == 0 else dbp_ref[...] + dbp
        dbd_ref[...] = dbd if i == 0 else dbd_ref[...] + dbd
        db2_s[rows] = gmid.astype(bf16)
        dmod_ref[i, 0:1] = jnp.sum(gmid * br1_s[rows].astype(f32), axis=0, keepdims=True)
        dmod_ref[i, 1:2] = jnp.sum(gn, axis=0, keepdims=True)
        dmod_ref[i, 2:3] = jnp.sum(gn * normed, axis=0, keepdims=True)
        dmod_ref[i, 3:4] = jnp.sum(cot * br2, axis=0, keepdims=True)

    for k in range(3):

        @pl.when(step == chunks + k)
        def _(k=k):
            finish(2 * k)
            finish(2 * k + 1)

    @pl.when(step == chunks + 3)
    def _():
        for c in outs:
            c.start()
        dom_ref[...] = dot(db1_s[...], wpm_ref[...], NT).astype(bf16)
        doo_ref[...] = dot(db1_s[...], wpo_ref[...], NT).astype(bf16)

    @pl.when(step == chunks + 4)
    def _():
        for side, ref in ((core, am_ref), (1 - core, ao_ref)):
            term = dot(ref[...], db1_s[...], TN)
            for c in range(2):
                rows = term[part * c : part * (c + 1)]
                for k, at in enumerate((0, width - pad)):
                    dwp_ref[(c + core) % 2, k, side] = rows[:, at : at + pad].astype(bf16)
        settle(outs)


def middle(x, cot, att_m, att_o, mod, w_proj, b_proj, b_down, w_up, b_up, w_down, blk):
    tokens, width = x.shape
    pad = att_m.shape[1]
    hidden = w_up.shape[1]
    chunk = 512
    chunks = hidden // chunk
    n = width // 16
    any_ref = pl.BlockSpec(memory_space=pl.ANY)

    def at(j):
        return jnp.minimum(j, chunks - 1)

    return pl.pallas_call(
        functools.partial(middle_kernel, blk, chunks),
        grid=(chunks + 6,),
        in_specs=[VMEM] * 5
        + [any_ref, VMEM, VMEM]
        + [
            pl.BlockSpec((width, chunk), lambda j: (0, at(j))),
            pl.BlockSpec((chunk,), lambda j: (at(j),)),
            pl.BlockSpec((chunk, width), lambda j: (at(j), 0)),
        ],
        out_specs=[any_ref, any_ref, VMEM, VMEM]
        + [
            pl.BlockSpec((n, chunk), lambda j: (0, jnp.maximum(j - 6, 0))),
            pl.BlockSpec((1, chunk), lambda j: (0, at(j))),
        ]
        + [VMEM] * 4,
        scratch_shapes=[
            pltpu.VMEM((tokens, width), f32),
            pltpu.VMEM((tokens, width), bf16),
            pltpu.VMEM((tokens, width), bf16),
            pltpu.VMEM((width, tokens), bf16),
            pltpu.VMEM((tokens, width), bf16),
            pltpu.VMEM((width, tokens), bf16),
            pltpu.VMEM((tokens, width), f32),
            pltpu.VMEM((tokens, width), f32),
            pltpu.VMEM((tokens, width), bf16),
            pltpu.VMEM((4, 2, 2, 4 * n, chunk), bf16),
            pltpu.VMEM((2, 2, 2, 4 * n, chunk), bf16),
            pltpu.VMEM((2, 2, 2, 4 * n, chunk), bf16),
            pltpu.VMEM((4, 2, 2, 2 * n, chunk), bf16),
            pltpu.VMEM((2, 2, 2 * n, chunk), bf16),
            pltpu.VMEM((2, 2, 2 * n, chunk), bf16),
            pltpu.VMEM((4, 2, 2 * n, chunk), bf16),
            pltpu.VMEM((2, 2, n, chunk), bf16),
            pltpu.VMEM((2, 2, n, chunk), bf16),
            pltpu.VMEM((2, n, chunk), bf16),
            pltpu.VMEM((2, n, chunk), bf16),
            pltpu.SemaphoreType.DMA((2, 7, 4)),
            pltpu.SemaphoreType.DMA((2,)),
            pltpu.VMEM((pad, width), bf16),
            pltpu.VMEM((pad, width), bf16),
        ],
        out_shape=(
            shaped((tokens, width)),
            shaped((tokens, width)),
            shaped((tokens, pad)),
            shaped((tokens, pad)),
            shaped((n, hidden)),
            shaped((1, hidden), f32),
            shaped((2, 2, 2, 4 * n, pad)),
            shaped((tokens // blk, 4, width), f32),
            shaped((1, width), f32),
            shaped((1, width), f32),
        ),
        compiler_params=pltpu.CompilerParams(
            vmem_limit_bytes=62 * 2**20, collective_id=1, has_side_effects=True
        ),
        cost_estimate=pl.CostEstimate(
            flops=2 * tokens * width * (6 * hidden + 6 * pad),
            bytes_accessed=60 * 2**20,
            transcendentals=tokens * hidden,
        ),
        name="middle",
    )(x, cot, att_m, att_o, mod, w_proj, b_proj, b_down, w_up, b_up, w_down)


def attend_back(heads, hd, count, base, bias, mine, sib, far, d_mine, d_sib, o_mine, o_sib, stat,
                g_mine, g_sib, g_far, q_s, k_s, v_s, do_s, kt_s, dqt_s, dk_s, dv_s, p_s, ds_s,
                lse_s, dd_s):
    pad = q_s.shape[1]
    inv = 1.0 / math.sqrt(hd)
    scale = LOG2E * inv
    pair = (mine, sib)
    gather_rows(q_s, 0, pair, base, count)
    gather_rows(k_s, pad, pair, base, count)
    gather_rows(v_s, 2 * pad, pair, base, count)
    gather_rows(do_s, 0, (d_mine, d_sib), base, count)
    if far is not None:
        k_s[256 * count :] = far[:, 0:pad]
        v_s[256 * count :] = far[:, pad : 2 * pad]
    kt_s[...] = k_s[...].astype(f32).T
    dqt_s[...] = jnp.zeros_like(dqt_s)
    dk_s[...] = jnp.zeros_like(dk_s)
    dv_s[...] = jnp.zeros_like(dv_s)
    blocks = k_s.shape[0] // 256
    used = 256 * count
    row = lax.broadcasted_iota(jnp.int32, (heads, pad), 0)
    col = lax.broadcasted_iota(jnp.int32, (heads, pad), 1)
    member = jnp.where(jnp.logical_and(col >= row * hd, col < row * hd + hd), 1.0, 0.0).astype(bf16)
    for i in range(count):
        rows = slice(256 * i, 256 * i + 256)
        at = 2 * base + 256 * i
        lse_s[i] = stat[at : at + 256].T[0:heads]
        o = jnp.concatenate(
            [ref[base + 128 * i : base + 128 * i + 128] for ref in (o_mine, o_sib)], axis=0
        )
        both = do_s[rows].astype(f32) * o.astype(f32)
        high = both.astype(bf16)
        low = (both - high.astype(f32)).astype(bf16)
        dd_s[i] = dot(member, high, NT) + dot(member, low, NT)

    def body(head, carry):
        win, inside = head_window(head, hd)
        own = pl.ds(pl.multiple_of(head * hd, 8), hd)
        zero = jnp.zeros((), bf16)
        for i in range(count):
            rows = slice(256 * i, 256 * i + 256)
            q = jnp.where(inside, q_s[rows, win], zero)
            do = jnp.where(inside, do_s[rows, win], zero)
            near = -lse_s[i, pl.ds(head, 1)]
            away = near + bias
            dd = dd_s[i, pl.ds(head, 1)]
            s = dot(k_s[:, win], q, NT)
            dp = dot(v_s[:, win], do, NT)
            for j in range(blocks):
                keys = slice(256 * j, 256 * j + 256)
                p = jnp.exp2(s[keys] * scale + (near if j == i else away))
                ds_s[keys, rows] = (p * (dp[keys] - dd)).astype(bf16)
                p_s[keys, rows] = p.astype(bf16)
        q = jnp.where(inside, q_s[0:used, win], zero)
        do = jnp.where(inside, do_s[0:used, win], zero)
        dv_s[:, win] += dot(p_s[:, 0:used], do, NN)
        dk_s[:, win] += dot(ds_s[:, 0:used], q, NN)
        dqt_s[own, 0:used] = dot(kt_s[own, :].astype(bf16), ds_s[:, 0:used], NN)
        return carry

    lax.fori_loop(0, heads, body, 0)
    for i in range(count):
        for j, dst in enumerate((g_mine, g_sib)):
            rows = slice(256 * i + 128 * j, 256 * i + 128 * j + 128)
            out = slice(base + 128 * i, base + 128 * i + 128)
            dst[out, 0:pad] = (dqt_s[:, rows] * inv).T.astype(bf16)
            dst[out, pad : 2 * pad] = (dk_s[rows] * inv).astype(bf16)
            dst[out, 2 * pad : 3 * pad] = dv_s[rows].astype(bf16)
    if far is not None:
        g_far[:, 0:pad] = (dk_s[used:] * inv).astype(bf16)
        g_far[:, pad : 2 * pad] = dv_s[used:].astype(bf16)


def return_moves(src, dst, send_sem, recv_sem, local_sem):
    r, z = lax.axis_index("row"), lax.axis_index("col")
    local, near, far, shared = [], [], [], []
    for dz in range(4):
        for group, dx, slot, at in (
            (near, 0, 3 * z + r // 2, dz),
            (far, 1, 3 * z + r // 2, 4 + dz),
            (shared, 0, 3 * z + 2, 8 + dz),
        ):
            if dx == 0 and dz == 0:
                sem = local_sem.at[0 if at else 1]
                local.append((at, pltpu.make_async_copy(src.at[at], dst.at[slot], sem)))
            else:
                sems = send_sem.at[at], recv_sem.at[at]
                copy = send(src.at[at], dst.at[slot], *sems, plane_device(dx, dz))
                group.append((at, copy))
    return local + near + far + shared


def back_kernel(
    heads,
    hd,
    mine_ref,
    sib_ref,
    far_ref,
    dom_ref,
    doo_ref,
    om_ref,
    os_ref,
    stat_ref,
    out_ref,
    sum_ref,
    bias_ref,
    gm_out,
    gs_out,
    tiles_out,
    dwu_out,
    dwd_out,
    mine_s,
    sib_s,
    far_s,
    dom_s,
    dos_s,
    om_s,
    os_s,
    stat_s,
    gm_s,
    gs_s,
    gfar_s,
    back_s,
    q_s,
    k_s,
    v_s,
    do_s,
    kt_s,
    dqt_s,
    dk_s,
    dv_s,
    p_s,
    ds_s,
    lse_s,
    dd_s,
    sum_s,
    piece_s,
    here_s,
    there_s,
    turn_s,
    dwd_s,
    dwu_s,
    tile_send,
    tile_recv,
    local_sem,
    side_send,
    side_recv,
    piece_send,
    piece_recv,
    load_sem,
    out_sem,
):
    row, z = lax.axis_index("row"), lax.axis_index("col")
    x, core, side = row // 2, row % 2, lax.axis_index("img") % 2
    to_core, to_x, to_img = partners()
    tokens = mine_s.shape[0]
    pad = om_s.shape[1]
    main = 2 * tokens // 3
    n = sum_s.shape[1]
    wide = piece_s.shape[4]

    loads = []

    def load(src, dst):
        copy = pltpu.make_async_copy(src, dst, load_sem.at[len(loads)])
        copy.start()
        loads.append(copy)

    sides = []

    def start(src, dst, device):
        k = len(sides)
        copy = send(src, dst, side_send.at[k], side_recv.at[k], device)
        copy.start()
        sides.append(copy)
        return copy

    for src, dst in (
        (mine_ref, mine_s),
        (sib_ref, sib_s),
        (far_ref, far_s),
        (dom_ref, dom_s),
        (om_ref, om_s),
        (os_ref, os_s),
        (stat_ref, stat_s),
    ):
        load(src, dst)
    load(sum_ref, sum_s.at[side])
    greet(
        [to_core, to_img] + [plane_device(dx, dz) for dx in range(2) for dz in range(4) if dx or dz]
    )
    from_core = start(doo_ref, dos_s, to_core)
    from_img = start(sum_ref, sum_s.at[side], to_img)
    moves = return_moves(out_ref, tiles_out, tile_send, tile_recv, local_sem)
    for _, copy in moves:
        copy.start()
    for copy in loads:
        copy.wait()
    from_core.wait_recv()
    scratch = (q_s, k_s, v_s, do_s, kt_s, dqt_s, dk_s, dv_s, p_s, ds_s, lse_s, dd_s)
    inputs = (dom_s, dos_s, om_s, os_s, stat_s, gm_s, gs_s, gfar_s)
    attend_back(heads, hd, 2, main, bias_ref[1], mine_s, sib_s, far_s, *inputs, *scratch)
    from_x = start(gfar_s, back_s, to_x)

    from_img.wait_recv()
    dwu_s[...] = sum_s[0].astype(f32)
    for a in range(2):
        for b in range(4):
            for c in range(2):
                first = ((2 * a + c) * 4 + b) * wide
                piece_s[a, b, c] = sum_s[1, :, first : first + wide]
    pieces = []
    for dx in range(2):
        for dz in range(4):
            src, dst = piece_s.at[(x + dx) % 2, hop(z, dz)], here_s.at[x, z]
            k = 4 * dx + dz
            if k:
                pieces.append(
                    send(src, dst, piece_send.at[k], piece_recv.at[k], plane_device(dx, dz))
                )
            else:
                pieces.append(pltpu.make_async_copy(src, dst, local_sem.at[2]))
    for copy in pieces:
        copy.start()

    attend_back(heads, hd, 4, 0, bias_ref[0], mine_s, sib_s, None, *inputs, *scratch)
    for copy in pieces:
        copy.wait()
    swap = start(here_s.at[:, :, 1 - core], there_s, to_core)
    from_x.wait_recv()
    size = tokens - main
    gm_s[main:, pad:] = plus(gm_s[main:, pad:], back_s[0:size])
    gs_s[main:, pad:] = plus(gs_s[main:, pad:], back_s[size:])
    outs = [
        pltpu.make_async_copy(src, dst, out_sem.at[k])
        for k, (src, dst) in enumerate(
            ((gm_s, gm_out), (gs_s, gs_out), (dwu_s, dwu_out), (dwd_s, dwd_out))
        )
    ]
    for copy in outs[:3]:
        copy.start()
    swap.wait_recv()
    for a in range(2):
        turn_s[a, core] = here_s[a, :, core].astype(f32)
        turn_s[a, 1 - core] = there_s[a].astype(f32)
    dwd_s[...] = turn_s[...].reshape(16 * n, wide).T
    outs[3].start()
    for copy in sides:
        copy.wait_send()
    for _, copy in moves:
        copy.wait()
    for copy in outs:
        copy.wait()


def back(mine, sib, far, dom, doo, om, os, stat, out, dw_sum, bias, heads, hd):
    tokens, pad = om.shape
    tile = tokens // 12
    n, hidden = dw_sum.shape
    width = 16 * n
    wide = hidden // 16
    any_ref = pl.BlockSpec(memory_space=pl.ANY)
    outs = (
        shaped((tokens, 3 * pad)),
        shaped((tokens, 3 * pad)),
        shaped((12, tile, width)),
        shaped((n, hidden), f32),
        shaped((wide, width), f32),
    )
    scratch = [
        shaped(mine.shape),
        shaped(sib.shape),
        shaped(far.shape),
        shaped(om.shape),
        shaped(om.shape),
        shaped(om.shape),
        shaped(om.shape),
        shaped(stat.shape, f32),
        outs[0],
        outs[1],
        shaped(far.shape),
        shaped(far.shape),
    ]
    scratch += [shaped((16 * tile, pad))] * 4
    scratch += [shaped((pad, 16 * tile), f32)] * 2
    scratch += [shaped((16 * tile, pad), f32)] * 2
    scratch += [shaped((16 * tile, 16 * tile))] * 2
    scratch += [shaped((4, heads, 256), f32)] * 2
    scratch += [
        shaped((2, n, hidden)),
        shaped((2, 4, 2, n, wide)),
        shaped((2, 4, 2, n, wide)),
        shaped((2, 4, n, wide)),
        shaped((2, 2, 4, n, wide), f32),
        outs[4],
        outs[3],
    ]
    return pl.pallas_call(
        functools.partial(back_kernel, heads, hd),
        in_specs=[any_ref] * 10 + [SMEM],
        out_specs=(any_ref,) * len(outs),
        scratch_shapes=[pltpu.VMEM(s.shape, s.dtype) for s in scratch]
        + [pltpu.SemaphoreType.DMA((k,)) for k in (12, 12, 3, 4, 4, 8, 8, 8, 4)],
        out_shape=outs,
        compiler_params=pltpu.CompilerParams(
            vmem_limit_bytes=62 * 2**20, collective_id=3, has_side_effects=True
        ),
        cost_estimate=pl.CostEstimate(
            flops=10240 * heads * tokens * 16 * tile,
            bytes_accessed=40 * 2**20,
            transcendentals=heads * 2 * tokens * 16 * tile,
        ),
        name="back",
    )(mine, sib, far, dom, doo, om, os, stat, out.reshape(12, tile, width), dw_sum, bias)


class Sum:
    def __init__(self, a, in2, out3, keep3, in3, c4, in4, d5, in5, all6, sems):
        self.refs = a, in2, out3, keep3, in3, c4, in4, d5, in5, all6
        self.sems = sems
        row, z = lax.axis_index("row"), lax.axis_index("col")
        self.x, self.y = row // 2, lax.axis_index("img") % 2
        self.zh, self.zl = z // 2, z % 2
        _, self.to_x, self.to_img = partners()
        self.waits = []

    def go(self, *copies):
        self.waits = [
            send(src, dst, self.sems.at[0, k], self.sems.at[1, k], device)
            for k, src, dst, device in copies
        ]
        for copy in self.waits:
            copy.start()

    def settle(self):
        for copy in self.waits:
            copy.wait()

    def step2(self):
        a, in2 = self.refs[:2]
        half = a.shape[2] // 2
        self.go(
            (0, a.at[:, 1 - self.x, pl.ds(0, half)], in2.at[0], self.to_x),
            (1, a.at[1 - self.y, :, pl.ds(half, half)], in2.at[1], self.to_img),
        )

    def step3(self):
        a, in2, out3, keep3, in3 = self.refs[:5]
        x, y = self.x, self.y
        half = a.shape[2] // 2
        low, high = slice(0, half), slice(half, 2 * half)
        self.settle()
        out3[0] = a[1 - y, x, low] + in2[0, 1 - y]
        out3[1] = a[y, 1 - x, high] + in2[1, 1 - x]
        self.go((2, out3.at[0], in3.at[0], self.to_img), (3, out3.at[1], in3.at[1], self.to_x))
        keep3[0] = a[y, x, low] + in2[0, y]
        keep3[1] = a[y, x, high] + in2[1, x]

    def step4(self):
        _, _, _, keep3, in3, c4, in4 = self.refs[:7]
        n = c4.shape[2]
        self.settle()
        for h in range(2):
            term = keep3[h].astype(f32) + in3[h].astype(f32)
            for k in range(2):
                c4[h, k] = term[k * n : (k + 1) * n].astype(bf16)
        self.go((4, c4.at[:, 1 - self.zl], in4, plane_device(0, 1)))

    def step5(self):
        c4, in4, d5, in5 = self.refs[5:9]
        self.settle()
        for h in range(2):
            d5[h] = c4[h, self.zl] + in4[h]
        self.go((5, d5.at[1 - self.zh], in5, plane_device(0, 2)))

    def step6(self):
        d5, in5, all6 = self.refs[7:]
        self.settle()
        all6[self.y] = d5[self.zh] + in5[...]
        self.go((6, all6.at[self.y], all6.at[self.y], self.to_img))


def sum_scratch(count, n, wide):
    return [
        shaped((count, 2, 2, 4 * n, wide)),
        shaped((count, 2, 2, 2 * n, wide)),
        shaped((count, 2, 2 * n, wide)),
        shaped((count, 2, 2 * n, wide)),
        shaped((count, 2, 2 * n, wide)),
        shaped((count, 2, 2, n, wide)),
        shaped((count, 2, n, wide)),
        shaped((count, 2, n, wide)),
        shaped((count, n, wide)),
        shaped((count, 2, n, wide)),
    ]


def last_kernel(
    blk,
    gm_ref,
    gs_ref,
    nt_ref,
    ntsib_ref,
    wh_ref,
    x_ref,
    gmid_ref,
    dwp_ref,
    wa_ref,
    mod_ref,
    dmod_ref,
    hot_ref,
    silu_ref,
    dbu_ref,
    dbp_ref,
    dbd_ref,
    tiles_out,
    dwp_out,
    dwq_out,
    dwa_out,
    dba_out,
    dsilu_out,
    small_out,
    gm_s,
    gs_s,
    nt_s,
    ntsib_s,
    w_s,
    x_s,
    gmid_s,
    tile_s,
    gnout_s,
    gnin_s,
    in1_s,
    a_s,
    in2_s,
    out3_s,
    keep3_s,
    in3_s,
    c4_s,
    in4_s,
    d5_s,
    in5_s,
    all6_s,
    swap_s,
    dwq_s,
    place_s,
    pcore_s,
    pmid_s,
    px_s,
    psum_s,
    every_s,
    wa_s,
    dwa_s,
    dwain_s,
    dwaf_s,
    dba_s,
    dbain_s,
    dbaf_s,
    small_s,
    smallin_s,
    sum_sem,
    gn_sem,
    tile_send,
    tile_recv,
    local_sem,
    small_sem,
    p_sem,
    ada_sem,
    swap_sem,
    load_sem,
    wa_sem,
    out_sem,
):
    row = lax.axis_index("row")
    core, side = row % 2, lax.axis_index("img") % 2
    to_core, to_x, to_img = partners()
    tokens, width = x_s.shape
    tile = tokens // 12
    pad = w_s.shape[1] // 3
    part = width // 4
    ones = jnp.ones((16, tokens), bf16)

    loads = [
        pltpu.make_async_copy(src, dst, load_sem.at[k])
        for k, (src, dst) in enumerate(
            (
                (gs_ref, gs_s),
                (wh_ref.at[core], w_s),
                (gm_ref, gm_s),
                (dwp_ref.at[0], a_s.at[0]),
                (nt_ref, nt_s),
                (ntsib_ref, ntsib_s),
                (gmid_ref, gmid_s),
                (x_ref, x_s),
            )
        )
    ]
    for copy in loads:
        copy.start()
    ada = [
        pltpu.make_async_copy(
            wa_ref.at[:, pl.ds(k * width, width)], wa_s.at[i % 2], wa_sem.at[i % 2]
        )
        for i, k in enumerate((2, 3, 4, 5, 0, 1))
    ]
    for copy in ada[:2]:
        copy.start()
    greet(
        [to_core, to_img] + [plane_device(dx, dz) for dx in range(2) for dz in range(4) if dx or dz]
    )
    pending = []

    def start(src, dst, sems, k, device):
        copy = send(src, dst, sems.at[0, k], sems.at[1, k], device)
        copy.start()
        pending.append(copy)
        return copy

    sums = [
        Sum(
            *[
                ref.at[k]
                for ref in (a_s, in2_s, out3_s, keep3_s, in3_s, c4_s, in4_s, d5_s, in5_s, all6_s)
            ],
            sum_sem.at[k],
        )
        for k in range(4)
    ]
    proj = start(dwp_ref.at[1], in1_s, gn_sem, 3, to_core)

    def place(first, rows):
        for k, values in enumerate(rows):
            place_s[first + k] = functools.reduce(
                jnp.add, [hot_ref[:, i : i + 1] * values[i] for i in range(len(values))]
            ).astype(bf16)

    def p_core(k, first, count):
        at = pl.ds(first, count)
        return start(place_s.at[at], pcore_s.at[at], p_sem, k, to_core)

    def p_x(k, first, count, before):
        before.wait_recv()
        at = pl.ds(first, count)
        for c in range(first, first + count):
            pmid_s[c] = place_s[c] + pcore_s[c]
        return start(pmid_s.at[at], px_s.at[at], p_sem, k, to_x)

    def p_col(k, first, count, before):
        before.wait_recv()
        at = pl.ds(first, count)
        for c in range(first, first + count):
            psum_s[c] = pmid_s[c] + px_s[c]
            every_s[c, 0:16] = psum_s[c]
        return [
            start(
                psum_s.at[at],
                every_s.at[at, pl.ds(16 * dz, 16)],
                p_sem,
                k + dz - 1,
                plane_device(0, dz),
            )
            for dz in range(1, 4)
        ]

    def p_ada(k, first, count, before):
        for copy in before:
            copy.wait_recv()
        at = pl.ds(first, count)
        for c in range(first, first + count):
            dwaf_s[c] = dot(silu_ref[...], every_s[c], NN)
            dwa_s[c] = dwaf_s[c].astype(bf16)
            dba_s[c : c + 1] = jnp.sum(every_s[c].astype(f32), axis=0, keepdims=True)
        return start(dwa_s.at[at], dwain_s.at[at], ada_sem, k, to_img)

    def p_silu(i, first):
        ada[i].wait()
        term = dot(every_s[first], wa_s[i % 2], NT)
        if i:
            dsilu_out[...] += term
        else:
            dsilu_out[...] = term
        if i + 2 < 6:
            ada[i + 2].start()

    dba_s[...] = jnp.zeros_like(dba_s)
    place(2, [[dmod_ref[i, k : k + 1] for i in range(6)] for k in range(4)])
    early = p_core(0, 2, 4)

    loads[0].wait()
    loads[2].wait()
    total = dot(ones, gs_s[...], NN)[0:1] + dot(ones, gm_s[...], NN)[0:1]
    small_s[0] = jnp.zeros(small_s.shape[1:], f32)
    for c in range(2):
        mask = jnp.where(core == c, 1.0, 0.0)
        small_s[0, c : c + 1, 0:pad] = total[:, 0:pad] * mask
        small_s[0, c : c + 1, pad : 2 * pad] = total[:, 2 * pad :] * mask
    small_s[0, 2:3, 0:width] = dbp_ref[...]
    small_s[0, 3:4, 0:width] = dbd_ref[...]
    for k in range(4):
        small_s[0, 4 + k : 5 + k, 0:width] = dbu_ref[:, k * width : (k + 1) * width]
    route = (to_core, to_x, plane_device(0, 1), plane_device(0, 2), to_img)
    small_copies = []

    def small_step():
        k = len(small_copies)
        if k:
            small_copies[-1].wait_recv()
            small_s[k] = small_s[k - 1] + smallin_s[k - 1]
        if k < 5:
            small_copies.append(start(small_s.at[k], smallin_s.at[k], small_sem, k, route[k]))

    small_step()

    loads[1].wait()
    gn_copies = {}
    for first in (8, 0, 4):
        rows, at = slice(first * tile, (first + 4) * tile), pl.ds(first * tile, 4 * tile)
        gnout_s[rows] = dot(gs_s[rows], w_s[...], NT).astype(bf16)
        gn_copies[first] = start(gnout_s.at[at], gnin_s.at[at], gn_sem, first // 4, to_core)

    loads[3].wait()
    proj.wait_recv()
    for k in range(2):
        for h in range(2):
            a_s[0, k, h] = a_s[0, k, h] + in1_s[k, h]
    sums[0].step2()
    early = p_x(1, 2, 4, early)
    small_step()
    loads[4].wait()
    loads[5].wait()
    loads[6].wait()
    loads[7].wait()
    tile_moves_back = dict(return_moves(tile_s, tiles_out, tile_send, tile_recv, local_sem))
    late_rows = [[None] * 6, [None] * 6]

    def product(k, p):
        cols = slice(p * pad, (p + 1) * pad)
        for h in range(2):
            for c in range(2):
                rows = slice((2 * h + c) * part, (2 * h + c + 1) * part)
                term = dot(nt_s[rows], gm_s[:, cols], NN) + dot(ntsib_s[rows], gs_s[:, cols], NN)
                a_s[k, c, h] = term.astype(bf16)
        sums[k].step2()

    def first_norm(first):
        rows = slice(first * tile, (first + 4) * tile)
        gn_copies[first].wait_recv()
        both = dot(gm_s[rows], w_s[...], NT) + gnin_s[rows].astype(f32)
        for h in range(2):
            i = first // 2 + h
            rows = slice((first + 2 * h) * tile, (first + 2 * h + 2) * tile)
            y, rstd = norm(x_s[rows].astype(f32))
            gn = both[h * blk : (h + 1) * blk]
            u = gn * (1.0 + mod_ref[1, i : i + 1])
            back_term = rstd * (
                u
                - jnp.mean(u, axis=-1, keepdims=True)
                - y * jnp.mean(u * y, axis=-1, keepdims=True)
            )
            value = (gmid_s[rows].astype(f32) + back_term).astype(bf16)
            for t in range(2):
                tile_s[first + 2 * h + t] = value[t * tile : (t + 1) * tile]
            late_rows[0][i] = jnp.sum(gn, axis=0, keepdims=True)
            late_rows[1][i] = jnp.sum(gn * y, axis=0, keepdims=True)
        for t in range(first, first + 4):
            tile_moves_back[t].start()

    product(1, 2)
    first_norm(8)
    early = p_col(2, 2, 4, early)
    small_step()
    sums[0].step3()
    product(2, 1)
    first_norm(0)
    small_step()
    sums[1].step3()
    product(3, 0)
    first_norm(4)
    place(0, late_rows)
    late = p_core(5, 0, 2)
    sums[0].step4()
    small_step()
    early = p_ada(0, 2, 4, early)
    late = p_x(6, 0, 2, late)
    sums[2].step3()
    sums[1].step4()
    sums[0].step5()
    for i in range(2):
        p_silu(i, 2 + i)
    late = p_col(7, 0, 2, late)
    sums[3].step3()
    sums[2].step4()
    sums[1].step5()
    sums[0].step6()
    small_step()
    for i in range(2, 4):
        p_silu(i, 2 + i)
    late = p_ada(1, 0, 2, late)
    dba_copy = start(dba_s, dbain_s, ada_sem, 2, to_img)
    sums[3].step4()
    sums[2].step5()
    sums[1].step6()
    for i in range(4, 6):
        p_silu(i, i - 4)
    sums[3].step5()
    sums[2].step6()
    early.wait_recv()
    for c in range(2, 6):
        dwaf_s[c] = dwaf_s[c] + dwain_s[c].astype(f32)
    sums[3].step6()
    sums[0].settle()
    outs = [pltpu.make_async_copy(all6_s.at[0], dwp_out, out_sem.at[0])]
    outs[0].start()
    swaps = []
    for k in range(1, 4):
        sums[k].settle()
        swaps.append(start(all6_s.at[k, 1 - core], swap_s.at[3 - k], swap_sem, k - 1, to_core))
        dwq_s[core, 3 - k] = all6_s[k, core]
    late.wait_recv()
    dba_copy.wait_recv()
    for c in range(2):
        dwaf_s[c] = dwaf_s[c] + dwain_s[c].astype(f32)
    dbaf_s[...] = dba_s[...] + dbain_s[...]
    for copy in swaps:
        copy.wait_recv()
    for p in range(3):
        dwq_s[1 - core, p] = swap_s[p]
    for k, (src, dst) in enumerate(
        ((dwq_s, dwq_out), (dwaf_s, dwa_out), (dbaf_s, dba_out), (small_s.at[5], small_out))
    ):
        outs.append(pltpu.make_async_copy(src, dst, out_sem.at[k + 1]))
        outs[-1].start()
    for copy in pending:
        copy.wait_send()
    for copy in tile_moves_back.values():
        copy.wait()
    for copy in outs:
        copy.wait()


def last(gm, gs, nt, ntsib, w_half, x, gmid, dwp, w_ada, mod, dmod, hot, silu_t, dbu, dbp, dbd, blk):
    tokens, width = x.shape
    tile = tokens // 12
    wide = gm.shape[1]
    pad = wide // 3
    n = width // 16
    any_ref = pl.BlockSpec(memory_space=pl.ANY)
    outs = (
        shaped((12, tile, width)),
        shaped((2, n, pad)),
        shaped((2, 3, n, pad)),
        shaped((6, n, width), f32),
        shaped((8, width), f32),
        shaped((64, width), f32),
        shaped((8, 2 * pad), f32),
    )
    scratch = [
        shaped(gm.shape),
        shaped(gs.shape),
        shaped(nt.shape),
        shaped(nt.shape),
        shaped((width, wide)),
        shaped(x.shape),
        shaped(x.shape),
        outs[0],
        shaped(x.shape),
        shaped(x.shape),
        shaped(dwp.shape[1:]),
    ]
    scratch += sum_scratch(4, n, pad)
    scratch += [shaped((3, n, pad)), outs[2]]
    scratch += [shaped((6, 16, width))] * 5
    scratch += [
        shaped((6, 64, width)),
        shaped((2, width, width)),
        shaped((6, n, width)),
        shaped((6, n, width)),
        outs[3],
        outs[4],
        outs[4],
        outs[4],
        shaped((6, 8, 2 * pad), f32),
        shaped((5, 8, 2 * pad), f32),
    ]
    sems = [(4, 2, 7), (2, 4), (12,), (12,), (3,), (2, 5), (2, 10), (2, 3), (2, 3), (8,), (2,), (5,)]
    return pl.pallas_call(
        functools.partial(last_kernel, blk),
        in_specs=[any_ref] * 9 + [VMEM] * 7,
        out_specs=(any_ref,) * 5 + (VMEM, any_ref),
        scratch_shapes=[pltpu.VMEM(s.shape, s.dtype) for s in scratch]
        + [pltpu.SemaphoreType.DMA(s) for s in sems],
        out_shape=outs,
        compiler_params=pltpu.CompilerParams(
            vmem_limit_bytes=62 * 2**20, collective_id=4, has_side_effects=True
        ),
        cost_estimate=pl.CostEstimate(
            flops=8 * tokens * width * wide, bytes_accessed=60 * 2**20, transcendentals=tokens
        ),
        name="last",
    )(gm, gs, nt, ntsib, w_half, x, gmid, dwp, w_ada, mod, dmod, hot, silu_t, dbu, dbp, dbd)


def pick(values, index, axis=0):
    return lax.dynamic_index_in_dim(values, index, axis, keepdims=False)


def over_rest(v):
    size = lax.axis_size("img")
    step = 2
    while step < size:
        v = v + lax.ppermute(v, "img", [(i, i ^ step) for i in range(size)])
        step *= 2
    return v


def shards(
    tokens,
    conditioning,
    images_in_slot,
    w_qkv,
    b_qv,
    w_proj,
    b_proj,
    w_up,
    b_up,
    w_down,
    b_down,
    w_ada,
    b_ada,
    cotangent,
):
    slots, rows_tile, cols_tile, width = tokens.shape
    tile = rows_tile * cols_tile
    blk = 2 * tile
    count = slots * tile
    main = 8 * tile
    hd = width // HEADS
    heads = HEADS // 2
    half = width // 2
    pad = -(-half // 128) * 128
    hidden = w_up.shape[1]
    r, z = lax.axis_index("row"), lax.axis_index("col")
    x, core = r // 2, r % 2
    assert lax.axis_size("row") == 4 and lax.axis_size("col") == 4 and slots == 12

    four_way = images_in_slot == 4
    kinds = pick(four_way.reshape(4, 3), z)
    main_four, shared_four = pick(kinds, x), kinds[2]
    quarter = jnp.stack([2 * (x ^ dx) + ((z // 2) ^ dz) for dx in range(2) for dz in range(2)])
    picks = jnp.concatenate(
        [jnp.where(main_four, quarter, 0), jnp.where(shared_four, quarter[:2], 0)]
    )
    places = jnp.concatenate([jnp.full((4,), x, jnp.int32), jnp.full((2,), 2, jnp.int32)]) * 4 + picks
    bias = jnp.where(jnp.stack([main_four, shared_four]), -1e30, 0.0).astype(f32)
    cond = conditioning.astype(f32)
    silu = jax.nn.silu(cond).astype(bf16)
    silu_groups = silu.reshape(4, 12, width)
    chosen = jnp.take(pick(silu_groups, z), places, axis=0)
    chosen = jnp.pad(chosen, ((0, 2), (0, 0)))

    def widen(v, axis):
        return jnp.pad(v, [(0, pad - half) if a == axis else (0, 0) for a in range(v.ndim)])

    b_three = jnp.stack([b_qv[:width], jnp.zeros_like(b_qv[:width]), b_qv[width:]])
    b_half = widen(b_three.reshape(3, 2, half).astype(f32), 2).transpose(1, 0, 2)
    b_half = b_half.reshape(2, 1, 3 * pad)

    (
        inputs,
        upstream,
        qkv_mine,
        qkv_sib,
        normed_t,
        normed_sib,
        far_kv,
        om,
        os,
        att_other,
        stat,
        mod,
        w_half,
    ) = forward(
        tokens.reshape(slots, tile, width),
        cotangent.reshape(slots, tile, width),
        w_qkv,
        w_ada,
        chosen,
        b_half,
        b_ada,
        bias,
        heads,
        hd,
    )
    inputs = inputs.reshape(count, width)
    upstream = upstream.reshape(count, width)

    (
        out,
        gmid,
        do_mine,
        do_other,
        dw_sum,
        dbu,
        dwp,
        dmod_mid,
        dbp,
        dbd,
    ) = middle(
        inputs,
        upstream,
        om,
        att_other,
        mod,
        w_proj,
        b_proj,
        b_down,
        w_up,
        b_up,
        w_down,
        blk,
    )
    g_mine, g_sib, output, grad_w_up, grad_w_down = back(
        qkv_mine, qkv_sib, far_kv, do_mine, do_other, om, os, stat, out, dw_sum, bias, heads, hd
    )
    output = output.reshape(tokens.shape)
    hot = (jnp.arange(16, dtype=jnp.int32)[:, None] == places[None, :]).astype(f32)
    hot = jnp.pad(hot, ((0, 0), (0, 2)))
    rank = r * 4 + z
    n = width // 16
    silu_t = jnp.stack([pick(silu_groups, z ^ dz) for dz in range(4)])
    silu_t = lax.dynamic_slice_in_dim(silu_t, rank * n, n, 2)
    silu_t = jnp.pad(silu_t, ((0, 0), (0, 4), (0, 0))).reshape(64, n).T
    grad_x, dwp_sum, dwq_sum, dwa, dba, dsilu, small = last(
        g_mine,
        g_sib,
        normed_t,
        normed_sib,
        w_half,
        inputs,
        gmid,
        dwp,
        w_ada,
        mod,
        dmod_mid,
        hot,
        silu_t,
        dbu,
        dbp,
        dbd,
        blk,
    )
    grad_tokens = grad_x.reshape(tokens.shape).astype(f32)
    dwp_sum, dwq_sum, dwa, dba, small, grad_w_up, grad_w_down = (
        over_rest(v) for v in (dwp_sum, dwq_sum, dwa, dba, small, grad_w_up, grad_w_down)
    )
    grad_w_proj = jnp.concatenate([dwp_sum[0], dwp_sum[1, :, 2 * pad - width :]], axis=1)
    grad_w_proj = grad_w_proj.astype(f32)
    grad_w_qkv = dwq_sum[..., :half].astype(f32).transpose(2, 1, 0, 3).reshape(n, 3 * width)
    grad_w_ada = dwa.transpose(1, 0, 2).reshape(n, 6 * width)
    grad_b_ada = lax.dynamic_slice_in_dim(dba[:6].reshape(6 * width), rank * 6 * n, 6 * n, 0)
    d_s = dsilu.reshape(4, 16, width)[:, :12]
    d_s = jnp.stack([pick(d_s, z ^ g) for g in range(4)]).reshape(slots, 4, width)
    sig = jax.nn.sigmoid(cond)
    grad_conditioning = d_s * (sig * (1.0 + cond * (1.0 - sig)))
    db_qv = small[:2].reshape(2, 2, pad)[..., :half].transpose(1, 0, 2).reshape(2 * width)

    def own(values):
        size = values.shape[0] // 16
        return lax.dynamic_slice_in_dim(values, rank * size, size, 0)

    return (
        output,
        grad_tokens,
        grad_conditioning,
        grad_w_qkv,
        own(db_qv),
        grad_w_proj,
        own(small[2, :width]),
        grad_w_up,
        own(small[4:, :width].reshape(hidden)),
        grad_w_down,
        own(small[3, :width]),
        grad_w_ada,
        grad_b_ada,
    )


def solution(mesh):
    grid = P("img", "row", "col", None)
    plane = ("row", "col")
    return jax.shard_map(
        shards,
        mesh=mesh,
        in_specs=(grid, P("img", None, None), P("img")) + (P(),) * 10 + (grid,),
        out_specs=(grid, grid, P("img", None, None))
        + (P(plane, None), P(plane)) * 5,
        check_vma=False,
    )
```

```python
import functools
import math

import jax
import jax.numpy as jnp
from jax import lax
from jax.experimental import pallas as pl
from jax.experimental.pallas import tpu as pltpu
from jax.sharding import PartitionSpec as P

HEADS = 16
EPS = 1e-06
LOG2E = math.log2(math.e)
GELU_A = math.sqrt(2.0 / math.pi)
GELU_B = 0.044715
VMEM_LIMIT = 60 * 2**20

f32 = jnp.float32
bf16 = jnp.bfloat16
NT = (((1,), (1,)), ((), ()))
NN = (((1,), (0,)), ((), ()))
TN = (((0,), (0,)), ((), ()))

VMEM = pl.BlockSpec(memory_space=pltpu.VMEM)
SMEM = pl.BlockSpec(memory_space=pltpu.SMEM)


def dot(left, right, dims):
    return lax.dot_general(left, right, dims, preferred_element_type=f32)


def shaped(shape, dtype=bf16):
    return jax.ShapeDtypeStruct(shape, dtype)


def norm(values):
    center = values - jnp.mean(values, axis=-1, keepdims=True)
    rstd = lax.rsqrt(jnp.mean(center * center, axis=-1, keepdims=True) + EPS)
    return center * rstd, rstd


def plus(a, b):
    return (a.astype(f32) + b.astype(f32)).astype(bf16)


def flip(index):
    return index + 1 - 2 * (index % 2)


def partners():
    img, r, z = lax.axis_index("img"), lax.axis_index("row"), lax.axis_index("col")
    return (img, flip(r), z), (img, (r + 2) % 4, z), (flip(img), r, z)


def plane_device(dx, dz):
    img, r, z = lax.axis_index("img"), lax.axis_index("row"), lax.axis_index("col")
    return img, (r + 2 * dx) % 4, hop(z, dz)


def hop(z, dz):
    return (z, flip(z), (z + 2) % 4, 3 - z)[dz]


def signal(devices):
    barrier = pltpu.get_barrier_semaphore()
    for device in devices:
        pl.semaphore_signal(
            barrier, inc=1, device_id=device, device_id_type=pl.DeviceIdType.MESH
        )


def await_signals(devices):
    pl.semaphore_wait(pltpu.get_barrier_semaphore(), len(devices))


def greet(devices):
    signal(devices)
    await_signals(devices)


def send(src, dst, send_sem, recv_sem, device):
    return pltpu.make_async_remote_copy(
        src_ref=src,
        dst_ref=dst,
        send_sem=send_sem,
        recv_sem=recv_sem,
        device_id=device,
        device_id_type=pl.DeviceIdType.MESH,
    )


def tile_moves(src, dst, send_sem, recv_sem, local_sem):
    r, z = lax.axis_index("row"), lax.axis_index("col")
    x = r // 2
    shared, near, far, local = [], [], [], []
    for dz in range(4):
        first = 3 * hop(z, dz)
        moves = (
            (shared, 0, first + 2, 8 + dz),
            (near, 0, first + x, dz),
            (far, 1, first + 1 - x, 4 + dz),
        )
        for group, dx, slot, place_at in moves:
            if dx == 0 and dz == 0:
                sem = local_sem.at[0 if place_at else 1]
                local.append(pltpu.make_async_copy(src.at[slot], dst.at[place_at], sem))
            else:
                sems = send_sem.at[place_at], recv_sem.at[place_at]
                group.append(
                    send(src.at[slot], dst.at[place_at], *sems, plane_device(dx, dz))
                )
    return local, shared, near, far


def head_window(head, hd):
    first = head * hd
    start = pl.multiple_of((first // 128) * 128, 128)
    lane = lax.broadcasted_iota(jnp.int32, (1, 256), 1) + start
    inside = jnp.logical_and(lane >= first, lane < first + hd)
    return pl.ds(start, 256), inside


def gather_rows(dst, col, sources, base, count):
    pad = dst.shape[1]
    for i in range(count):
        for j, src in enumerate(sources):
            row = 256 * i + 128 * j
            dst[row : row + 128] = src[base + 128 * i : base + 128 * i + 128, col : col + pad]


def attend(heads, hd, count, base, bias, mine, sib, far, o_mine, o_sib, stat, q_s, k_s, v_s, o_s):
    pad = q_s.shape[1]
    scale = LOG2E / math.sqrt(hd)
    gather_rows(q_s, 0, (mine, sib), base, count)
    gather_rows(k_s, pad, (mine, sib), base, count)
    gather_rows(v_s, 2 * pad, (mine, sib), base, count)
    if far is not None:
        k_s[256 * count :] = far[:, 0:pad]
        v_s[256 * count :] = far[:, pad : 2 * pad]
    blocks = k_s.shape[0] // 256
    lane = lax.broadcasted_iota(jnp.int32, (1, 128), 1)

    def body(head, carry):
        win, inside = head_window(head, hd)
        for i in range(count):
            rows = slice(256 * i, 256 * i + 256)
            q = jnp.where(inside, q_s[rows, win], jnp.zeros((), bf16))
            s = dot(q, k_s[:, win], NT)
            cols = [s[:, 256 * j : 256 * j + 256] for j in range(blocks)]
            best = [jnp.max(col, axis=1, keepdims=True) for col in cols]
            own = best[i]
            rest = best[:i] + best[i + 1 :]
            top = jnp.maximum(own, functools.reduce(jnp.maximum, rest) + bias)
            near = -scale * top
            away = near + bias
            cols = [
                jnp.exp2(col * scale + (near if j == i else away)) for j, col in enumerate(cols)
            ]
            total = functools.reduce(
                jnp.add, [jnp.sum(col, axis=1, keepdims=True) for col in cols]
            )
            p = jnp.concatenate([col.astype(bf16) for col in cols], axis=1)
            o = dot(p, v_s[:, win], NN) / total
            o_s[rows, win] = jnp.where(inside, o.astype(bf16), o_s[rows, win])
            at = slice(2 * base + 256 * i, 2 * base + 256 * i + 256)
            stat[at] = jnp.where(lane == head, top * scale + jnp.log2(total), stat[at])
        return carry

    lax.fori_loop(0, heads, body, 0)
    for i in range(count):
        at = slice(base + 128 * i, base + 128 * i + 128)
        o_mine[at] = o_s[256 * i : 256 * i + 128]
        o_sib[at] = o_s[256 * i + 128 : 256 * i + 256]


def forward_kernel(
    heads,
    hd,
    tok_ref,
    cot_ref,
    wq_ref,
    wa_ref,
    chosen_ref,
    bh_ref,
    ba_ref,
    bias_ref,
    x_out,
    cot_out,
    mine_out,
    sib_out,
    nt_out,
    ntsib_out,
    far_out,
    om_out,
    os_out,
    ao_out,
    stat_out,
    mod_out,
    wh_out,
    x_s,
    raw_s,
    w_s,
    wa_s,
    mod_s,
    nt_s,
    ntsib_s,
    other_s,
    mine_s,
    sib_s,
    far_s,
    q_s,
    k_s,
    v_s,
    o_s,
    om_s,
    os_s,
    ao_s,
    stat_s,
    tok_send,
    tok_recv,
    cot_send,
    cot_recv,
    local_sem,
    raw_sem,
    wa_sem,
    side_send,
    side_recv,
    out_sem,
):
    tile, width = x_s.shape[1:]
    tokens = 12 * tile
    main = 8 * tile
    half = width // 2
    pad = w_s.shape[2] // 3
    rows_step = raw_s.shape[1]
    core = lax.axis_index("row") % 2
    to_core, to_x, _ = partners()

    raw = [
        pltpu.make_async_copy(
            wq_ref.at[pl.ds(i * rows_step, rows_step)], raw_s.at[i % 2], raw_sem.at[i % 2]
        )
        for i in range(width // rows_step)
    ]
    ada = [
        pltpu.make_async_copy(
            wa_ref.at[:, pl.ds(i * width, width)], wa_s.at[i % 2], wa_sem.at[i % 2]
        )
        for i in range(6)
    ]
    for copy in raw[:2] + ada[:2]:
        copy.start()
    greet([to_core] + [plane_device(dx, dz) for dx in range(2) for dz in range(4) if dx or dz])
    local, shared, near, far = tile_moves(tok_ref, x_s, tok_send, tok_recv, local_sem)
    for copy in local + shared + near + far:
        copy.start()

    w_s[...] = jnp.zeros_like(w_s)
    for i, copy in enumerate(raw):
        copy.wait()
        rows = slice(i * rows_step, (i + 1) * rows_step)
        for h in range(2):
            for p in range(3):
                start = half * (2 * p + h)
                w_s[h, rows, p * pad : p * pad + half] = raw_s[i % 2, :, start : start + half]
        if i + 2 < len(raw):
            raw[i + 2].start()
    for i, copy in enumerate(ada):
        copy.wait()
        bias = ba_ref[i * width : (i + 1) * width].astype(f32).reshape(1, width)
        mod_s[i] = dot(chosen_ref[...], wa_s[i % 2], NN) + bias
        if i + 2 < len(ada):
            ada[i + 2].start()
    outs = []

    def put(src, dst):
        copy = pltpu.make_async_copy(src, dst, out_sem.at[len(outs)])
        copy.start()
        outs.append(copy)

    put(w_s, wh_out)
    put(mod_s, mod_out)

    sides = []

    def side(src, dst, device):
        k = len(sides)
        copy = send(src, dst, side_send.at[k], side_recv.at[k], device)
        copy.start()
        sides.append(copy)
        return copy

    moves = None
    from_core = []
    for first, waits in ((8, local[:1] + shared), (0, local[1:] + near), (4, far)):
        for copy in waits:
            copy.wait()
        if first == 4:
            moves = tile_moves(cot_ref, cot_out, cot_send, cot_recv, local_sem)
            for group in moves:
                for copy in group:
                    copy.start()
        parts = []
        for i in range(2):
            at = first // 2 + i
            values = x_s[first + 2 * i : first + 2 * i + 2].reshape(2 * tile, width)
            normed, _ = norm(values.astype(f32))
            parts.append((normed * (1.0 + mod_s[1, at : at + 1]) + mod_s[0, at : at + 1]).astype(bf16))
        normed = jnp.concatenate(parts, axis=0)
        rows = slice(first * tile, (first + 4) * tile)
        other_s[rows] = (dot(normed, w_s[1 - core], NN) + bh_ref[1 - core]).astype(bf16)
        at = pl.ds(first * tile, 4 * tile)
        from_core.append(side(other_s.at[at], sib_s.at[at], to_core))
        mine_s[rows] = (dot(normed, w_s[core], NN) + bh_ref[core]).astype(bf16)
        nt_s[:, rows] = normed.T
        if first == 0:
            from_core[0].wait_recv()
            at, cols = pl.ds(main, tokens - main), pl.ds(pad, 2 * pad)
            size = tokens - main
            from_x = [
                side(src.at[at, cols], far_s.at[pl.ds(size * k, size)], to_x)
                for k, src in enumerate((mine_s, sib_s))
            ]
    put(x_s, x_out)
    put(mine_s, mine_out)
    put(nt_s, nt_out)
    nt_copy = side(nt_s, ntsib_s, to_core)

    o_s[...] = jnp.zeros_like(o_s)
    stat_s[...] = jnp.zeros_like(stat_s)
    for copy in from_core[1:]:
        copy.wait_recv()
    put(sib_s, sib_out)
    scratch = (om_s, os_s, stat_s, q_s, k_s, v_s, o_s)
    attend(heads, hd, 4, 0, bias_ref[0], mine_s, sib_s, None, *scratch)
    back = [side(os_s.at[pl.ds(0, main)], ao_s.at[pl.ds(0, main)], to_core)]
    for copy in from_x:
        copy.wait_recv()
    put(far_s, far_out)
    attend(heads, hd, 2, main, bias_ref[1], mine_s, sib_s, far_s, *scratch)
    at = pl.ds(main, tokens - main)
    back.append(side(os_s.at[at], ao_s.at[at], to_core))
    put(om_s, om_out)
    put(os_s, os_out)
    put(stat_s, stat_out)
    nt_copy.wait_recv()
    put(ntsib_s, ntsib_out)
    for copy in back:
        copy.wait_recv()
    put(ao_s, ao_out)
    for copy in sides:
        copy.wait_send()
    for group in moves:
        for copy in group:
            copy.wait()
    for copy in outs:
        copy.wait()


def forward(tok, cot, w_qkv, w_ada, chosen, b_half, b_ada, bias, heads, hd):
    _, tile, width = tok.shape
    tokens = 12 * tile
    pad = b_half.shape[2] // 3
    any_ref = pl.BlockSpec(memory_space=pl.ANY)
    outs = (
        shaped((12, tile, width)),
        shaped((12, tile, width)),
        shaped((tokens, 3 * pad)),
        shaped((tokens, 3 * pad)),
        shaped((width, tokens)),
        shaped((width, tokens)),
        shaped((8 * tile, 2 * pad)),
        shaped((tokens, pad)),
        shaped((tokens, pad)),
        shaped((tokens, pad)),
        shaped((2 * tokens, 128), f32),
        shaped((6, 8, width), f32),
        shaped((2, width, 3 * pad)),
    )
    scratch = [
        outs[0],
        shaped((2, width // 4, 3 * width)),
        outs[12],
        shaped((2, width, width)),
        outs[11],
        outs[4],
        outs[4],
        outs[2],
        outs[2],
        outs[2],
        outs[6],
        shaped((16 * tile, pad)),
        shaped((16 * tile, pad)),
        shaped((16 * tile, pad)),
        shaped((16 * tile, pad)),
        outs[7],
        outs[7],
        outs[7],
        outs[10],
    ]
    return pl.pallas_call(
        functools.partial(forward_kernel, heads, hd),
        in_specs=[any_ref] * 4 + [VMEM] * 3 + [SMEM],
        out_specs=(any_ref,) * len(outs),
        scratch_shapes=[pltpu.VMEM(s.shape, s.dtype) for s in scratch]
        + [pltpu.SemaphoreType.DMA((k,)) for k in (12, 12, 12, 12, 2, 2, 2, 10, 10, 12)],
        out_shape=outs,
        compiler_params=pltpu.CompilerParams(
            vmem_limit_bytes=62 * 2**20, collective_id=2, has_side_effects=True
        ),
        cost_estimate=pl.CostEstimate(
            flops=4 * tokens * width * 3 * pad + 4096 * heads * tokens * 16 * tile,
            bytes_accessed=70 * 2**20,
            transcendentals=heads * 2 * tokens * 16 * tile,
        ),
        name="forward",
    )(tok, cot, w_qkv, w_ada, chosen, b_half, b_ada, bias)


def middle_kernel(
    blk,
    chunks,
    x_ref,
    cot_ref,
    am_ref,
    ao_ref,
    mod_ref,
    wp_ref,
    bp_ref,
    bd_ref,
    wu_ref,
    bu_ref,
    wd_ref,
    out_ref,
    gmid_ref,
    dom_ref,
    doo_ref,
    sum_ref,
    dbu_ref,
    dwp_ref,
    dmod_ref,
    dbp_ref,
    dbd_ref,
    mid_s,
    br1_s,
    n_s,
    nt_s,
    db2_s,
    db2t_s,
    br2_s,
    gn_s,
    db1_s,
    mine_s,
    other_s,
    in1_s,
    in2_s,
    out3_s,
    keep3_s,
    in3_s,
    sum4_s,
    in4_s,
    sum5_s,
    in5_s,
    sems,
    done,
    wpm_ref,
    wpo_ref,
):
    step = pl.program_id(0)
    tokens, width = x_ref.shape
    pad = am_ref.shape[1]
    blocks = tokens // blk
    part = width // 4
    row = lax.axis_index("row")
    x, core, y = row // 2, row % 2, lax.axis_index("img") % 2
    z = lax.axis_index("col")
    zh, zl = z // 2, z % 2
    to_core, to_x, to_img = partners()
    to_near, to_far = plane_device(0, 1), plane_device(0, 2)
    neighbours = to_core, to_x, to_img, to_near, to_far
    halves = [
        pltpu.make_async_copy(
            wp_ref.at[pl.ds(pl.multiple_of(2 * part * c, 16), 2 * part)],
            dst.at[pl.ds(0, 2 * part)],
            done.at[k],
        )
        for k, (c, dst) in enumerate(((core, wpm_ref), (1 - core, wpo_ref)))
    ]

    half = mine_s.shape[3] // 2
    low, high = slice(0, half), slice(half, 2 * half)

    def copy(k, a, src, dst, device):
        return send(src, dst, sems.at[0, k, a % 4], sems.at[1, k, a % 4], device)

    def stage1(a):
        return [copy(0, a, other_s.at[a % 2], in1_s.at[a % 2], to_core)]

    def stage2(a):
        t = a % 4
        return [
            copy(1, a, mine_s.at[t, :, 1 - x, pl.ds(0, half)], in2_s.at[t, 0], to_x),
            copy(2, a, mine_s.at[t, 1 - y, :, pl.ds(half, half)], in2_s.at[t, 1], to_img),
        ]

    def stage3(a):
        return [
            copy(3 + h, a, out3_s.at[a % 2, h], in3_s.at[a % 4, h], (to_img, to_x)[h])
            for h in range(2)
        ]

    def stage4(a):
        return [copy(5, a, sum4_s.at[:, 1 - zl], in4_s.at[a % 2], to_near)]

    def stage5(a):
        return [copy(6, a, sum5_s.at[1 - zh], in5_s.at[a % 2], to_far)]

    def when(lag):
        return pl.when(jnp.logical_and(step >= lag, step < chunks + lag))

    def go(copies):
        for c in copies:
            c.start()

    def settle(copies):
        for c in copies:
            c.wait()

    @pl.when(step == 0)
    def _():
        signal(neighbours)
        for c in halves:
            c.start()
        pad_rows = jnp.zeros((pad - 2 * part, width), bf16)
        wpm_ref[2 * part :] = pad_rows
        wpo_ref[2 * part :] = pad_rows
        for c in halves:
            c.wait()
        br1_s[...] = (
            dot(am_ref[...], wpm_ref[...], NN) + dot(ao_ref[...], wpo_ref[...], NN) + bp_ref[...].astype(f32).reshape(1, width)
        ).astype(bf16)
        for i in range(blocks):
            rows = slice(i * blk, (i + 1) * blk)
            mid = x_ref[rows].astype(f32) + mod_ref[2, i : i + 1] * br1_s[rows].astype(f32)
            mid_s[rows] = mid
            normed, _ = norm(mid)
            n_s[rows] = (normed * (1.0 + mod_ref[4, i : i + 1]) + mod_ref[3, i : i + 1]).astype(bf16)
            db2_s[rows] = (mod_ref[5, i : i + 1] * cot_ref[rows].astype(f32)).astype(bf16)
        for b in range(width // 128):
            for src, dst in ((n_s, nt_s), (db2_s, db2t_s)):
                turned = src[:, 128 * b : 128 * b + 128].T
                for q in range(4):
                    first = 128 * b + 32 * q
                    g = first // part
                    to = ((g + core) % 2) * (2 * part) + (g // 2) * part + first % part
                    dst[pl.ds(pl.multiple_of(to, 16), 32)] = turned[32 * q : 32 * q + 32]
        br2_s[...] = jnp.zeros_like(br2_s)
        gn_s[...] = jnp.zeros_like(gn_s)

    @pl.when(step < chunks)
    def _():
        pre = dot(n_s[...], wu_ref[...], NN) + bu_ref[...].astype(f32).reshape(1, -1)
        square = pre * pre
        t = jnp.tanh(pre * (GELU_A + (GELU_A * GELU_B) * square))
        hidden = (0.5 * pre * (1.0 + t)).astype(bf16)
        slope = 0.5 * (1.0 + t) + 0.5 * pre * (1.0 - t * t) * (
            GELU_A + (3.0 * GELU_A * GELU_B) * square
        )
        gpre = dot(db2_s[...], wd_ref[...], NT) * slope
        gp = gpre.astype(bf16)
        for k, (left, right) in enumerate(((nt_s, gp), (db2t_s, hidden))):
            for own, dst in enumerate((mine_s.at[step % 4, k], other_s.at[step % 2, k])):
                for h in range(2):
                    rows = slice((2 * own + h) * part, (2 * own + h + 1) * part)
                    dst[h] = dot(left[rows], right, NN).astype(bf16)

        @pl.when(step == 0)
        def _():
            await_signals(neighbours)

        go(stage1(step))
        br2_s[...] += dot(hidden, wd_ref[...], NN)
        gn_s[...] += dot(gp, wu_ref[...], NT)
        dbu_ref[...] = jnp.sum(gpre, axis=0, keepdims=True)

    @when(6)
    def _():
        a = step - 6
        settle(stage5(a))
        sum_ref[...] = sum5_s[zh] + in5_s[a % 2]

    @when(5)
    def _():
        a = step - 5
        settle(stage4(a))
        for h in range(2):
            sum5_s[h] = sum4_s[h, zl] + in4_s[a % 2, h]
        go(stage5(a))

    @when(4)
    def _():
        a = step - 4
        settle(stage3(a))
        for h in range(2):
            term = keep3_s[a % 2, h].astype(f32) + in3_s[a % 4, h].astype(f32)
            for k in range(2):
                sum4_s[h, k] = term[k * half // 2 : (k + 1) * half // 2].astype(bf16)
        go(stage4(a))

    @when(2)
    def _():
        a = step - 2
        s, t = a % 2, a % 4
        settle(stage2(a))
        out3_s[s, 0] = mine_s[t, 1 - y, x, low] + in2_s[t, 0, 1 - y]
        out3_s[s, 1] = mine_s[t, y, 1 - x, high] + in2_s[t, 1, 1 - x]
        go(stage3(a))
        keep3_s[s, 0] = mine_s[t, y, x, low] + in2_s[t, 0, y]
        keep3_s[s, 1] = mine_s[t, y, x, high] + in2_s[t, 1, x]

    @when(0)
    def _():
        a = step - 0
        settle(stage1(a))
        for k in range(2):
            for h in range(2):
                mine_s[a % 4, k, h] = mine_s[a % 4, k, h] + in1_s[a % 2, k, h]
        go(stage2(a))

    outs = [
        pltpu.make_async_copy(n_s, out_ref, done.at[0]),
        pltpu.make_async_copy(db2_s, gmid_ref, done.at[1]),
    ]

    def finish(i):
        rows = slice(i * blk, (i + 1) * blk)
        cot = cot_ref[rows].astype(f32)
        br2 = br2_s[rows] + bd_ref[...].astype(f32).reshape(1, width)
        mid = mid_s[rows]
        n_s[rows] = (mid + mod_ref[5, i : i + 1] * br2).astype(bf16)
        normed, rstd = norm(mid)
        gn = gn_s[rows]
        u = gn * (1.0 + mod_ref[4, i : i + 1])
        gmid = cot + rstd * (
            u
            - jnp.mean(u, axis=-1, keepdims=True)
            - normed * jnp.mean(u * normed, axis=-1, keepdims=True)
        )
        db1 = mod_ref[2, i : i + 1] * gmid
        db1_s[rows] = db1.astype(bf16)
        dbp = jnp.sum(db1, axis=0, keepdims=True)
        dbd = jnp.sum(db2_s[rows].astype(f32), axis=0, keepdims=True)
        dbp_ref[...] = dbp if i == 0 else dbp_ref[...] + dbp
        dbd_ref[...] = dbd if i == 0 else dbd_ref[...] + dbd
        db2_s[rows] = gmid.astype(bf16)
        dmod_ref[i, 0:1] = jnp.sum(gmid * br1_s[rows].astype(f32), axis=0, keepdims=True)
        dmod_ref[i, 1:2] = jnp.sum(gn, axis=0, keepdims=True)
        dmod_ref[i, 2:3] = jnp.sum(gn * normed, axis=0, keepdims=True)
        dmod_ref[i, 3:4] = jnp.sum(cot * br2, axis=0, keepdims=True)

    for k in range(3):

        @pl.when(step == chunks + k)
        def _(k=k):
            finish(2 * k)
            finish(2 * k + 1)

    @pl.when(step == chunks + 3)
    def _():
        for c in outs:
            c.start()
        dom_ref[...] = dot(db1_s[...], wpm_ref[...], NT).astype(bf16)
        doo_ref[...] = dot(db1_s[...], wpo_ref[...], NT).astype(bf16)

    @pl.when(step == chunks + 4)
    def _():
        for side, ref in ((core, am_ref), (1 - core, ao_ref)):
            term = dot(ref[...], db1_s[...], TN)
            for c in range(2):
                rows = term[part * c : part * (c + 1)]
                for k, at in enumerate((0, width - pad)):
                    dwp_ref[(c + core) % 2, k, side] = rows[:, at : at + pad].astype(bf16)
        settle(outs)


def middle(x, cot, att_m, att_o, mod, w_proj, b_proj, b_down, w_up, b_up, w_down, blk):
    tokens, width = x.shape
    pad = att_m.shape[1]
    hidden = w_up.shape[1]
    chunk = 512
    chunks = hidden // chunk
    n = width // 16
    any_ref = pl.BlockSpec(memory_space=pl.ANY)

    def at(j):
        return jnp.minimum(j, chunks - 1)

    return pl.pallas_call(
        functools.partial(middle_kernel, blk, chunks),
        grid=(chunks + 6,),
        in_specs=[VMEM] * 5
        + [any_ref, VMEM, VMEM]
        + [
            pl.BlockSpec((width, chunk), lambda j: (0, at(j))),
            pl.BlockSpec((chunk,), lambda j: (at(j),)),
            pl.BlockSpec((chunk, width), lambda j: (at(j), 0)),
        ],
        out_specs=[any_ref, any_ref, VMEM, VMEM]
        + [
            pl.BlockSpec((n, chunk), lambda j: (0, jnp.maximum(j - 6, 0))),
            pl.BlockSpec((1, chunk), lambda j: (0, at(j))),
        ]
        + [VMEM] * 4,
        scratch_shapes=[
            pltpu.VMEM((tokens, width), f32),
            pltpu.VMEM((tokens, width), bf16),
            pltpu.VMEM((tokens, width), bf16),
            pltpu.VMEM((width, tokens), bf16),
            pltpu.VMEM((tokens, width), bf16),
            pltpu.VMEM((width, tokens), bf16),
            pltpu.VMEM((tokens, width), f32),
            pltpu.VMEM((tokens, width), f32),
            pltpu.VMEM((tokens, width), bf16),
            pltpu.VMEM((4, 2, 2, 4 * n, chunk), bf16),
            pltpu.VMEM((2, 2, 2, 4 * n, chunk), bf16),
            pltpu.VMEM((2, 2, 2, 4 * n, chunk), bf16),
            pltpu.VMEM((4, 2, 2, 2 * n, chunk), bf16),
            pltpu.VMEM((2, 2, 2 * n, chunk), bf16),
            pltpu.VMEM((2, 2, 2 * n, chunk), bf16),
            pltpu.VMEM((4, 2, 2 * n, chunk), bf16),
            pltpu.VMEM((2, 2, n, chunk), bf16),
            pltpu.VMEM((2, 2, n, chunk), bf16),
            pltpu.VMEM((2, n, chunk), bf16),
            pltpu.VMEM((2, n, chunk), bf16),
            pltpu.SemaphoreType.DMA((2, 7, 4)),
            pltpu.SemaphoreType.DMA((2,)),
            pltpu.VMEM((pad, width), bf16),
            pltpu.VMEM((pad, width), bf16),
        ],
        out_shape=(
            shaped((tokens, width)),
            shaped((tokens, width)),
            shaped((tokens, pad)),
            shaped((tokens, pad)),
            shaped((n, hidden)),
            shaped((1, hidden), f32),
            shaped((2, 2, 2, 4 * n, pad)),
            shaped((tokens // blk, 4, width), f32),
            shaped((1, width), f32),
            shaped((1, width), f32),
        ),
        compiler_params=pltpu.CompilerParams(
            vmem_limit_bytes=62 * 2**20, collective_id=1, has_side_effects=True
        ),
        cost_estimate=pl.CostEstimate(
            flops=2 * tokens * width * (6 * hidden + 6 * pad),
            bytes_accessed=60 * 2**20,
            transcendentals=tokens * hidden,
        ),
        name="middle",
    )(x, cot, att_m, att_o, mod, w_proj, b_proj, b_down, w_up, b_up, w_down)


def attend_back(heads, hd, count, base, bias, mine, sib, far, d_mine, d_sib, o_mine, o_sib, stat,
                g_mine, g_sib, g_far, q_s, k_s, v_s, do_s, kt_s, dqt_s, dk_s, dv_s, p_s, ds_s,
                lse_s, dd_s):
    pad = q_s.shape[1]
    inv = 1.0 / math.sqrt(hd)
    scale = LOG2E * inv
    pair = (mine, sib)
    gather_rows(q_s, 0, pair, base, count)
    gather_rows(k_s, pad, pair, base, count)
    gather_rows(v_s, 2 * pad, pair, base, count)
    gather_rows(do_s, 0, (d_mine, d_sib), base, count)
    if far is not None:
        k_s[256 * count :] = far[:, 0:pad]
        v_s[256 * count :] = far[:, pad : 2 * pad]
    kt_s[...] = k_s[...].T.astype(f32)
    dqt_s[...] = jnp.zeros_like(dqt_s)
    dk_s[...] = jnp.zeros_like(dk_s)
    dv_s[...] = jnp.zeros_like(dv_s)
    blocks = k_s.shape[0] // 256
    used = 256 * count
    row = lax.broadcasted_iota(jnp.int32, (heads, pad), 0)
    col = lax.broadcasted_iota(jnp.int32, (heads, pad), 1)
    member = jnp.where(jnp.logical_and(col >= row * hd, col < row * hd + hd), 1.0, 0.0).astype(bf16)
    for i in range(count):
        rows = slice(256 * i, 256 * i + 256)
        at = 2 * base + 256 * i
        lse_s[i] = stat[at : at + 256].T[0:heads]
        o = jnp.concatenate(
            [ref[base + 128 * i : base + 128 * i + 128] for ref in (o_mine, o_sib)], axis=0
        )
        both = do_s[rows].astype(f32) * o.astype(f32)
        high = both.astype(bf16)
        low = (both - high.astype(f32)).astype(bf16)
        dd_s[i] = dot(member, high, NT) + dot(member, low, NT)

    def body(head, carry):
        win, inside = head_window(head, hd)
        own = pl.ds(pl.multiple_of(head * hd, 8), hd)
        zero = jnp.zeros((), bf16)
        for i in range(count):
            rows = slice(256 * i, 256 * i + 256)
            q = jnp.where(inside, q_s[rows, win], zero)
            do = jnp.where(inside, do_s[rows, win], zero)
            near = -lse_s[i, pl.ds(head, 1)]
            away = near + bias
            dd = dd_s[i, pl.ds(head, 1)]
            s = dot(k_s[:, win], q, NT)
            dp = dot(v_s[:, win], do, NT)
            for j in range(blocks):
                keys = slice(256 * j, 256 * j + 256)
                p = jnp.exp2(s[keys] * scale + (near if j == i else away))
                ds_s[keys, rows] = (p * (dp[keys] - dd)).astype(bf16)
                p_s[keys, rows] = p.astype(bf16)
        q = jnp.where(inside, q_s[0:used, win], zero)
        do = jnp.where(inside, do_s[0:used, win], zero)
        dv_s[:, win] += dot(p_s[:, 0:used], do, NN)
        dk_s[:, win] += dot(ds_s[:, 0:used], q, NN)
        dqt_s[own, 0:used] = dot(kt_s[own, :].astype(bf16), ds_s[:, 0:used], NN)
        return carry

    lax.fori_loop(0, heads, body, 0)
    for i in range(count):
        for j, dst in enumerate((g_mine, g_sib)):
            rows = slice(256 * i + 128 * j, 256 * i + 128 * j + 128)
            out = slice(base + 128 * i, base + 128 * i + 128)
            dst[out, 0:pad] = (dqt_s[:, rows] * inv).astype(bf16).T
            dst[out, pad : 2 * pad] = (dk_s[rows] * inv).astype(bf16)
            dst[out, 2 * pad : 3 * pad] = dv_s[rows].astype(bf16)
    if far is not None:
        g_far[:, 0:pad] = (dk_s[used:] * inv).astype(bf16)
        g_far[:, pad : 2 * pad] = dv_s[used:].astype(bf16)


def return_moves(src, dst, send_sem, recv_sem, local_sem):
    r, z = lax.axis_index("row"), lax.axis_index("col")
    local, near, far, shared = [], [], [], []
    for dz in range(4):
        for group, dx, slot, at in (
            (near, 0, 3 * z + r // 2, dz),
            (far, 1, 3 * z + r // 2, 4 + dz),
            (shared, 0, 3 * z + 2, 8 + dz),
        ):
            if dx == 0 and dz == 0:
                sem = local_sem.at[0 if at else 1]
                local.append((at, pltpu.make_async_copy(src.at[at], dst.at[slot], sem)))
            else:
                sems = send_sem.at[at], recv_sem.at[at]
                copy = send(src.at[at], dst.at[slot], *sems, plane_device(dx, dz))
                group.append((at, copy))
    return local + near + far + shared


def back_kernel(
    heads,
    hd,
    mine_ref,
    sib_ref,
    far_ref,
    dom_ref,
    doo_ref,
    om_ref,
    os_ref,
    stat_ref,
    out_ref,
    sum_ref,
    bias_ref,
    gm_out,
    gs_out,
    tiles_out,
    dwu_out,
    dwd_out,
    mine_s,
    sib_s,
    far_s,
    dom_s,
    dos_s,
    om_s,
    os_s,
    stat_s,
    gm_s,
    gs_s,
    gfar_s,
    back_s,
    q_s,
    k_s,
    v_s,
    do_s,
    kt_s,
    dqt_s,
    dk_s,
    dv_s,
    p_s,
    ds_s,
    lse_s,
    dd_s,
    sum_s,
    piece_s,
    here_s,
    there_s,
    turn_s,
    dwd_s,
    dwu_s,
    tile_send,
    tile_recv,
    local_sem,
    side_send,
    side_recv,
    piece_send,
    piece_recv,
    load_sem,
    out_sem,
):
    row, z = lax.axis_index("row"), lax.axis_index("col")
    x, core, side = row // 2, row % 2, lax.axis_index("img") % 2
    to_core, to_x, to_img = partners()
    tokens = mine_s.shape[0]
    pad = om_s.shape[1]
    main = 2 * tokens // 3
    n = sum_s.shape[1]
    wide = piece_s.shape[4]

    loads = []

    def load(src, dst):
        copy = pltpu.make_async_copy(src, dst, load_sem.at[len(loads)])
        copy.start()
        loads.append(copy)

    sides = []

    def start(src, dst, device):
        k = len(sides)
        copy = send(src, dst, side_send.at[k], side_recv.at[k], device)
        copy.start()
        sides.append(copy)
        return copy

    for src, dst in (
        (mine_ref, mine_s),
        (sib_ref, sib_s),
        (far_ref, far_s),
        (dom_ref, dom_s),
        (om_ref, om_s),
        (os_ref, os_s),
        (stat_ref, stat_s),
    ):
        load(src, dst)
    load(sum_ref, sum_s.at[side])
    greet(
        [to_core, to_img] + [plane_device(dx, dz) for dx in range(2) for dz in range(4) if dx or dz]
    )
    from_core = start(doo_ref, dos_s, to_core)
    from_img = start(sum_ref, sum_s.at[side], to_img)
    moves = return_moves(out_ref, tiles_out, tile_send, tile_recv, local_sem)
    for _, copy in moves:
        copy.start()
    for copy in loads:
        copy.wait()
    from_core.wait_recv()
    scratch = (q_s, k_s, v_s, do_s, kt_s, dqt_s, dk_s, dv_s, p_s, ds_s, lse_s, dd_s)
    inputs = (dom_s, dos_s, om_s, os_s, stat_s, gm_s, gs_s, gfar_s)
    attend_back(heads, hd, 2, main, bias_ref[1], mine_s, sib_s, far_s, *inputs, *scratch)
    from_x = start(gfar_s, back_s, to_x)

    from_img.wait_recv()
    dwu_s[...] = sum_s[0].astype(f32)
    for a in range(2):
        for b in range(4):
            for c in range(2):
                first = ((2 * a + c) * 4 + b) * wide
                piece_s[a, b, c] = sum_s[1, :, first : first + wide]
    pieces = []
    for dx in range(2):
        for dz in range(4):
            src, dst = piece_s.at[(x + dx) % 2, hop(z, dz)], here_s.at[x, z]
            k = 4 * dx + dz
            if k:
                pieces.append(
                    send(src, dst, piece_send.at[k], piece_recv.at[k], plane_device(dx, dz))
                )
            else:
                pieces.append(pltpu.make_async_copy(src, dst, local_sem.at[2]))
    for copy in pieces:
        copy.start()

    attend_back(heads, hd, 4, 0, bias_ref[0], mine_s, sib_s, None, *inputs, *scratch)
    for copy in pieces:
        copy.wait()
    swap = start(here_s.at[:, :, 1 - core], there_s, to_core)
    from_x.wait_recv()
    size = tokens - main
    gm_s[main:, pad:] = plus(gm_s[main:, pad:], back_s[0:size])
    gs_s[main:, pad:] = plus(gs_s[main:, pad:], back_s[size:])
    outs = [
        pltpu.make_async_copy(src, dst, out_sem.at[k])
        for k, (src, dst) in enumerate(
            ((gm_s, gm_out), (gs_s, gs_out), (dwu_s, dwu_out), (dwd_s, dwd_out))
        )
    ]
    for copy in outs[:3]:
        copy.start()
    swap.wait_recv()
    for a in range(2):
        turn_s[a, core] = here_s[a, :, core].astype(f32)
        turn_s[a, 1 - core] = there_s[a].astype(f32)
    dwd_s[...] = turn_s[...].reshape(16 * n, wide).T
    outs[3].start()
    for copy in sides:
        copy.wait_send()
    for _, copy in moves:
        copy.wait()
    for copy in outs:
        copy.wait()


def back(mine, sib, far, dom, doo, om, os, stat, out, dw_sum, bias, heads, hd):
    tokens, pad = om.shape
    tile = tokens // 12
    n, hidden = dw_sum.shape
    width = 16 * n
    wide = hidden // 16
    any_ref = pl.BlockSpec(memory_space=pl.ANY)
    outs = (
        shaped((tokens, 3 * pad)),
        shaped((tokens, 3 * pad)),
        shaped((12, tile, width)),
        shaped((n, hidden), f32),
        shaped((wide, width), f32),
    )
    scratch = [
        shaped(mine.shape),
        shaped(sib.shape),
        shaped(far.shape),
        shaped(om.shape),
        shaped(om.shape),
        shaped(om.shape),
        shaped(om.shape),
        shaped(stat.shape, f32),
        outs[0],
        outs[1],
        shaped(far.shape),
        shaped(far.shape),
    ]
    scratch += [shaped((16 * tile, pad))] * 4
    scratch += [shaped((pad, 16 * tile), f32)] * 2
    scratch += [shaped((16 * tile, pad), f32)] * 2
    scratch += [shaped((16 * tile, 16 * tile))] * 2
    scratch += [shaped((4, heads, 256), f32)] * 2
    scratch += [
        shaped((2, n, hidden)),
        shaped((2, 4, 2, n, wide)),
        shaped((2, 4, 2, n, wide)),
        shaped((2, 4, n, wide)),
        shaped((2, 2, 4, n, wide), f32),
        outs[4],
        outs[3],
    ]
    return pl.pallas_call(
        functools.partial(back_kernel, heads, hd),
        in_specs=[any_ref] * 10 + [SMEM],
        out_specs=(any_ref,) * len(outs),
        scratch_shapes=[pltpu.VMEM(s.shape, s.dtype) for s in scratch]
        + [pltpu.SemaphoreType.DMA((k,)) for k in (12, 12, 3, 4, 4, 8, 8, 8, 4)],
        out_shape=outs,
        compiler_params=pltpu.CompilerParams(
            vmem_limit_bytes=62 * 2**20, collective_id=3, has_side_effects=True
        ),
        cost_estimate=pl.CostEstimate(
            flops=10240 * heads * tokens * 16 * tile,
            bytes_accessed=40 * 2**20,
            transcendentals=heads * 2 * tokens * 16 * tile,
        ),
        name="back",
    )(mine, sib, far, dom, doo, om, os, stat, out.reshape(12, tile, width), dw_sum, bias)


class Sum:
    def __init__(self, a, in2, out3, keep3, in3, c4, in4, d5, in5, all6, sems):
        self.refs = a, in2, out3, keep3, in3, c4, in4, d5, in5, all6
        self.sems = sems
        row, z = lax.axis_index("row"), lax.axis_index("col")
        self.x, self.y = row // 2, lax.axis_index("img") % 2
        self.zh, self.zl = z // 2, z % 2
        _, self.to_x, self.to_img = partners()
        self.waits = []

    def go(self, *copies):
        self.waits = [
            send(src, dst, self.sems.at[0, k], self.sems.at[1, k], device)
            for k, src, dst, device in copies
        ]
        for copy in self.waits:
            copy.start()

    def settle(self):
        for copy in self.waits:
            copy.wait()

    def step2(self):
        a, in2 = self.refs[:2]
        half = a.shape[2] // 2
        self.go(
            (0, a.at[:, 1 - self.x, pl.ds(0, half)], in2.at[0], self.to_x),
            (1, a.at[1 - self.y, :, pl.ds(half, half)], in2.at[1], self.to_img),
        )

    def step3(self):
        a, in2, out3, keep3, in3 = self.refs[:5]
        x, y = self.x, self.y
        half = a.shape[2] // 2
        low, high = slice(0, half), slice(half, 2 * half)
        self.settle()
        out3[0] = a[1 - y, x, low] + in2[0, 1 - y]
        out3[1] = a[y, 1 - x, high] + in2[1, 1 - x]
        self.go((2, out3.at[0], in3.at[0], self.to_img), (3, out3.at[1], in3.at[1], self.to_x))
        keep3[0] = a[y, x, low] + in2[0, y]
        keep3[1] = a[y, x, high] + in2[1, x]

    def step4(self):
        _, _, _, keep3, in3, c4, in4 = self.refs[:7]
        n = c4.shape[2]
        self.settle()
        for h in range(2):
            term = keep3[h].astype(f32) + in3[h].astype(f32)
            for k in range(2):
                c4[h, k] = term[k * n : (k + 1) * n].astype(bf16)
        self.go((4, c4.at[:, 1 - self.zl], in4, plane_device(0, 1)))

    def step5(self):
        c4, in4, d5, in5 = self.refs[5:9]
        self.settle()
        for h in range(2):
            d5[h] = c4[h, self.zl] + in4[h]
        self.go((5, d5.at[1 - self.zh], in5, plane_device(0, 2)))

    def step6(self):
        d5, in5, all6 = self.refs[7:]
        self.settle()
        all6[self.y] = d5[self.zh] + in5[...]
        self.go((6, all6.at[self.y], all6.at[self.y], self.to_img))


def sum_scratch(count, n, wide):
    return [
        shaped((count, 2, 2, 4 * n, wide)),
        shaped((count, 2, 2, 2 * n, wide)),
        shaped((count, 2, 2 * n, wide)),
        shaped((count, 2, 2 * n, wide)),
        shaped((count, 2, 2 * n, wide)),
        shaped((count, 2, 2, n, wide)),
        shaped((count, 2, n, wide)),
        shaped((count, 2, n, wide)),
        shaped((count, n, wide)),
        shaped((count, 2, n, wide)),
    ]


def last_kernel(
    blk,
    gm_ref,
    gs_ref,
    nt_ref,
    ntsib_ref,
    wh_ref,
    x_ref,
    gmid_ref,
    dwp_ref,
    wa_ref,
    mod_ref,
    dmod_ref,
    hot_ref,
    silu_ref,
    dbu_ref,
    dbp_ref,
    dbd_ref,
    tiles_out,
    dwp_out,
    dwq_out,
    dwa_out,
    dba_out,
    dsilu_out,
    small_out,
    gm_s,
    gs_s,
    nt_s,
    ntsib_s,
    w_s,
    x_s,
    gmid_s,
    tile_s,
    gnout_s,
    gnin_s,
    in1_s,
    a_s,
    in2_s,
    out3_s,
    keep3_s,
    in3_s,
    c4_s,
    in4_s,
    d5_s,
    in5_s,
    all6_s,
    swap_s,
    dwq_s,
    place_s,
    pcore_s,
    pmid_s,
    px_s,
    psum_s,
    every_s,
    wa_s,
    dwa_s,
    dwain_s,
    dwaf_s,
    dba_s,
    dbain_s,
    dbaf_s,
    ds_s,
    dsin_s,
    small_s,
    smallin_s,
    sum_sem,
    gn_sem,
    tile_send,
    tile_recv,
    local_sem,
    small_sem,
    p_sem,
    ada_sem,
    swap_sem,
    load_sem,
    wa_sem,
    out_sem,
):
    row = lax.axis_index("row")
    core, side = row % 2, lax.axis_index("img") % 2
    to_core, to_x, to_img = partners()
    tokens, width = x_s.shape
    tile = tokens // 12
    pad = w_s.shape[1] // 3
    part = width // 4
    ones = jnp.ones((16, tokens), bf16)

    loads = [
        pltpu.make_async_copy(src, dst, load_sem.at[k])
        for k, (src, dst) in enumerate(
            (
                (gs_ref, gs_s),
                (wh_ref.at[core], w_s),
                (gm_ref, gm_s),
                (dwp_ref.at[0], a_s.at[0]),
                (nt_ref, nt_s),
                (ntsib_ref, ntsib_s),
                (gmid_ref, gmid_s),
                (x_ref, x_s),
            )
        )
    ]
    for copy in loads:
        copy.start()
    ada = [
        pltpu.make_async_copy(
            wa_ref.at[:, pl.ds(pl.multiple_of(k * width, 128), width)], wa_s.at[i % 2], wa_sem.at[i % 2]
        )
        for i, k in enumerate((2 + 2 * core, 3 + 2 * core, core))
    ]
    for copy in ada[:2]:
        copy.start()
    greet(
        [to_core, to_img] + [plane_device(dx, dz) for dx in range(2) for dz in range(4) if dx or dz]
    )
    pending = []

    def start(src, dst, sems, k, device):
        copy = send(src, dst, sems.at[0, k], sems.at[1, k], device)
        copy.start()
        pending.append(copy)
        return copy

    sums = [
        Sum(
            *[
                ref.at[k]
                for ref in (a_s, in2_s, out3_s, keep3_s, in3_s, c4_s, in4_s, d5_s, in5_s, all6_s)
            ],
            sum_sem.at[k],
        )
        for k in range(4)
    ]
    proj = start(dwp_ref.at[1], in1_s, gn_sem, 3, to_core)

    def place(first, rows):
        for k, values in enumerate(rows):
            place_s[first + k] = functools.reduce(
                jnp.add, [hot_ref[:, i : i + 1] * values[i] for i in range(len(values))]
            ).astype(bf16)

    def p_core(k, first, count):
        at = pl.ds(first, count)
        other = pl.ds(4 - 2 * core, 2) if first == 0 else pl.ds(1 - core, 1)
        return start(place_s.at[other], pcore_s.at[at], p_sem, k, to_core)

    def p_x(k, first, count, before):
        before.wait_recv()
        at = pl.ds(first, count)
        for c in range(first, first + count):
            own = place_s[2 + 2 * core + c] if first == 0 else place_s[core]
            pmid_s[c] = own + pcore_s[c]
        return start(pmid_s.at[at], px_s.at[at], p_sem, k, to_x)

    def p_col(k, first, count, before):
        before.wait_recv()
        at = pl.ds(first, count)
        for c in range(first, first + count):
            psum_s[c] = pmid_s[c] + px_s[c]
            every_s[c, 0:16] = psum_s[c]
        return [
            start(
                psum_s.at[at],
                every_s.at[at, pl.ds(16 * dz, 16)],
                p_sem,
                k + dz - 1,
                plane_device(0, dz),
            )
            for dz in range(1, 4)
        ]

    def p_ada(k, first, count, before):
        for copy in before:
            copy.wait_recv()
        at = pl.ds(first, count)
        for c in range(first, first + count):
            for side_rows in range(2):
                dwa_s[c, side_rows] = dot(silu_ref[side_rows], every_s[c], NN).astype(bf16)
            dba_s[c : c + 1] = jnp.sum(every_s[c].astype(f32), axis=0, keepdims=True)
        return start(dwa_s.at[at], dwain_s.at[at], ada_sem, k, to_img)

    def p_silu(i):
        ada[i].wait()
        term = dot(every_s[i], wa_s[i % 2], NT)
        if i:
            ds_s[...] += term
        else:
            ds_s[...] = term
        if i + 2 < 3:
            ada[i + 2].start()

    place(2, [[dmod_ref[i, k : k + 1] for i in range(6)] for k in range(4)])
    early = p_core(0, 0, 2)

    loads[0].wait()
    loads[2].wait()
    total = dot(ones, gs_s[...], NN)[0:1] + dot(ones, gm_s[...], NN)[0:1]
    small_s[0] = jnp.zeros(small_s.shape[1:], f32)
    for c in range(2):
        mask = jnp.where(core == c, 1.0, 0.0)
        small_s[0, c : c + 1, 0:pad] = total[:, 0:pad] * mask
        small_s[0, c : c + 1, pad : 2 * pad] = total[:, 2 * pad :] * mask
    small_s[0, 2:3, 0:width] = dbp_ref[...]
    small_s[0, 3:4, 0:width] = dbd_ref[...]
    for k in range(4):
        small_s[0, 4 + k : 5 + k, 0:width] = dbu_ref[:, k * width : (k + 1) * width]
    route = (to_core, to_x, plane_device(0, 1), plane_device(0, 2), to_img)
    small_copies = []

    def small_step():
        k = len(small_copies)
        if k:
            small_copies[-1].wait_recv()
            small_s[k] = small_s[k - 1] + smallin_s[k - 1]
        if k < 5:
            small_copies.append(start(small_s.at[k], smallin_s.at[k], small_sem, k, route[k]))

    small_step()

    loads[1].wait()
    gn_copies = {}
    for first in (8, 0, 4):
        rows, at = slice(first * tile, (first + 4) * tile), pl.ds(first * tile, 4 * tile)
        gnout_s[rows] = dot(gs_s[rows], w_s[...], NT).astype(bf16)
        gn_copies[first] = start(gnout_s.at[at], gnin_s.at[at], gn_sem, first // 4, to_core)

    loads[3].wait()
    proj.wait_recv()
    for k in range(2):
        for h in range(2):
            a_s[0, k, h] = a_s[0, k, h] + in1_s[k, h]
    sums[0].step2()
    early = p_x(1, 0, 2, early)
    small_step()
    loads[4].wait()
    loads[5].wait()
    loads[6].wait()
    loads[7].wait()
    tile_moves_back = dict(return_moves(tile_s, tiles_out, tile_send, tile_recv, local_sem))
    late_rows = [[None] * 6, [None] * 6]

    def product(k, p):
        cols = slice(p * pad, (p + 1) * pad)
        for h in range(2):
            for c in range(2):
                rows = slice((2 * h + c) * part, (2 * h + c + 1) * part)
                term = dot(nt_s[rows], gm_s[:, cols], NN) + dot(ntsib_s[rows], gs_s[:, cols], NN)
                a_s[k, c, h] = term.astype(bf16)
        sums[k].step2()

    def first_norm(first):
        rows = slice(first * tile, (first + 4) * tile)
        gn_copies[first].wait_recv()
        both = dot(gm_s[rows], w_s[...], NT) + gnin_s[rows].astype(f32)
        for h in range(2):
            i = first // 2 + h
            rows = slice((first + 2 * h) * tile, (first + 2 * h + 2) * tile)
            y, rstd = norm(x_s[rows].astype(f32))
            gn = both[h * blk : (h + 1) * blk]
            u = gn * (1.0 + mod_ref[1, i : i + 1])
            back_term = rstd * (
                u
                - jnp.mean(u, axis=-1, keepdims=True)
                - y * jnp.mean(u * y, axis=-1, keepdims=True)
            )
            value = (gmid_s[rows].astype(f32) + back_term).astype(bf16)
            for t in range(2):
                tile_s[first + 2 * h + t] = value[t * tile : (t + 1) * tile]
            late_rows[0][i] = jnp.sum(gn, axis=0, keepdims=True)
            late_rows[1][i] = jnp.sum(gn * y, axis=0, keepdims=True)
        for t in range(first, first + 4):
            tile_moves_back[t].start()

    product(1, 2)
    first_norm(8)
    early = p_col(2, 0, 2, early)
    small_step()
    sums[0].step3()
    product(2, 1)
    first_norm(0)
    small_step()
    sums[1].step3()
    product(3, 0)
    first_norm(4)
    place(0, late_rows)
    late = p_core(5, 2, 1)
    sums[0].step4()
    small_step()
    early = p_ada(0, 0, 2, early)
    late = p_x(6, 2, 1, late)
    sums[2].step3()
    sums[1].step4()
    sums[0].step5()
    p_silu(0)
    late = p_col(7, 2, 1, late)
    sums[3].step3()
    sums[2].step4()
    sums[1].step5()
    sums[0].step6()
    small_step()
    p_silu(1)
    late = p_ada(1, 2, 1, late)
    dba_copy = start(dba_s, dbain_s, ada_sem, 2, to_img)
    sums[3].step4()
    sums[2].step5()
    sums[1].step6()
    p_silu(2)
    ds_copy = start(ds_s, dsin_s, ada_sem, 5, to_core)
    sums[3].step5()
    sums[2].step6()
    early.wait_recv()
    late.wait_recv()
    dba_copy.wait_recv()
    for c in range(3):
        dwaf_s[core, c] = dwa_s[c, 0] + dwain_s[c, 0]
        dwain_s[c, 1] = dwa_s[c, 1] + dwain_s[c, 1]
    dbaf_s[core] = dba_s[...] + dbain_s[...]
    ada_swaps = [
        start(dwain_s.at[:, 1], dwaf_s.at[core], ada_sem, 3, to_core),
        start(dbaf_s.at[core], dbaf_s.at[core], ada_sem, 4, to_core),
    ]
    sums[3].step6()
    sums[0].settle()
    outs = [pltpu.make_async_copy(all6_s.at[0], dwp_out, out_sem.at[0])]
    outs[0].start()
    swaps = []
    for k in range(1, 4):
        sums[k].settle()
        swaps.append(start(all6_s.at[k, 1 - core], swap_s.at[3 - k], swap_sem, k - 1, to_core))
        dwq_s[core, 3 - k] = all6_s[k, core]
    ds_copy.wait_recv()
    dsilu_out[...] = ds_s[...] + dsin_s[...]
    for copy in swaps + ada_swaps:
        copy.wait_recv()
    for p in range(3):
        dwq_s[1 - core, p] = swap_s[p]
    for k, (src, dst) in enumerate(
        ((dwq_s, dwq_out), (dwaf_s, dwa_out), (dbaf_s, dba_out), (small_s.at[5], small_out))
    ):
        outs.append(pltpu.make_async_copy(src, dst, out_sem.at[k + 1]))
        outs[-1].start()
    for copy in pending:
        copy.wait_send()
    for copy in tile_moves_back.values():
        copy.wait()
    for copy in outs:
        copy.wait()


def last(gm, gs, nt, ntsib, w_half, x, gmid, dwp, w_ada, mod, dmod, hot, silu_t, dbu, dbp, dbd, blk):
    tokens, width = x.shape
    tile = tokens // 12
    wide = gm.shape[1]
    pad = wide // 3
    n = width // 16
    any_ref = pl.BlockSpec(memory_space=pl.ANY)
    outs = (
        shaped((12, tile, width)),
        shaped((2, n, pad)),
        shaped((2, 3, n, pad)),
        shaped((2, 3, n, width)),
        shaped((2, 8, width), f32),
        shaped((64, width), f32),
        shaped((8, 2 * pad), f32),
    )
    scratch = [
        shaped(gm.shape),
        shaped(gs.shape),
        shaped(nt.shape),
        shaped(nt.shape),
        shaped((width, wide)),
        shaped(x.shape),
        shaped(x.shape),
        outs[0],
        shaped(x.shape),
        shaped(x.shape),
        shaped(dwp.shape[1:]),
    ]
    scratch += sum_scratch(4, n, pad)
    scratch += [shaped((3, n, pad)), outs[2]]
    scratch += [shaped((6, 16, width))]
    scratch += [shaped((3, 16, width))] * 4
    scratch += [
        shaped((3, 64, width)),
        shaped((2, width, width)),
        shaped((3, 2, n, width)),
        shaped((3, 2, n, width)),
        outs[3],
        shaped((8, width), f32),
        shaped((8, width), f32),
        outs[4],
        outs[5],
        outs[5],
        shaped((6, 8, 2 * pad), f32),
        shaped((5, 8, 2 * pad), f32),
    ]
    sems = [(4, 2, 7), (2, 4), (12,), (12,), (3,), (2, 5), (2, 10), (2, 6), (2, 3), (8,), (2,), (5,)]
    return pl.pallas_call(
        functools.partial(last_kernel, blk),
        in_specs=[any_ref] * 9 + [VMEM] * 7,
        out_specs=(any_ref,) * 5 + (VMEM, any_ref),
        scratch_shapes=[pltpu.VMEM(s.shape, s.dtype) for s in scratch]
        + [pltpu.SemaphoreType.DMA(s) for s in sems],
        out_shape=outs,
        compiler_params=pltpu.CompilerParams(
            vmem_limit_bytes=62 * 2**20, collective_id=4, has_side_effects=True
        ),
        cost_estimate=pl.CostEstimate(
            flops=8 * tokens * width * wide, bytes_accessed=60 * 2**20, transcendentals=tokens
        ),
        name="last",
    )(gm, gs, nt, ntsib, w_half, x, gmid, dwp, w_ada, mod, dmod, hot, silu_t, dbu, dbp, dbd)


def pick(values, index, axis=0):
    return lax.dynamic_index_in_dim(values, index, axis, keepdims=False)


def over_rest(v):
    size = lax.axis_size("img")
    step = 2
    while step < size:
        v = v + lax.ppermute(v, "img", [(i, i ^ step) for i in range(size)])
        step *= 2
    return v


def shards(
    tokens,
    conditioning,
    images_in_slot,
    w_qkv,
    b_qv,
    w_proj,
    b_proj,
    w_up,
    b_up,
    w_down,
    b_down,
    w_ada,
    b_ada,
    cotangent,
):
    slots, rows_tile, cols_tile, width = tokens.shape
    tile = rows_tile * cols_tile
    blk = 2 * tile
    count = slots * tile
    main = 8 * tile
    hd = width // HEADS
    heads = HEADS // 2
    half = width // 2
    pad = -(-half // 128) * 128
    hidden = w_up.shape[1]
    r, z = lax.axis_index("row"), lax.axis_index("col")
    x, core = r // 2, r % 2
    assert lax.axis_size("row") == 4 and lax.axis_size("col") == 4 and slots == 12

    four_way = images_in_slot == 4
    kinds = pick(four_way.reshape(4, 3), z)
    main_four, shared_four = pick(kinds, x), kinds[2]
    quarter = jnp.stack([2 * (x ^ dx) + ((z // 2) ^ dz) for dx in range(2) for dz in range(2)])
    picks = jnp.concatenate(
        [jnp.where(main_four, quarter, 0), jnp.where(shared_four, quarter[:2], 0)]
    )
    places = jnp.concatenate([jnp.full((4,), x, jnp.int32), jnp.full((2,), 2, jnp.int32)]) * 4 + picks
    bias = jnp.where(jnp.stack([main_four, shared_four]), -1e30, 0.0).astype(f32)
    cond = conditioning.astype(f32)
    silu = jax.nn.silu(cond).astype(bf16)
    silu_groups = silu.reshape(4, 12, width)
    chosen = jnp.take(pick(silu_groups, z), places, axis=0)
    chosen = jnp.pad(chosen, ((0, 2), (0, 0)))

    def widen(v, axis):
        return jnp.pad(v, [(0, pad - half) if a == axis else (0, 0) for a in range(v.ndim)])

    b_three = jnp.stack([b_qv[:width], jnp.zeros_like(b_qv[:width]), b_qv[width:]])
    b_half = widen(b_three.reshape(3, 2, half).astype(f32), 2).transpose(1, 0, 2)
    b_half = b_half.reshape(2, 1, 3 * pad)

    (
        inputs,
        upstream,
        qkv_mine,
        qkv_sib,
        normed_t,
        normed_sib,
        far_kv,
        om,
        os,
        att_other,
        stat,
        mod,
        w_half,
    ) = forward(
        tokens.reshape(slots, tile, width),
        cotangent.reshape(slots, tile, width),
        w_qkv,
        w_ada,
        chosen,
        b_half,
        b_ada,
        bias,
        heads,
        hd,
    )
    inputs = inputs.reshape(count, width)
    upstream = upstream.reshape(count, width)

    (
        out,
        gmid,
        do_mine,
        do_other,
        dw_sum,
        dbu,
        dwp,
        dmod_mid,
        dbp,
        dbd,
    ) = middle(
        inputs,
        upstream,
        om,
        att_other,
        mod,
        w_proj,
        b_proj,
        b_down,
        w_up,
        b_up,
        w_down,
        blk,
    )
    g_mine, g_sib, output, grad_w_up, grad_w_down = back(
        qkv_mine, qkv_sib, far_kv, do_mine, do_other, om, os, stat, out, dw_sum, bias, heads, hd
    )
    output = output.reshape(tokens.shape)
    hot = (jnp.arange(16, dtype=jnp.int32)[:, None] == places[None, :]).astype(f32)
    hot = jnp.pad(hot, ((0, 0), (0, 2)))
    rank = r * 4 + z
    n = width // 16
    silu_t = jnp.stack([pick(silu_groups, z ^ dz) for dz in range(4)])
    silu_t = jnp.pad(silu_t, ((0, 0), (0, 4), (0, 0))).reshape(64, width)
    silu_t = jnp.stack(
        [lax.dynamic_slice_in_dim(silu_t, k * n, n, 1).T for k in (rank, (r ^ 1) * 4 + z)]
    )
    grad_x, dwp_sum, dwq_sum, dwa, dba, dsilu, small = last(
        g_mine,
        g_sib,
        normed_t,
        normed_sib,
        w_half,
        inputs,
        gmid,
        dwp,
        w_ada,
        mod,
        dmod_mid,
        hot,
        silu_t,
        dbu,
        dbp,
        dbd,
        blk,
    )
    grad_tokens = grad_x.reshape(tokens.shape).astype(f32)
    dwp_sum, dwq_sum, dwa, dba, small, grad_w_up, grad_w_down = (
        over_rest(v) for v in (dwp_sum, dwq_sum, dwa, dba, small, grad_w_up, grad_w_down)
    )
    grad_w_proj = jnp.concatenate([dwp_sum[0], dwp_sum[1, :, 2 * pad - width :]], axis=1)
    grad_w_proj = grad_w_proj.astype(f32)
    grad_w_qkv = dwq_sum[..., :half].astype(f32).transpose(2, 1, 0, 3).reshape(n, 3 * width)
    parts = ((0, 2), (1, 2), (0, 0), (0, 1), (1, 0), (1, 1))
    grad_w_ada = jnp.concatenate([dwa[c, k] for c, k in parts], axis=1).astype(f32)
    dba = jnp.concatenate([dba[c, k] for c, k in parts])
    grad_b_ada = lax.dynamic_slice_in_dim(dba, rank * 6 * n, 6 * n, 0)
    d_s = dsilu.reshape(4, 16, width)[:, :12]
    d_s = jnp.stack([pick(d_s, z ^ g) for g in range(4)]).reshape(slots, 4, width)
    sig = jax.nn.sigmoid(cond)
    grad_conditioning = d_s * (sig * (1.0 + cond * (1.0 - sig)))
    db_qv = small[:2].reshape(2, 2, pad)[..., :half].transpose(1, 0, 2).reshape(2 * width)

    def own(values):
        size = values.shape[0] // 16
        return lax.dynamic_slice_in_dim(values, rank * size, size, 0)

    return (
        output,
        grad_tokens,
        grad_conditioning,
        grad_w_qkv,
        own(db_qv),
        grad_w_proj,
        own(small[2, :width]),
        grad_w_up,
        own(small[4:, :width].reshape(hidden)),
        grad_w_down,
        own(small[3, :width]),
        grad_w_ada,
        grad_b_ada,
    )


def solution(mesh):
    grid = P("img", "row", "col", None)
    plane = ("row", "col")
    return jax.shard_map(
        shards,
        mesh=mesh,
        in_specs=(grid, P("img", None, None), P("img")) + (P(),) * 10 + (grid,),
        out_specs=(grid, grid, P("img", None, None))
        + (P(plane, None), P(plane)) * 5,
        check_vma=False,
    )
```
